32 devices in a mesh: section: 2 (over core), dp: 4 (over y, x), seq: 4 (over z).
Axes of the slice: x: 2, y: 2, z: 4, core: 2. Of those that a mesh axis runs over, the one named last changes fastest.
Arguments:
- ends_in: bfloat16 [2, 4, 4, 1024, 1280], P('section', None, 'dp', 'seq'), may hold values from -6 to 6
- lengths: int32 [4, 4], P(None, 'dp'), may hold values from 30 to 1024, as said below
- outer_gain: float32 [2, 1280], P('section'), may hold values from 0.5 to 1.5
- inner_gains: float32 [2, 2, 640], P('section'), may hold values from 0.5 to 1.5
- outer_biases: float32 [2, 2, 1280], P('section'), may hold values from -1.75 to 1.75
- inner_biases: float32 [2, 4, 640], P('section'), may hold values from -1.75 to 1.75
- down_in: bfloat16 [2, 1280, 640], P('section'), may hold values from -0.15625 to 0.15625
- conv_weight: bfloat16 [2, 5, 640, 640], P('section'), may hold values from -0.109375 to 0.109375
- up_out: bfloat16 [2, 640, 1280], P('section'), may hold values from -0.25 to 0.25
Outputs:
- ends_out: float32 [2, 4, 4, 1024, 1280], P('section', None, 'dp', 'seq')
- grad_outer_gain: float32 [2, 1280], P('section')
- grad_inner_gains: float32 [2, 2, 640], P('section')
- grad_outer_biases: float32 [2, 2, 1280], P('section')
- grad_inner_biases: float32 [2, 4, 640], P('section')
- grad_down_in: float32 [2, 1280, 640], P('section')
- grad_conv_weight: float32 [2, 5, 640, 640], P('section')
- grad_up_out: float32 [2, 640, 1280], P('section')
- rms: float32 [2, 2], P('section')
The draws below stay inside these ranges and needn't reach their ends.
Inputs may be any that keep to these rules, and one draw needn't show every extreme that they name: `lengths`: in every micro-batch, each block of 1 consecutive items holds one item of the full 1024 positions.
All inputs are finite; a program needn't handle non-finite values.
Results may differ from the reference program's by a relative error of at most 0.011.
Values may be sent and summed in bfloat16 or wider, within the bound.
A program may use at most 128 MiB of HBM per device.

```python
import jax
import jax.numpy as jnp
from jax import lax

D = 1280
INNER = 640
FILTER_TAPS = 5
FIRST_DILATION = 2
SECOND_DILATION = 128
MB = 4
B_DEV = 1
LEN = 1024
ITEMS_MB = 4
N_DP = 4


def draw_lengths(key, part):
    key = jax.random.fold_in(key, 11)
    key_base, key_pick = jax.random.split(key)
    base = jax.random.randint(key_base, (MB, ITEMS_MB), 30, LEN + 1)
    pick = jax.random.randint(key_pick, (MB, N_DP), 0, B_DEV)
    slot = jnp.arange(ITEMS_MB, dtype=jnp.int32) % B_DEV
    full = slot[None, :] == jnp.repeat(pick, B_DEV, axis=1)
    return jnp.where(full, LEN, base).astype(jnp.int32)


def steps_of(own_key, extent, cuts, least, top_value):
    loudness, own = 1.0, jax.random.fold_in(own_key, 6)
    for dim, shards_of in cuts:
        steps = jnp.exp(jax.random.uniform(jax.random.fold_in(own, dim), (shards_of,), jnp.float32, least / len(cuts), top_value / len(cuts)))
        loudness = loudness * jnp.repeat(steps, extent[dim] // shards_of).reshape([-1 if axis == dim else 1 for axis in range(len(extent))])
    return loudness


def bell_draw(stream_key, shape, width, bound, cuts=(), kind=jnp.bfloat16):
    result = jax.random.normal(stream_key, shape, jnp.float32) * width
    if len(cuts) > 0:
        result = steps_of(stream_key, shape, cuts, -0.22, 0.18) * result
    return jnp.clip(result, min=-bound, max=bound).astype(kind)


def setup_inputs(seed: int = 0) -> dict:
    seeds = jax.random.split(jax.random.key(seed), 10)
    ends_in = bell_draw(seeds[0], (2, MB, ITEMS_MB, LEN, D), 1.0, 6.0, ((0, 2), (2, 4), (3, 4)))
    lengths = draw_lengths(jax.random.fold_in(seeds[9], 71), 0)
    outer_gain = jnp.clip(1.0 + 0.1 * jax.random.normal(seeds[2], (2, D), jnp.float32), 0.5, 1.5)
    inner_gains = jnp.clip(1.0 + 0.1 * jax.random.normal(seeds[3], (2, 2, INNER), jnp.float32), 0.5, 1.5)
    outer_biases = bell_draw(seeds[4], (2, 2, D), 0.3, 1.75, ((0, 2),), jnp.float32)
    inner_biases = bell_draw(seeds[5], (2, 4, INNER), 0.3, 1.75, ((0, 2),), jnp.float32)
    down_in = bell_draw(seeds[6], (2, D, INNER), D ** -0.5, 0.15625, ((0, 2),))
    conv_weight = bell_draw(seeds[7], (2, FILTER_TAPS, INNER, INNER), (FILTER_TAPS * INNER) ** -0.5, 0.109375, ((0, 2),))
    up_out = bell_draw(seeds[8], (2, INNER, D), INNER ** -0.5, 0.25, ((0, 2),))
    return dict(ends_in=ends_in, lengths=lengths, outer_gain=outer_gain, inner_gains=inner_gains, outer_biases=outer_biases, inner_biases=inner_biases, down_in=down_in, conv_weight=conv_weight, up_out=up_out)


@jax.custom_vjp
def low(v):
    return lax.optimization_barrier(v.astype(jnp.bfloat16)).astype(jnp.float32)

@jax.custom_vjp
def low_back(v):
    return v

def low_keep(v):
    return (low(v), None)

def low_pass(kept, grad):
    return (grad,)

def back_keep(v):
    return (v, None)

def back_low(kept, grad):
    return (low(grad),)
low.defvjp(low_keep, low_pass)
low_back.defvjp(back_keep, back_low)

def matmul(left, right):
    return jnp.dot(left, right, precision=lax.Precision.HIGHEST, preferred_element_type=jnp.float32)

def norm_gelu(value, gain, shift):
    mean = lax.optimization_barrier(jnp.mean(value, axis=-1, keepdims=True))
    centred = value - mean
    spread = lax.optimization_barrier(jnp.mean(centred * centred, axis=-1, keepdims=True))
    return jax.nn.gelu(centred * lax.rsqrt(spread + 1e-05) * gain + shift)

def conv_taps(values, weight, dilation_step):
    receptive_reach = FILTER_TAPS // 2 * dilation_step
    padded = jnp.pad(values, ((receptive_reach, receptive_reach), (0, 0)))
    length = values.shape[0]
    taps = jnp.concatenate([padded[tap * dilation_step:tap * dilation_step + length] for tap in range(FILTER_TAPS)], axis=1)
    return matmul(taps, weight.reshape(FILTER_TAPS * INNER, INNER))

def block_index(input_rows, parameters, valid_mask, dilation_step):
    gain_a, shift_a, bias_out, gain_b, gain_c, shift_b, shift_c, bias_in, bias_conv, weight_in, weight_conv, weight_out = parameters
    hidden_a = norm_gelu(input_rows, gain_a, shift_a)
    proj = low_back(matmul(low(hidden_a), weight_in)) + bias_in
    conv_in = low(norm_gelu(proj, gain_b, shift_b) * valid_mask)
    conv = low_back(conv_taps(conv_in, weight_conv, dilation_step)) + bias_conv
    hidden_c = norm_gelu(conv, gain_c, shift_c)
    branch = (low_back(matmul(low(hidden_c), weight_out)) + bias_out) * valid_mask
    return (input_rows + branch, branch)

def two_blocks(input_rows, weights, valid_mask):
    outer_gain, inner_gains, outer_biases, inner_biases, down_in, conv_weight, up_out = weights

    def parameters(index):
        return (outer_gain[index], outer_biases[index, 0], outer_biases[index, 1], inner_gains[index, 0], inner_gains[index, 1], inner_biases[index, 0], inner_biases[index, 1], inner_biases[index, 2], inner_biases[index, 3], down_in[index], conv_weight[index], up_out[index])
    middle_result, residual_branch_one = block_index(input_rows, parameters(0), valid_mask, FIRST_DILATION)
    handed_rows = low_back(low(middle_result))
    output_rows, residual_branch_two = block_index(handed_rows, parameters(1), valid_mask, SECOND_DILATION)
    sums = jnp.stack([jnp.sum(input_rows * input_rows * valid_mask), jnp.sum(residual_branch_one * residual_branch_one), jnp.sum(handed_rows * handed_rows * valid_mask), jnp.sum(residual_branch_two * residual_branch_two)])
    return (output_rows, sums)

def reference(ends_in, lengths, outer_gain, inner_gains, outer_biases, inner_biases, down_in, conv_weight, up_out):
    weights = tuple((array.astype(jnp.float32) for array in (outer_gain, inner_gains, outer_biases, inner_biases, down_in, conv_weight, up_out)))
    item_count = MB * ITEMS_MB
    firsts = ends_in[0].reshape(item_count, LEN, D)
    cotangents = ends_in[1].reshape(item_count, LEN, D)
    item_lengths = lengths.reshape(item_count).astype(jnp.int32)

    def one_item(carry, item):
        grads, sums, valid_rows = carry
        input_rows, cotangent, length = item
        valid_mask = (jnp.arange(LEN, dtype=jnp.int32) < length).astype(jnp.float32)[:, None]
        output_rows, pullback, item_sums = jax.vjp(lambda value, parameters: two_blocks(value, parameters, valid_mask), input_rows.astype(jnp.float32), weights, has_aux=True)
        grad_input, grad_weights = pullback(cotangent.astype(jnp.float32))
        grads = jax.tree.map(jnp.add, grads, grad_weights)
        return ((grads, sums + item_sums, valid_rows + jnp.sum(valid_mask)), (grad_input, output_rows))
    zeros = jax.tree.map(jnp.zeros_like, weights)
    start = (zeros, jnp.zeros((4,), jnp.float32), jnp.zeros((), jnp.float32))
    (grads, sums, valid_rows), (grad_inputs, outputs) = lax.scan(one_item, start, (firsts, cotangents, item_lengths))
    ends_out = jnp.stack([grad_inputs, outputs]).reshape(2, MB, ITEMS_MB, LEN, D)
    rms = jnp.sqrt(sums / (valid_rows * D)).reshape(2, 2)
    return (ends_out, grads[0], grads[1], grads[2], grads[3], grads[4], grads[5], grads[6], rms)
```

```python
import functools

import jax
import jax.numpy as jnp
from jax import lax
from jax.experimental import pallas as pl
from jax.experimental.pallas import tpu as pltpu
from jax.sharding import PartitionSpec as P

MESH = pl.DeviceIdType.MESH
BF = jnp.bfloat16
F32 = jnp.float32
GROUPS = 9
BLOCK = 640
LROWS = 384
ZROWS = 256
CH = ZROWS // 4
KINDS = ["ru", "rv", "za", "zb", "zc", "av", "au", "ze", "zm", "zo", "ex", "ey", "ge", "gm", "go"]
SKINDS = ["sx", "sy", "sa", "sb", "sc"]


class Reduce:
    def __init__(self, grad, res, r, sm, send, recv, ssend, srecv):
        self.grad, self.res, self.r, self.sm = grad, res, r, sm
        self.send, self.recv, self.ssend, self.srecv = send, recv, ssend, srecv
        self.c = lax.axis_index("section")
        self.dp = lax.axis_index("dp")
        self.z = lax.axis_index("seq")
        self.x = lax.rem(self.dp, 2)
        self.y = self.dp // 2
        z = self.z
        self.end = jnp.logical_or(z == 0, z == 3)
        self.mid = jnp.logical_not(self.end)
        self.up = z // 2
        self.px = (self.c, self.dp + 1 - 2 * self.x, z)
        self.py = (self.c, lax.rem(self.dp + 2, 4), z)
        self.pair = (self.c, self.dp, 1 - z + 4 * self.up)
        self.other = (self.c, self.dp, jnp.clip(3 - z, 1, 2))

    def copy(self, kind, g, src, dst, to):
        j = KINDS.index(kind)
        return pltpu.make_async_remote_copy(
            src_ref=src, dst_ref=dst, send_sem=self.send.at[g, j], recv_sem=self.recv.at[g, j],
            device_id=to, device_id_type=MESH)

    def scopy(self, kind, src, dst, to):
        j = SKINDS.index(kind)
        return pltpu.make_async_remote_copy(
            src_ref=src, dst_ref=dst, send_sem=self.ssend.at[j], recv_sem=self.srecv.at[j],
            device_id=to, device_id_type=MESH)

    def rows(self, ref, off, n):
        if not isinstance(off, int):
            off = pl.multiple_of(off, 16)
        return ref.at[pl.ds(off, n)]

    def add(self, dst, doff, srcs, n, tile=32):
        def body(i, carry):
            o = i * tile
            acc = None
            for ref, off in srcs:
                v = ref[pl.ds(pl.multiple_of(off + o, 16), tile), :]
                if len(srcs) > 2:
                    v = v.astype(F32)
                acc = v if acc is None else acc + v
            dst[pl.ds(pl.multiple_of(doff + o, 16), tile), :] = acc.astype(BF)
            return carry
        lax.fori_loop(0, n // tile, body, 0, unroll=True)

    def lgeo(self, g):
        b = g * BLOCK
        if g % 2 == 0:
            u, v, pu, pv = self.x, self.y, self.px, self.py
        else:
            u, v, pu, pv = self.y, self.x, self.py, self.px
        h, q = LROWS // 2, LROWS // 4
        return b, h, q, u, v, pu, pv

    def lcopies(self, g):
        b, h, q, u, v, pu, pv = self.lgeo(g)
        own_h = b + u * h
        own_q = own_h + v * q
        oth_q = own_h + (1 - v) * q
        G, R = self.grad, self.res
        rows = self.rows
        r = self.r
        qq = rows(R, own_q, q)
        return dict(
            ru=self.copy("ru", g, rows(G, b + (1 - u) * h, h), r["ru"].at[g], pu),
            rv=self.copy("rv", g, rows(G, oth_q, q), r["rv"].at[g], pv),
            za=self.copy("za", g, rows(G, own_q, q), r["za"].at[g], self.pair),
            zb=self.copy("zb", g, rows(G, own_q, q), r["zb"].at[g], self.other),
            zc=self.copy("zc", g, qq, qq, self.pair),
            av=self.copy("av", g, qq, qq, pv),
            au=self.copy("au", g, rows(R, own_h, h), rows(R, own_h, h), pu),
        )

    def L(self, g, level):
        b, h, q, u, v, pu, pv = self.lgeo(g)
        own_h = b + u * h
        own_q = own_h + v * q
        oth_q = own_h + (1 - v) * q
        c = self.lcopies(g)
        r = self.r
        G, R = self.grad, self.res
        if level == 0:
            c["ru"].start()
        elif level == 1:
            c["ru"].wait_recv()
            self.add(G, oth_q, [(G, oth_q), (r["ru"].at[g], (1 - v) * q)], q)
            c["rv"].start()
            self.add(G, own_q, [(G, own_q), (r["ru"].at[g], v * q)], q)
        elif level == 2:
            c["rv"].wait_recv()
            self.add(G, own_q, [(G, own_q), (r["rv"].at[g], 0)], q)
            pl.when(self.end)(c["za"].start)
        elif level == 3:
            @pl.when(self.mid)
            def _():
                c["za"].wait_recv()
                self.add(G, own_q, [(G, own_q), (r["za"].at[g], 0)], q)
                c["zb"].start()
        elif level == 4:
            @pl.when(self.mid)
            def _():
                c["zb"].wait_recv()
                self.add(R, own_q, [(G, own_q), (r["zb"].at[g], 0)], q)
                c["zc"].start()
                c["av"].start()
        elif level == 5:
            @pl.when(self.end)
            def _():
                c["zc"].wait_recv()
                c["av"].start()
        elif level == 6:
            c["av"].wait_recv()
            c["au"].start()
        elif level == 7:
            c["au"].wait_recv()

    def zcopies(self, g):
        zb = g * BLOCK + LROWS
        z, up = self.z, self.up
        G, R, r, rows = self.grad, self.res, self.r, self.rows
        e_off = zb + CH * (1 - up)
        m_off = zb + 2 * CH * (1 - up)
        p_off = zb + 2 * CH * up
        o_off = zb + 3 * CH * up
        own = zb + CH * z
        return dict(
            ze=self.copy("ze", g, rows(G, e_off, 3 * CH), r["ze"].at[g], self.pair),
            zm=self.copy("zm", g, rows(G, m_off, 2 * CH), r["zm"].at[g], self.other),
            zo=self.copy("zo", g, rows(G, o_off, CH), r["zo"].at[g], self.pair),
            ex=self.copy("ex", g, rows(G, own, CH), r["ex"].at[g], self.px),
            ey=self.copy("ey", g, r["tx"].at[g], r["ey"].at[g], self.py),
            ge=self.copy("ge", g, rows(R, own, CH), rows(R, own, CH), self.pair),
            gm=self.copy("gm", g, rows(R, p_off, 2 * CH), rows(R, p_off, 2 * CH), self.other),
            go=self.copy("go", g, rows(R, e_off, 3 * CH), rows(R, e_off, 3 * CH), self.pair),
        ), zb, e_off, m_off, p_off, o_off, own

    def Z(self, g, level):
        c, zb, e_off, m_off, p_off, o_off, own = self.zcopies(g)
        z, up = self.z, self.up
        G, R, r = self.grad, self.res, self.r
        if level == 0:
            pl.when(self.end)(c["ze"].start)
        elif level == 1:
            @pl.when(self.mid)
            def _():
                c["ze"].wait_recv()
                self.add(G, m_off, [(G, m_off), (r["ze"].at[g], m_off - e_off)], 2 * CH)
                c["zm"].start()
        elif level == 2:
            @pl.when(self.mid)
            def _():
                c["zm"].wait_recv()
                self.add(G, o_off, [(G, o_off), (r["zm"].at[g], o_off - p_off)], CH)
                c["zo"].start()
                self.add(G, own, [(G, own), (r["ze"].at[g], own - e_off), (r["zm"].at[g], own - p_off)], CH)
                c["ex"].start()
        elif level == 3:
            @pl.when(self.end)
            def _():
                c["zo"].wait_recv()
                self.add(G, own, [(G, own), (r["zo"].at[g], 0)], CH)
                c["ex"].start()
        elif level == 4:
            c["ex"].wait_recv()
            self.add(r["tx"].at[g], 0, [(G, own), (r["ex"].at[g], 0)], CH)
            c["ey"].start()
        elif level == 5:
            c["ey"].wait_recv()
            self.add(R, own, [(r["tx"].at[g], 0), (r["ey"].at[g], 0)], CH)
            pl.when(self.end)(c["ge"].start)
        elif level == 6:
            @pl.when(self.mid)
            def _():
                c["ge"].wait_recv()
                c["gm"].start()
        elif level == 7:
            @pl.when(self.mid)
            def _():
                c["gm"].wait_recv()
                c["go"].start()
        elif level == 8:
            pl.when(self.end)(c["go"].wait_recv)

    def scopies(self):
        s = self.sm
        return dict(
            sx=self.scopy("sx", s.at[0], s.at[5], self.px),
            sy=self.scopy("sy", s.at[1], s.at[6], self.py),
            sa=self.scopy("sa", s.at[2], s.at[7], self.pair),
            sb=self.scopy("sb", s.at[3], s.at[8], self.other),
            sc=self.scopy("sc", s.at[4], s.at[4], self.pair),
        )

    def S(self, level):
        c = self.scopies()
        s = self.sm
        if level == 0:
            c["sx"].start()
        elif level == 1:
            c["sx"].wait_recv()
            s[1] = s[0] + s[5]
            c["sy"].start()
        elif level == 2:
            c["sy"].wait_recv()
            s[2] = s[1] + s[6]
            pl.when(self.end)(c["sa"].start)
        elif level == 3:
            @pl.when(self.mid)
            def _():
                c["sa"].wait_recv()
                s[3] = s[2] + s[7]
                c["sb"].start()
        elif level == 4:
            @pl.when(self.mid)
            def _():
                c["sb"].wait_recv()
                s[4] = s[3] + s[8]
                c["sc"].start()
        elif level == 5:
            pl.when(self.end)(c["sc"].wait_recv)

    def drain(self, groups=GROUPS):
        for g in range(groups):
            c = dict(self.lcopies(g))
            c.update(self.zcopies(g)[0])
            for k in ("ru", "rv", "av", "au", "ex", "ey"):
                c[k].wait_send()

            @pl.when(self.end)
            def _():
                for k in ("za", "ze", "ge"):
                    c[k].wait_send()

            @pl.when(self.mid)
            def _():
                for k in ("zb", "zc", "zm", "zo", "gm", "go"):
                    c[k].wait_send()
        c = self.scopies()
        c["sx"].wait_send()
        c["sy"].wait_send()
        pl.when(self.end)(c["sa"].wait_send)

        @pl.when(self.mid)
        def _():
            c["sb"].wait_send()
            c["sc"].wait_send()


def schedule(gap, hl, hz=None, oz=0.0, old=1):
    hz = hl if hz is None else hz
    ops = []
    for g in range(GROUPS):
        for lv in range(8):
            ops.append((gap * g + hl * lv, old * g, 0, g, "L", lv))
        for lv in range(9):
            ops.append((gap * g + oz + hz * lv, old * g, 1, g, "Z", lv))
    return [(t, p, g, k, lv) for t, _, p, g, k, lv in sorted(ops)]


def scratch():
    q, h = LROWS // 4, LROWS // 2
    n = GROUPS
    v = lambda rows: pltpu.VMEM((n, rows, BLOCK), BF)
    bufs = dict(ru=v(h), rv=v(q), za=v(q), zb=v(q), ze=v(3 * CH), zm=v(2 * CH), zo=v(CH), ex=v(CH), ey=v(CH), tx=v(CH))
    sems = [pltpu.SemaphoreType.DMA((n, len(KINDS))), pltpu.SemaphoreType.DMA((n, len(KINDS))),
            pltpu.SemaphoreType.DMA((len(SKINDS),)), pltpu.SemaphoreType.DMA((len(SKINDS),))]
    return bufs, sems


def reduce_kernel(names, ops, g_hbm, s_hbm, o_hbm, so_hbm, grad, res, sm, *rest):
    count = len(names)
    r = dict(zip(names, rest[:count]))
    send, recv, ssend, srecv, lsem = rest[count:]
    red = Reduce(grad, res, r, sm, send, recv, ssend, srecv)
    load = pltpu.make_async_copy(g_hbm, grad, lsem.at[0])
    load.start()
    load_small = pltpu.make_async_copy(s_hbm, sm.at[0], lsem.at[1])
    load_small.start()
    barrier = pltpu.get_barrier_semaphore()
    for to in (red.px, red.py, red.pair):
        pl.semaphore_signal(barrier, inc=1, device_id=to, device_id_type=MESH)

    @pl.when(red.mid)
    def _():
        pl.semaphore_signal(barrier, inc=1, device_id=red.other, device_id_type=MESH)
        pl.semaphore_wait(barrier, 4)

    pl.when(red.end)(lambda: pl.semaphore_wait(barrier, 3))
    load.wait()
    load_small.wait()
    for _, _, g, kind, level in ops:
        if kind == "L":
            red.L(g, level)
            if g == GROUPS - 1 and level < 6:
                red.S(level)
        else:
            red.Z(g, level)
    red.drain()
    store = pltpu.make_async_copy(res, o_hbm, lsem.at[2])
    store.start()
    store_small = pltpu.make_async_copy(sm.at[4], so_hbm, lsem.at[3])
    store_small.start()
    store.wait()
    store_small.wait()


def all_sum(rows, small):
    bufs, sems = scratch()
    names = list(bufs)
    total = GROUPS * BLOCK
    return pl.pallas_call(
        functools.partial(reduce_kernel, names, schedule(1.0, 1.0)),
        name="weight_sums",
        out_shape=(
            jax.ShapeDtypeStruct((total, BLOCK), BF),
            jax.ShapeDtypeStruct((16, BLOCK), F32),
        ),
        in_specs=[pl.BlockSpec(memory_space=pl.ANY)] * 2,
        out_specs=[pl.BlockSpec(memory_space=pl.ANY)] * 2,
        scratch_shapes=[
            pltpu.VMEM((total, BLOCK), BF),
            pltpu.VMEM((total, BLOCK), BF),
            pltpu.VMEM((9, 16, BLOCK), F32),
        ]
        + [bufs[k] for k in names]
        + sems
        + [pltpu.SemaphoreType.DMA((4,))],
        compiler_params=pltpu.CompilerParams(
            collective_id=1, has_side_effects=True, vmem_limit_bytes=48 * 2**20
        ),
    )(rows, small)


def summed_over_items(totals, stats):
    if (lax.axis_size("dp"), lax.axis_size("seq")) != (4, 4):
        return lax.psum((*totals, stats), ("dp", "seq"))
    outer_gain, inner_gains, outer_biases, inner_biases, down, conv, up = totals
    rows = jnp.concatenate(
        [up[:, :BLOCK], up[:, BLOCK:], conv.reshape(-1, BLOCK), down], axis=0
    ).astype(BF)
    small = jnp.concatenate(
        [
            outer_gain.reshape(-1, BLOCK),
            inner_gains,
            outer_biases.reshape(-1, BLOCK),
            inner_biases,
            jnp.pad(stats[None], ((0, 0), (0, BLOCK - 3))),
        ],
        axis=0,
    )
    used = small.shape[0]
    small = jnp.pad(small, ((0, 16 - used), (0, 0)))
    rows, small = all_sum(rows, small)
    up = jnp.concatenate([rows[:BLOCK], rows[BLOCK : 2 * BLOCK]], axis=1).astype(F32)
    conv = rows[2 * BLOCK : 7 * BLOCK].reshape(5, BLOCK, BLOCK).astype(F32)
    down = rows[7 * BLOCK :].astype(F32)
    return (
        small[0:2].reshape(-1),
        small[2:4],
        small[4:8].reshape(2, -1),
        small[8:12],
        down,
        conv,
        up,
        small[12, :3],
    )


FILTER_TAPS = 5
FIRST_DILATION = 2
SECOND_DILATION = 128


def passed_along(value, axis, steps):
    count = lax.axis_size(axis)
    leading, last = (max(0, -steps), min(count, count - steps))
    return lax.ppermute(value, axis, [(source, source + steps) for source in range(leading, last)])


def norm_gelu(value, gain, shift):
    mean = jnp.mean(value, axis=-1, keepdims=True)
    centred = value - mean
    spread = jnp.mean(centred * centred, axis=-1, keepdims=True)
    return jax.nn.gelu(centred * lax.rsqrt(spread + 1e-05) * gain + shift)


def extend(block_index, backward):
    lower_rows = []
    upper_rows = []
    step = 1
    if backward:
        lower_rows.append(passed_along(block_index, "seq", step))
    else:
        lower_rows.append(passed_along(block_index, "seq", step))
    step = 1
    if backward:
        upper_rows.append(passed_along(block_index, "seq", -step))
    else:
        upper_rows.append(passed_along(block_index, "seq", -step))
    return jnp.concatenate(lower_rows + [block_index] + upper_rows, axis=1)


def take_taps(wide, starts, rows):
    return jnp.concatenate(
        [lax.dynamic_slice_in_dim(wide, start, rows, 1) for start in starts], axis=2
    )


def forward(input_rows, valid_mask, weights, starts):
    (
        gain_a,
        shift_a,
        bias_out,
        gain_b,
        gain_c,
        shift_b,
        shift_c,
        bias_in,
        bias_conv,
        weight_in,
        weight_conv,
        weight_out,
    ) = weights
    hidden_a, back_a = jax.vjp(norm_gelu, input_rows, gain_a, shift_a)
    low_a = hidden_a.astype(jnp.bfloat16)
    proj = jnp.dot(low_a, weight_in, preferred_element_type=jnp.float32) + bias_in
    hidden_b, back_b = jax.vjp(
        lambda value, gain, shift: norm_gelu(value, gain, shift) * valid_mask, proj, gain_b, shift_b
    )
    conv_in = hidden_b.astype(jnp.bfloat16)
    wide = extend(conv_in, False)
    taps = take_taps(wide, starts, input_rows.shape[1])
    flat_weight = weight_conv.reshape(-1, weight_conv.shape[2])
    conv = jnp.dot(taps, flat_weight, preferred_element_type=jnp.float32) + bias_conv
    hidden_c, back_c = jax.vjp(norm_gelu, conv, gain_c, shift_c)
    low_c = hidden_c.astype(jnp.bfloat16)
    branch = (
        jnp.dot(low_c, weight_out, preferred_element_type=jnp.float32) + bias_out
    ) * valid_mask
    return (input_rows + branch, branch, wide, (low_a, taps, low_c, back_a, back_b, back_c))


def backward(grad_out, valid_mask, weights, back_starts, saved):
    (
        gain_a,
        shift_a,
        bias_out,
        gain_b,
        gain_c,
        shift_b,
        shift_c,
        bias_in,
        bias_conv,
        weight_in,
        weight_conv,
        weight_out,
    ) = weights
    low_a, taps, low_c, back_a, back_b, back_c = saved
    grad_branch = grad_out * valid_mask
    low_branch = grad_branch.astype(jnp.bfloat16)
    grad_bias_out = jnp.sum(grad_branch, axis=(0, 1))
    grad_weight_out = jnp.einsum(
        "bri,brd->id", low_c, low_branch, preferred_element_type=jnp.float32
    )
    grad_hidden_c = jnp.einsum(
        "brd,id->bri", low_branch, weight_out, preferred_element_type=jnp.float32
    )
    grad_conv, grad_gain_c, grad_shift_c = back_c(grad_hidden_c)
    low_conv = grad_conv.astype(jnp.bfloat16)
    grad_bias_conv = jnp.sum(grad_conv, axis=(0, 1))
    grad_weight_conv = jnp.einsum(
        "brk,bro->ko", taps, low_conv, preferred_element_type=jnp.float32
    ).reshape(weight_conv.shape)
    wide_grad = extend(low_conv, True)
    grad_taps = take_taps(wide_grad, back_starts, grad_out.shape[1])
    turned = jnp.transpose(weight_conv, (1, 0, 2)).reshape(weight_conv.shape[1], -1)
    grad_hidden_b = jnp.einsum("brk,ik->bri", grad_taps, turned, preferred_element_type=jnp.float32)
    grad_proj, grad_gain_b, grad_shift_b = back_b(grad_hidden_b)
    low_proj = grad_proj.astype(jnp.bfloat16)
    grad_bias_in = jnp.sum(grad_proj, axis=(0, 1))
    grad_weight_in = jnp.einsum("brd,bri->di", low_a, low_proj, preferred_element_type=jnp.float32)
    grad_hidden_a = jnp.einsum(
        "bri,di->brd", low_proj, weight_in, preferred_element_type=jnp.float32
    )
    grad_inputs, grad_gain_a, grad_shift_a = back_a(grad_hidden_a)
    grads = (
        grad_gain_a,
        jnp.stack([grad_gain_b, grad_gain_c]),
        jnp.stack([grad_shift_a, grad_bias_out]),
        jnp.stack([grad_shift_b, grad_shift_c, grad_bias_in, grad_bias_conv]),
        grad_weight_in,
        grad_weight_conv,
        grad_weight_out,
    )
    return (grad_out + grad_inputs, grads)


def body(
    ends_in,
    lengths,
    outer_gain,
    inner_gains,
    outer_biases,
    inner_biases,
    down_in,
    conv_weight,
    up_out,
):
    weights = (
        outer_gain[0],
        outer_biases[0, 0],
        outer_biases[0, 1],
        inner_gains[0, 0],
        inner_gains[0, 1],
        inner_biases[0, 0],
        inner_biases[0, 1],
        inner_biases[0, 2],
        inner_biases[0, 3],
        down_in[0],
        conv_weight[0],
        up_out[0],
    )
    section = lax.axis_index("section")
    first_result = section == 0
    local = ends_in[0]
    micro_count = local.shape[0]
    rows = local.shape[2]
    width = local.shape[3]
    position = lax.axis_index("seq") * rows + jnp.arange(rows, dtype=jnp.int32)
    dilation_step = jnp.where(first_result, FIRST_DILATION, SECOND_DILATION).astype(jnp.int32)
    receptive_reach = FILTER_TAPS // 2 * SECOND_DILATION
    offsets = [(tap - FILTER_TAPS // 2) * dilation_step for tap in range(FILTER_TAPS)]
    starts = [receptive_reach + offset for offset in offsets]
    back_starts = [receptive_reach - offset for offset in offsets]

    def valid_rows(micro_index):
        index = jnp.clip(micro_index, 0, micro_count - 1)
        item_lengths = lax.dynamic_index_in_dim(lengths, index, 0, keepdims=False)
        return (position[None, :] < item_lengths[:, None]).astype(jnp.float32)[:, :, None]

    received = jnp.zeros(local.shape[1:], jnp.bfloat16)
    inputs_seen = []
    outputs_seen = []
    kept = []
    stats = jnp.zeros((3,), jnp.float32)
    for step in range(micro_count + 1):
        own = local[min(step, micro_count - 1)].astype(jnp.float32)
        input_rows = jnp.where(first_result, own, received.astype(jnp.float32))
        valid_mask = valid_rows(step - section)
        output_rows, branch, wide, saved = forward(input_rows, valid_mask, weights, starts)
        active = jnp.where(first_result, float(step < micro_count), float(step >= 1))
        stats = stats + active * jnp.stack(
            [
                jnp.sum(input_rows * input_rows * valid_mask),
                jnp.sum(branch * branch),
                jnp.sum(valid_mask),
            ]
        )
        inputs_seen.append(input_rows)
        outputs_seen.append(output_rows)
        kept.append(wide)
        if step < micro_count:
            received = passed_along(output_rows.astype(jnp.bfloat16), "section", 1)
    handed_rows = jnp.zeros(local.shape[1:], jnp.bfloat16)
    totals = None
    grads_seen = []
    for step in range(micro_count + 1):
        index = micro_count - step
        input_rows = inputs_seen[index]
        valid_mask = valid_rows(index - section)
        cotangent = local[max(micro_count - 1 - step, 0)].astype(jnp.float32)
        grad_out = jnp.where(first_result, handed_rows.astype(jnp.float32), cotangent)
        output_rows, branch, wide, saved = forward(input_rows, valid_mask, weights, starts)
        grad_inputs, step_grads = backward(grad_out, valid_mask, weights, back_starts, saved)
        active = jnp.where(first_result, float(step >= 1), float(step < micro_count))
        scaled = tuple((active * grad for grad in step_grads))
        if totals is None:
            totals = scaled
        else:
            totals = tuple((total + grad for total, grad in zip(totals, scaled)))
        grads_seen.append(grad_inputs)
        if step < micro_count:
            handed_rows = passed_along(grad_inputs.astype(jnp.bfloat16), "section", -1)
    ends_out = jnp.stack(
        [
            jnp.where(first_result, grads_seen[micro_count - slot], outputs_seen[slot + 1])
            for slot in range(micro_count)
        ]
    )[None]
    summed = summed_over_items(totals, stats)
    sums = summed[7]
    rms = jnp.sqrt(sums[:2] / (sums[2] * width))[None]
    return (
        ends_out,
        summed[0][None],
        summed[1][None],
        summed[2][None],
        summed[3][None],
        summed[4][None],
        summed[5][None],
        summed[6][None],
        rms,
    )


def solution(mesh):
    in_specs = (
        P("section", None, "dp", "seq", None),
        P(None, "dp"),
        P("section", None),
        P("section", None, None),
        P("section", None, None),
        P("section", None, None),
        P("section", None, None),
        P("section", None, None, None),
        P("section", None, None),
    )
    out_specs = (
        P("section", None, "dp", "seq", None),
        P("section", None),
        P("section", None, None),
        P("section", None, None),
        P("section", None, None),
        P("section", None, None),
        P("section", None, None, None),
        P("section", None, None),
        P("section", None),
    )
    return jax.shard_map(body, mesh=mesh, in_specs=in_specs, out_specs=out_specs, check_vma=False)
```

```python
import functools
import math

import jax
import jax.numpy as jnp
from jax import lax
from jax.experimental import pallas as pl
from jax.experimental.pallas import tpu as pltpu
from jax.sharding import PartitionSpec as P

MESH = pl.DeviceIdType.MESH
BF = jnp.bfloat16
F32 = jnp.float32
FILTER_TAPS = 5
FIRST_DILATION = 2
SECOND_DILATION = 128
REACH = FILTER_TAPS // 2
EPS = 1e-05
GELU_A = math.sqrt(2.0 / math.pi)
GELU_B = GELU_A * 0.044715
EDGE = 16

GROUPS = 9
BLOCK = 640
LROWS = 384
HALF = LROWS // 2
QUARTER = LROWS // 4
CHUNK = (BLOCK - LROWS) // 4
KINDS = (
    "ru", "rv", "za", "zb", "zc", "av", "au", "aw",
    "ze", "zm", "zo", "ex", "ey", "ge", "gn", "gd", "gf", "gp", "gq",
)
SMALL_KINDS = ("sx", "sy", "sa", "sb", "sc")
RECEIVE = dict(ru=HALF, rv=QUARTER, za=QUARTER, zb=QUARTER, fl=QUARTER, ze=3 * CHUNK, zm=2 * CHUNK,
               zo=CHUNK, ex=CHUNK, ey=CHUNK, tx=CHUNK, fz=CHUNK)
L_LEVELS = 8
Z_LEVELS = 9
TICKS = GROUPS + Z_LEVELS - 1


def aligned(offset):
    return offset if isinstance(offset, int) else pl.multiple_of(offset, 16)


def part(ref, offset, rows):
    return ref.at[pl.ds(aligned(offset), rows)]


def added(target, offset, sources, rows, tile=32):
    for start in range(0, rows, tile):
        total = None
        for ref, at in sources:
            value = ref[pl.ds(aligned(at + start), tile), :]
            if len(sources) > 2:
                value = value.astype(F32)
            total = value if total is None else total + value
        target[pl.ds(aligned(offset + start), tile), :] = total.astype(BF)


class WeightSums:
    def __init__(self, grad, res, small, buffers, send, recv, local, small_send, small_recv):
        self.grad, self.res, self.small, self.r = grad, res, small, buffers
        self.send, self.recv, self.local = send, recv, local
        self.small_send, self.small_recv = small_send, small_recv
        self.c = lax.axis_index("section")
        self.dp = lax.axis_index("dp")
        self.z = lax.axis_index("seq")
        self.x = lax.rem(self.dp, 2)
        self.y = self.dp // 2
        z = self.z
        self.upper = z // 2
        self.end = jnp.logical_or(z == 0, z == 3)
        self.mid = jnp.logical_not(self.end)
        self.dp_x = self.dp + 1 - 2 * self.x
        self.dp_y = lax.rem(self.dp + 2, 4)
        self.px = (self.c, self.dp_x, z)
        self.py = (self.c, self.dp_y, z)
        self.pair = (self.c, self.dp, 1 - z + 4 * self.upper)
        self.other = (self.c, self.dp, jnp.clip(3 - z, 1, 2))

    def copy(self, kind, g, source, target, to):
        j = KINDS.index(kind)
        return pltpu.make_async_remote_copy(
            src_ref=source, dst_ref=target, send_sem=self.send.at[g, j], recv_sem=self.recv.at[g, j],
            device_id=to, device_id_type=MESH)

    def square(self, g):
        odd = lax.rem(g, 2)
        u = jnp.where(odd == 0, self.x, self.y)
        v = jnp.where(odd == 0, self.y, self.x)
        to_u = (self.c, jnp.where(odd == 0, self.dp_x, self.dp_y), self.z)
        to_v = (self.c, jnp.where(odd == 0, self.dp_y, self.dp_x), self.z)
        base = g * BLOCK
        own_half = base + u * HALF
        own = own_half + v * QUARTER
        beside = own_half + (1 - v) * QUARTER
        return base, u, v, to_u, to_v, own, beside

    def square_copy(self, kind, g):
        base, u, v, to_u, to_v, own, beside = self.square(g)
        grad, res, r = self.grad, self.res, self.r
        final = r["fl"].at[g]
        if kind == "ru":
            return self.copy(kind, g, part(grad, base + (1 - u) * HALF, HALF), r["ru"].at[g], to_u)
        if kind == "rv":
            return self.copy(kind, g, part(grad, beside, QUARTER), r["rv"].at[g], to_v)
        if kind == "za":
            return self.copy(kind, g, part(grad, own, QUARTER), r["za"].at[g], self.pair)
        if kind == "zb":
            return self.copy(kind, g, part(grad, own, QUARTER), r["zb"].at[g], self.other)
        if kind == "zc":
            return self.copy(kind, g, final, final, self.pair)
        if kind == "av":
            return self.copy(kind, g, final, part(res, own, QUARTER), to_v)
        if kind == "au":
            return self.copy(kind, g, final, part(res, own, QUARTER), to_u)
        if kind == "aw":
            return self.copy(kind, g, part(res, beside, QUARTER), part(res, beside, QUARTER), to_u)
        return pltpu.make_async_copy(final, part(res, own, QUARTER), self.local.at[g, 0])

    def square_level(self, g, level):
        base, u, v, to_u, to_v, own, beside = self.square(g)
        grad, r = self.grad, self.r
        copy = functools.partial(self.square_copy, g=g)
        if level == 0:
            copy("ru").start()
        elif level == 1:
            copy("ru").wait_recv()
            added(grad, beside, [(grad, beside), (r["ru"].at[g], (1 - v) * QUARTER)], QUARTER)
            copy("rv").start()
            added(grad, own, [(grad, own), (r["ru"].at[g], v * QUARTER)], QUARTER)
        elif level == 2:
            copy("rv").wait_recv()
            added(grad, own, [(grad, own), (r["rv"].at[g], 0)], QUARTER)

            @pl.when(self.end)
            def _():
                copy("za").start()
        elif level == 3:

            @pl.when(self.mid)
            def _():
                copy("za").wait_recv()
                added(grad, own, [(grad, own), (r["za"].at[g], 0)], QUARTER)
                copy("zb").start()
        elif level == 4:

            @pl.when(self.mid)
            def _():
                copy("zb").wait_recv()
                added(r["fl"].at[g], 0, [(grad, own), (r["zb"].at[g], 0)], QUARTER)
                copy("zc").start()
                copy("av").start()
                copy("au").start()
                copy("fl").start()
        elif level == 5:

            @pl.when(self.end)
            def _():
                copy("zc").wait_recv()
                copy("av").start()
                copy("au").start()
                copy("fl").start()
        elif level == 6:
            copy("av").wait_recv()
            copy("aw").start()
        elif level == 7:
            copy("au").wait_recv()
            copy("aw").wait_recv()
            copy("fl").wait()

    def line(self, g):
        base = g * BLOCK + LROWS
        upper = self.upper
        three = base + CHUNK * (1 - upper)
        far = base + 2 * CHUNK * (1 - upper)
        near = base + 2 * CHUNK * upper
        outer = base + 3 * CHUNK * upper
        own = base + CHUNK * self.z
        return three, far, near, outer, own

    def line_copy(self, kind, g):
        three, far, near, outer, own = self.line(g)
        grad, res, r = self.grad, self.res, self.r
        base = g * BLOCK + LROWS
        final = r["fz"].at[g]
        here = part(res, own, CHUNK)
        if kind == "ze":
            return self.copy(kind, g, part(grad, three, 3 * CHUNK), r["ze"].at[g], self.pair)
        if kind == "zm":
            return self.copy(kind, g, part(grad, far, 2 * CHUNK), r["zm"].at[g], self.other)
        if kind == "zo":
            return self.copy(kind, g, part(grad, outer, CHUNK), r["zo"].at[g], self.pair)
        if kind == "ex":
            return self.copy(kind, g, part(grad, own, CHUNK), r["ex"].at[g], self.px)
        if kind == "ey":
            return self.copy(kind, g, r["tx"].at[g], r["ey"].at[g], self.py)
        if kind in ("ge", "gd"):
            return self.copy(kind, g, final, here, self.pair)
        if kind == "gn":
            return self.copy(kind, g, final, here, self.other)
        if kind == "gf":
            rows = part(res, outer, CHUNK)
            return self.copy(kind, g, rows, rows, self.other)
        if kind == "gp":
            rows = part(res, base + CHUNK * (3 - self.z), CHUNK)
            return self.copy(kind, g, rows, rows, self.pair)
        if kind == "gq":
            rows = part(res, base + 3 * CHUNK * (1 - self.upper), CHUNK)
            return self.copy(kind, g, rows, rows, self.pair)
        return pltpu.make_async_copy(final, here, self.local.at[g, 1])

    def line_level(self, g, level):
        three, far, near, outer, own = self.line(g)
        grad, r = self.grad, self.r
        copy = functools.partial(self.line_copy, g=g)
        if level == 0:

            @pl.when(self.end)
            def _():
                copy("ze").start()
        elif level == 1:

            @pl.when(self.mid)
            def _():
                copy("ze").wait_recv()
                added(grad, far, [(grad, far), (r["ze"].at[g], far - three)], 2 * CHUNK)
                copy("zm").start()
        elif level == 2:

            @pl.when(self.mid)
            def _():
                copy("zm").wait_recv()
                added(grad, outer, [(grad, outer), (r["zm"].at[g], outer - near)], CHUNK)
                copy("zo").start()
                added(grad, own, [(grad, own), (r["ze"].at[g], own - three), (r["zm"].at[g], own - near)], CHUNK)
                copy("ex").start()
        elif level == 3:

            @pl.when(self.end)
            def _():
                copy("zo").wait_recv()
                added(grad, own, [(grad, own), (r["zo"].at[g], 0)], CHUNK)
                copy("ex").start()
        elif level == 4:
            copy("ex").wait_recv()
            added(r["tx"].at[g], 0, [(grad, own), (r["ex"].at[g], 0)], CHUNK)
            copy("ey").start()
        elif level == 5:
            copy("ey").wait_recv()
            added(r["fz"].at[g], 0, [(r["tx"].at[g], 0), (r["ey"].at[g], 0)], CHUNK)
            copy("fz").start()

            @pl.when(self.end)
            def _():
                copy("ge").start()

            @pl.when(self.mid)
            def _():
                copy("gn").start()
                copy("gd").start()
        elif level == 6:

            @pl.when(self.mid)
            def _():
                copy("ge").wait_recv()
                copy("gf").start()
                copy("gn").wait_recv()
                copy("gp").start()
        elif level == 7:

            @pl.when(self.mid)
            def _():
                copy("gf").wait_recv()
                copy("gq").start()
        elif level == 8:
            copy("fz").wait()

            @pl.when(self.end)
            def _():
                copy("gd").wait_recv()
                copy("gp").wait_recv()
                copy("gq").wait_recv()

    def small_copy(self, kind):
        j = SMALL_KINDS.index(kind)
        s = self.small
        source, target, to = dict(
            sx=(s.at[0], s.at[5], self.px),
            sy=(s.at[1], s.at[6], self.py),
            sa=(s.at[2], s.at[7], self.pair),
            sb=(s.at[3], s.at[8], self.other),
            sc=(s.at[4], s.at[4], self.pair),
        )[kind]
        return pltpu.make_async_remote_copy(
            src_ref=source, dst_ref=target, send_sem=self.small_send.at[j], recv_sem=self.small_recv.at[j],
            device_id=to, device_id_type=MESH)

    def small_level(self, level):
        copy, s = self.small_copy, self.small
        if level == 0:
            copy("sx").start()
        elif level == 1:
            copy("sx").wait_recv()
            s[1] = s[0] + s[5]
            copy("sy").start()
        elif level == 2:
            copy("sy").wait_recv()
            s[2] = s[1] + s[6]

            @pl.when(self.end)
            def _():
                copy("sa").start()
        elif level == 3:

            @pl.when(self.mid)
            def _():
                copy("sa").wait_recv()
                s[3] = s[2] + s[7]
                copy("sb").start()
        elif level == 4:

            @pl.when(self.mid)
            def _():
                copy("sb").wait_recv()
                s[4] = s[3] + s[8]
                copy("sc").start()
        elif level == 5:

            @pl.when(self.end)
            def _():
                copy("sc").wait_recv()

    def tick(self, t):
        for level in reversed(range(Z_LEVELS)):
            g = t - level

            @pl.when(jnp.logical_and(g >= 0, g < GROUPS))
            def _():
                if level < L_LEVELS:
                    self.square_level(g, level)
                self.line_level(g, level)

        for level in range(6):

            @pl.when(t == level)
            def _():
                self.small_level(level)

    def drain(self):
        def group(g, carry):
            for kind in ("ru", "rv", "av", "au", "aw"):
                self.square_copy(kind, g).wait_send()
            for kind in ("ex", "ey"):
                self.line_copy(kind, g).wait_send()

            @pl.when(self.end)
            def _():
                self.square_copy("za", g).wait_send()
                self.line_copy("ze", g).wait_send()
                self.line_copy("ge", g).wait_send()

            @pl.when(self.mid)
            def _():
                self.square_copy("zb", g).wait_send()
                self.square_copy("zc", g).wait_send()
                for kind in ("zm", "zo", "gn", "gd", "gf", "gp", "gq"):
                    self.line_copy(kind, g).wait_send()

            return carry

        lax.fori_loop(0, GROUPS, group, 0)
        self.small_copy("sx").wait_send()
        self.small_copy("sy").wait_send()

        @pl.when(self.end)
        def _():
            self.small_copy("sa").wait_send()

        @pl.when(self.mid)
        def _():
            self.small_copy("sb").wait_send()
            self.small_copy("sc").wait_send()


def normed(value):
    mean = jnp.mean(value, axis=-1, keepdims=True)
    centred = value - mean
    spread = jnp.mean(centred * centred, axis=-1, keepdims=True)
    scale = lax.rsqrt(spread + EPS)
    return centred * scale, mean, scale


def gelu(v):
    half = 0.5 * v
    t = jnp.tanh(v * (GELU_A + GELU_B * (v * v)))
    return half + half * t


def gelu_slope(v):
    square = v * v
    t = jnp.tanh(v * (GELU_A + GELU_B * square))
    return (0.5 + 0.5 * t) + (0.5 * v) * (1.0 - t * t) * (GELU_A + (3.0 * GELU_B) * square)


def norm_gelu_back(grad, n, scale, gain, shift):
    dv = grad * gelu_slope(n * gain + shift)
    terms = dv * n
    dn = dv * gain
    first = jnp.mean(dn, axis=-1, keepdims=True)
    second = jnp.mean(dn * n, axis=-1, keepdims=True)
    return dv, terms, scale * (dn - first - n * second)


def fold(value):
    rows, width = value.shape
    return jnp.sum(value.reshape(rows // 8, 8, width), axis=0)


def nn(a, b):
    return jnp.dot(a, b, preferred_element_type=F32)


def nt(a, b):
    return lax.dot_general(a, b, (((1,), (1,)), ((), ())), preferred_element_type=F32)


def tn(a, b):
    return lax.dot_general(a, b, (((0,), (0,)), ((), ())), preferred_element_type=F32)


TILE = 32


def blocks_kernel(
    names, with_sums, last,
    ends, lengths, outer_gain, inner_gains, outer_biases, inner_biases, down_hbm, conv_hbm, up_hbm,
    ends_out, res, small_out,
    down, conv, up, X, GY, HA, CW, HC, GCW, GP, NB, NC, MA, RA, RB, RC, proj, wide, handing, taps, oacc, iacc, grad, small,
    *rest,
):
    buffers = dict(zip(names, rest[: len(names)]))
    send, recv, local, small_send, small_recv, load, hand_send, hand_recv, halo_send, halo_recv, store = rest[len(names) :]
    micro, rows, width = X.shape
    inner = down.shape[1]
    section = lax.axis_index("section")
    dp = lax.axis_index("dp")
    z = lax.axis_index("seq")
    first = section == 0
    second = section == 1
    has_left = z > 0
    has_right = z < last
    across = (1 - section, dp, z)
    left = (section, dp, jnp.maximum(z - 1, 0))
    right = (section, dp, jnp.minimum(z + 1, last))
    sums = WeightSums(grad, res, small, buffers, send, recv, local, small_send, small_recv)

    def when(condition, act):
        pl.when(condition)(lambda: act() and None)

    def weight_load(j):
        return pltpu.make_async_copy((down_hbm, conv_hbm, up_hbm)[j], (down, conv, up)[j], load.at[micro + j])

    def end_load(mb, target):
        return pltpu.make_async_copy(ends.at[mb], target.at[mb], load.at[mb])

    @pl.when(first)
    def _():
        for mb in range(micro):
            end_load(mb, X).start()
            if mb == 0:
                weight_load(0).start()
                weight_load(1).start()
                weight_load(2).start()

    @pl.when(second)
    def _():
        for j in range(3):
            weight_load(j).start()
        for mb in range(micro):
            end_load(mb, GY).start()

    barrier = pltpu.get_barrier_semaphore()

    def greet(to):
        pl.semaphore_signal(barrier, inc=1, device_id=to, device_id_type=MESH)

    greet(across)
    when(has_left, lambda: greet(left))
    when(has_right, lambda: greet(right))
    if with_sums:
        greet(sums.px)
        greet(sums.py)

    oacc[...] = jnp.zeros_like(oacc)
    iacc[...] = jnp.zeros_like(iacc)
    edge = jnp.zeros((rows, inner), BF)
    for mb in range(micro):

        @pl.when(jnp.logical_not(has_left))
        def _():
            CW[mb, 0:rows, :] = edge
            GCW[mb, 0:rows, :] = edge

        @pl.when(jnp.logical_not(has_right))
        def _():
            CW[mb, 2 * rows : 3 * rows, :] = edge
            GCW[mb, 2 * rows : 3 * rows, :] = edge

    peers = (3 if with_sums else 1) + has_left.astype(jnp.int32) + has_right.astype(jnp.int32)
    pl.semaphore_wait(barrier, peers)

    def halo_copies(ref, which, mb):
        def make(side, count):
            if side == 0:
                source, target, to = ref.at[mb, pl.ds(2 * rows - count, count)], ref.at[mb, pl.ds(rows - count, count)], right
            else:
                source, target, to = ref.at[mb, pl.ds(rows, count)], ref.at[mb, pl.ds(2 * rows, count)], left
            return pltpu.make_async_remote_copy(
                src_ref=source, dst_ref=target, send_sem=halo_send.at[which, mb, side],
                recv_sem=halo_recv.at[which, mb, side], device_id=to, device_id_type=MESH)

        return make

    def halo(ref, which, mb, act_right, act_left):
        make = halo_copies(ref, which, mb)
        for mine, count in ((first, EDGE), (second, rows)):

            @pl.when(mine)
            def _():
                when(act_right[0], lambda: act_right[1](make(0, count)))
                when(act_left[0], lambda: act_left[1](make(1, count)))

    def halo_start(ref, which, mb):
        go = lambda c: c.start()
        halo(ref, which, mb, (has_right, go), (has_left, go))

    def halo_arrived(ref, which, mb):
        go = lambda c: c.wait_recv()
        halo(ref, which, mb, (has_left, go), (has_right, go))

    def halo_sent(ref, which, mb):
        go = lambda c: c.wait_send()
        halo(ref, which, mb, (has_right, go), (has_left, go))

    def shifted(ref, mb, k, sign, target, at):
        shift = sign * (k - REACH)

        @pl.when(first)
        def _():
            target[pl.ds(at, rows), :] = ref[mb, pl.ds(rows + shift * FIRST_DILATION, rows), :]

        @pl.when(second)
        def _():
            target[pl.ds(at, rows), :] = ref[mb, pl.ds(rows + shift * SECOND_DILATION, rows), :]

    def hand_over(mb, target):
        slot = lax.rem(mb, 2)
        return pltpu.make_async_remote_copy(
            src_ref=handing.at[slot], dst_ref=target.at[mb], send_sem=hand_send.at[mb], recv_sem=hand_recv.at[mb],
            device_id=across, device_id_type=MESH)

    def store_end(mb):
        return pltpu.make_async_copy(wide.at[lax.rem(mb, 2)], ends_out.at[mb], store.at[mb])

    def tiles(act):
        def step(i, carry):
            act(pl.ds(pl.multiple_of(i * TILE, TILE), TILE), i * TILE)
            return carry

        lax.fori_loop(0, rows // TILE, step, 0)

    def valid_of(mb, start):
        position = z * rows + start + lax.broadcasted_iota(jnp.int32, (TILE, 1), 0)
        return (position < lengths[mb]).astype(F32)

    def forward_a(mb):
        when(first, lambda: end_load(mb, X).wait())
        when(second, lambda: hand_over(mb, X).wait_recv())

        def norm_a(at, start):
            value = X[mb, at, :].astype(F32)
            oacc[3] += fold(value * value * valid_of(mb, start))
            n, mean, scale = normed(value)
            MA[mb, at, :] = mean
            RA[mb, at, :] = scale
            HA[mb, at, :] = gelu(n * outer_gain[...] + outer_biases[0:1, :]).astype(BF)

        tiles(norm_a)
        when(mb == 0, lambda: weight_load(0).wait())
        proj[...] = nn(HA[mb], down[...])

        def norm_b(at, start):
            n, _, scale = normed(proj[at, :] + inner_biases[2:3, :])
            NB[mb, at, :] = n
            RB[mb, at, :] = scale
            value = gelu(n * inner_gains[0:1, :] + inner_biases[0:1, :]) * valid_of(mb, start)
            CW[mb, pl.ds(pl.multiple_of(rows + start, TILE), TILE), :] = value.astype(BF)

        tiles(norm_b)
        halo_start(CW, 0, mb)

    def forward_b(mb):
        slot = lax.rem(mb, 2)
        halo_arrived(CW, 0, mb)
        for k in range(FILTER_TAPS):
            shifted(CW, mb, k, 1, taps, k * rows)

        @pl.when(mb == 0)
        def _():
            weight_load(1).wait()
            weight_load(2).wait()

        total = nn(taps[0:rows, :], conv[0])
        for k in range(1, FILTER_TAPS):
            total = total + nn(taps[k * rows : (k + 1) * rows, :], conv[k])
        proj[...] = total

        def norm_c(at, start):
            n, _, scale = normed(proj[at, :] + inner_biases[3:4, :])
            NC[mb, at, :] = n
            RC[mb, at, :] = scale
            value = gelu(n * inner_gains[1:2, :] + inner_biases[1:2, :]) * valid_of(mb, start)
            HC[mb, at, :] = value.astype(BF)

        tiles(norm_c)

        @pl.when(mb >= 2)
        def _():
            when(first, lambda: hand_over(mb - 2, X).wait_send())
            when(second, lambda: store_end(mb - 2).wait())

        wide[slot] = nn(HC[mb], up[...])

        def close(at, start):
            branch = (wide[slot, at, :] + outer_biases[1:2, :]) * valid_of(mb, start)
            oacc[4] += fold(branch * branch)
            value = X[mb, at, :].astype(F32) + branch

            @pl.when(first)
            def _():
                handing[slot, at, :] = value.astype(BF)

            @pl.when(second)
            def _():
                wide[slot, at, :] = value

        tiles(close)
        when(first, lambda: hand_over(mb, X).start())
        when(second, lambda: store_end(mb).start())

    def backward_a(mb):
        when(first, lambda: hand_over(mb, GY).wait_recv())
        when(second, lambda: end_load(mb, GY).wait())
        proj[...] = nt(GY[mb], up[...])

        def norm_c(at, start):
            valid = valid_of(mb, start)
            oacc[2] += fold(GY[mb, at, :].astype(F32) * valid)
            dv, terms, dz = norm_gelu_back(
                proj[at, :] * valid, NC[mb, at, :], RC[mb, at, :], inner_gains[1:2, :], inner_biases[1:2, :]
            )
            iacc[3] += fold(terms)
            iacc[4] += fold(dv)
            iacc[5] += fold(dz)
            GCW[mb, pl.ds(pl.multiple_of(rows + start, TILE), TILE), :] = dz.astype(BF)

        tiles(norm_c)
        halo_start(GCW, 1, mb)

    def backward_b(mb):
        slot = lax.rem(mb, 2)
        halo_arrived(GCW, 1, mb)
        for k in range(FILTER_TAPS):
            shifted(GCW, mb, k, -1, taps, k * rows)
        total = nt(taps[0:rows, :], conv[0])
        for k in range(1, FILTER_TAPS):
            total = total + nt(taps[k * rows : (k + 1) * rows, :], conv[k])
        proj[...] = total

        def norm_b(at, start):
            dv, terms, dz = norm_gelu_back(
                proj[at, :] * valid_of(mb, start), NB[mb, at, :], RB[mb, at, :], inner_gains[0:1, :], inner_biases[0:1, :]
            )
            iacc[0] += fold(terms)
            iacc[1] += fold(dv)
            iacc[2] += fold(dz)
            GP[mb, at, :] = dz.astype(BF)

        tiles(norm_b)

        @pl.when(mb >= 2)
        def _():
            when(second, lambda: hand_over(mb - 2, GY).wait_send())
            when(first, lambda: store_end(mb - 2).wait())

        wide[slot] = nt(GP[mb], down[...])

        def norm_a(at, start):
            scale = RA[mb, at, :]
            n = (X[mb, at, :].astype(F32) - MA[mb, at, :]) * scale
            dv, terms, dz = norm_gelu_back(wide[slot, at, :], n, scale, outer_gain[...], outer_biases[0:1, :])
            oacc[0] += fold(terms)
            oacc[1] += fold(dv)
            value = GY[mb, at, :].astype(F32) + dz

            @pl.when(second)
            def _():
                handing[slot, at, :] = value.astype(BF)

            @pl.when(first)
            def _():
                wide[slot, at, :] = value

        tiles(norm_a)
        when(second, lambda: hand_over(mb, GY).start())
        when(first, lambda: store_end(mb).start())

    def staggered(a, b):
        def step(i, carry):
            when(i < micro, lambda: a(i))
            when(i >= 1, lambda: b(i - 1))
            return carry

        lax.fori_loop(0, micro + 1, step, 0)

    staggered(forward_a, forward_b)
    for mb in range(micro - 2, micro):
        when(second, functools.partial(lambda m: store_end(m).wait(), mb))
        when(first, functools.partial(lambda m: hand_over(m, X).wait_send(), mb))
    staggered(backward_a, backward_b)

    def weights_of(g):
        @pl.when(g == 0)
        def _():
            c = HC[...].reshape(micro * rows, inner)
            for h in range(2):
                y = GY[:, :, h * inner : (h + 1) * inner].reshape(micro * rows, inner)
                grad[h * BLOCK : (h + 1) * BLOCK, :] = tn(c, y).astype(BF)

        for k in range(FILTER_TAPS):

            @pl.when(g == 2 + k)
            def _():
                for mb in range(micro):
                    shifted(CW, mb, k, 1, taps, mb * rows)

        @pl.when(jnp.logical_and(g >= 2, g < 2 + FILTER_TAPS))
        def _():
            c = taps[0 : micro * rows, :]
            y = GCW[:, rows : 2 * rows, :].reshape(micro * rows, inner)
            grad[pl.ds(pl.multiple_of(g * BLOCK, BLOCK), BLOCK), :] = tn(c, y).astype(BF)

        @pl.when(g == 2 + FILTER_TAPS)
        def _():
            y = GP[...].reshape(micro * rows, inner)
            for h in range(2):
                at = (2 + FILTER_TAPS + h) * BLOCK
                a = HA[:, :, h * inner : (h + 1) * inner].reshape(micro * rows, inner)
                grad[at : at + BLOCK, :] = tn(a, y).astype(BF)

    def row(value):
        return jnp.sum(value, axis=0, keepdims=True)

    small[0] = jnp.zeros_like(small[0])
    place = 0
    for j, ref in ((0, oacc), (None, 0), (None, 3), (1, oacc), (2, oacc), (None, 1), (None, 4), (None, 2), (None, 5)):
        if j is None:
            small[0, place : place + 1, :] = row(iacc[ref])
            place += 1
        else:
            value = row(oacc[j])
            small[0, place : place + 1, :] = value[:, :inner]
            small[0, place + 1 : place + 2, :] = value[:, inner:]
            place += 2
    for j in (3, 4):
        value = row(oacc[j])
        small[0, place : place + 1, :] = value[:, :inner] + value[:, inner:]
        place += 1
    count = jnp.float32(0)
    for mb in range(micro):
        count += jnp.clip(lengths[mb] - z * rows, 0, rows).astype(F32)
    small[0, place : place + 1, :] = jnp.zeros((1, inner), F32) + count

    if with_sums:

        def step(t, carry):
            when(t < GROUPS, lambda: weights_of(t))
            sums.tick(t)
            return carry

        lax.fori_loop(0, TICKS, step, 0)
        sums.drain()
        done = pltpu.make_async_copy(small.at[4], small_out, load.at[0])
        done.start()
        done.wait()
    else:

        def step(t, carry):
            weights_of(t)
            return carry

        lax.fori_loop(0, GROUPS, step, 0)
        done = pltpu.make_async_copy(small.at[0], small_out, load.at[0])
        done.start()
        done.wait()
        done = pltpu.make_async_copy(grad, res, load.at[1])
        done.start()
        done.wait()
    for mb in range(micro):
        if mb >= micro - 2:
            when(first, functools.partial(lambda m: store_end(m).wait(), mb))
            when(second, functools.partial(lambda m: hand_over(m, GY).wait_send(), mb))
        halo_sent(CW, 0, mb)
        halo_sent(GCW, 1, mb)


def run_blocks(mesh_shape, ends, lengths, outer_gain, inner_gains, outer_biases, inner_biases, down, conv, up):
    micro, rows, width = ends.shape
    inner = down.shape[1]
    taps = conv.shape[0]
    with_sums = (mesh_shape["dp"], mesh_shape["seq"]) == (4, 4)
    buffers = {k: pltpu.VMEM((GROUPS, n, BLOCK), BF) for k, n in RECEIVE.items()} if with_sums else {}
    names = tuple(buffers)
    total = GROUPS * BLOCK
    anywhere = pl.BlockSpec(memory_space=pl.ANY)
    vmem = pl.BlockSpec(memory_space=pltpu.VMEM)
    dma = pltpu.SemaphoreType.DMA
    scratch = [
        pltpu.VMEM(down.shape, BF),
        pltpu.VMEM(conv.shape, BF),
        pltpu.VMEM(up.shape, BF),
        pltpu.VMEM((micro, rows, width), BF),
        pltpu.VMEM((micro, rows, width), BF),
        pltpu.VMEM((micro, rows, width), BF),
        pltpu.VMEM((micro, 3 * rows, inner), BF),
        pltpu.VMEM((micro, rows, inner), BF),
        pltpu.VMEM((micro, 3 * rows, inner), BF),
        pltpu.VMEM((micro, rows, inner), BF),
        pltpu.VMEM((micro, rows, inner), F32),
        pltpu.VMEM((micro, rows, inner), F32),
        pltpu.VMEM((micro, rows, 1), F32),
        pltpu.VMEM((micro, rows, 1), F32),
        pltpu.VMEM((micro, rows, 1), F32),
        pltpu.VMEM((micro, rows, 1), F32),
        pltpu.VMEM((rows, inner), F32),
        pltpu.VMEM((2, rows, width), F32),
        pltpu.VMEM((2, rows, width), BF),
        pltpu.VMEM((taps * rows, inner), BF),
        pltpu.VMEM((5, 8, width), F32),
        pltpu.VMEM((6, 8, inner), F32),
        pltpu.VMEM((total, BLOCK), BF),
        pltpu.VMEM((9, 16, inner), F32),
        *[buffers[k] for k in names],
        dma((GROUPS, len(KINDS))),
        dma((GROUPS, len(KINDS))),
        dma((GROUPS, 2)),
        dma((len(SMALL_KINDS),)),
        dma((len(SMALL_KINDS),)),
        dma((micro + 3,)),
        dma((micro,)),
        dma((micro,)),
        dma((2, micro, 2)),
        dma((2, micro, 2)),
        dma((micro,)),
    ]
    flops = 2 * 3 * micro * rows * (2 * width * inner + taps * inner * inner)
    return pl.pallas_call(
        functools.partial(blocks_kernel, names, with_sums, mesh_shape["seq"] - 1),
        name="two_blocks",
        out_shape=(
            jax.ShapeDtypeStruct((micro, rows, width), F32),
            jax.ShapeDtypeStruct((total, BLOCK), BF),
            jax.ShapeDtypeStruct((16, inner), F32),
        ),
        in_specs=[anywhere, pl.BlockSpec(memory_space=pltpu.SMEM), vmem, vmem, vmem, vmem, anywhere, anywhere, anywhere],
        out_specs=[anywhere] * 3,
        scratch_shapes=scratch,
        cost_estimate=pl.CostEstimate(flops=flops, bytes_accessed=40 * 2**20, transcendentals=0),
        compiler_params=pltpu.CompilerParams(collective_id=1, has_side_effects=True, vmem_limit_bytes=62 * 2**20),
    )(ends, lengths, outer_gain, inner_gains, outer_biases, inner_biases, down, conv, up)


def body(
    mesh_shape, ends_in, lengths, outer_gain, inner_gains, outer_biases, inner_biases, down_in, conv_weight, up_out
):
    width = ends_in.shape[-1]
    ends, rows, small = run_blocks(
        mesh_shape, ends_in.reshape(ends_in.shape[1], -1, width), lengths.reshape(-1), outer_gain, inner_gains[0],
        outer_biases[0], inner_biases[0], down_in[0], conv_weight[0], up_out[0],
    )
    if (mesh_shape["dp"], mesh_shape["seq"]) != (4, 4):
        rows, small = lax.psum((rows.astype(F32), small), ("dp", "seq"))
    up = jnp.concatenate([rows[:BLOCK], rows[BLOCK : 2 * BLOCK]], axis=1).astype(F32)
    conv = rows[2 * BLOCK : (2 + FILTER_TAPS) * BLOCK].reshape(conv_weight.shape[1:]).astype(F32)
    down = rows[(2 + FILTER_TAPS) * BLOCK :].astype(F32)
    rms = jnp.sqrt(jnp.sum(small[12:14], axis=1) / (small[14, 0] * width))
    return (
        ends.reshape(ends_in.shape),
        small[0:2].reshape(1, -1),
        small[None, 2:4],
        small[4:8].reshape(1, 2, -1),
        small[None, 8:12],
        down[None],
        conv[None],
        up[None],
        rms[None],
    )


def solution(mesh):
    in_specs = (
        P("section", None, "dp", "seq", None),
        P(None, "dp"),
        P("section", None),
        P("section", None, None),
        P("section", None, None),
        P("section", None, None),
        P("section", None, None),
        P("section", None, None, None),
        P("section", None, None),
    )
    out_specs = (
        P("section", None, "dp", "seq", None),
        P("section", None),
        P("section", None, None),
        P("section", None, None),
        P("section", None, None),
        P("section", None, None),
        P("section", None, None, None),
        P("section", None, None),
        P("section", None),
    )
    return jax.shard_map(
        functools.partial(body, dict(mesh.shape)), mesh=mesh, in_specs=in_specs, out_specs=out_specs, check_vma=False
    )
```

```python
import functools
import math

import jax
import jax.numpy as jnp
from jax import lax
from jax.experimental import pallas as pl
from jax.experimental.pallas import tpu as pltpu
from jax.sharding import PartitionSpec as P

MESH = pl.DeviceIdType.MESH
BF = jnp.bfloat16
F32 = jnp.float32
FILTER_TAPS = 5
FIRST_DILATION = 2
SECOND_DILATION = 128
REACH = FILTER_TAPS // 2
EPS = 1e-05
GELU_A = math.sqrt(2.0 / math.pi)
GELU_B = GELU_A * 0.044715
EDGE = 16

BLOCK = 640
UP_BLOCKS = 2
DOWN_AT = UP_BLOCKS + FILTER_TAPS
BLOCKS = DOWN_AT + 2
GROUPS = 10
ROWS = BLOCKS * BLOCK // GROUPS
LROWS = 384
HALF = LROWS // 2
QUARTER = LROWS // 4
CHUNK = (ROWS - LROWS) // 4
KINDS = (
    "ru", "rv", "za", "zb", "zc", "av", "au", "aw",
    "ze", "zm", "zo", "ex", "ey", "ge", "gn", "gd", "gf", "gp", "gq",
)
SMALL_KINDS = ("sx", "sy", "sa", "sb", "sc")
RECEIVE = dict(ru=HALF, rv=QUARTER, za=QUARTER, zb=QUARTER, fl=QUARTER, ze=3 * CHUNK, zm=2 * CHUNK,
               zo=CHUNK, ex=CHUNK, ey=CHUNK, tx=CHUNK, fz=CHUNK)
L_LEVELS = 8
Z_LEVELS = 9
L_STRIDE, Z_STRIDE, Z_LATE, GAP = 1, 1, 0, 1
FA, FB, WU, BA, BB, WC, WD = range(1, 8)
FIRST_PLAN = (
    (FA, 0, 0), (FA, 1, 0), (FB, 0, 0), (FA, 2, 0), (FB, 1, 0), (FA, 3, 0), (FB, 2, 0), (FB, 3, 0), (BA, 0, 0), (BA, 1, 0), (BB, 0, 0), (BA, 2, 0), (BB, 1, 0), (WU, 0, 1), (BA, 3, 0), (BB, 2, 0), (BB, 3, 1), (WC, 0, 1), (WC, 1, 1), (WC, 2, 1), (WC, 3, 1), (WC, 4, 1), (WD, 0, 2),
)
SECOND_PLAN = (
    (FA, 0, 0), (FA, 1, 0), (FB, 0, 0), (FA, 2, 0), (FB, 1, 0), (FA, 3, 0), (FB, 2, 0), (BA, 0, 0), (FB, 3, 0), (WU, 0, 1), (BA, 1, 0), (BA, 2, 0), (BA, 3, 0), (BB, 0, 1), (BB, 1, 1), (BB, 2, 1), (BB, 3, 1), (WC, 0, 1), (WC, 1, 1), (WC, 2, 1), (WC, 3, 1), (WC, 4, 1), (WD, 0, 2),
)


def begins_of(plan):
    ready, steps = {}, 0
    for what, k, count in plan:
        for block in {WU: range(UP_BLOCKS), WC: (UP_BLOCKS + k,), WD: range(DOWN_AT, BLOCKS)}.get(what, ()):
            ready[block] = steps
        steps += count
    begins = []
    for g in range(GROUPS):
        there = max(ready[block] for block in range(g * ROWS // BLOCK, ((g + 1) * ROWS - 1) // BLOCK + 1))
        begins.append(max(there, begins[-1] + GAP) if begins else there)
    return begins


def steps_of(plan):
    return begins_of(plan)[-1] + max(L_STRIDE * (L_LEVELS - 1), Z_LATE + Z_STRIDE * (Z_LEVELS - 1)) + 1


def aligned(offset):
    return offset if isinstance(offset, int) else pl.multiple_of(offset, 16)


def part(ref, offset, rows):
    return ref.at[pl.ds(aligned(offset), rows)]


def added(target, offset, sources, rows, tile=16):
    for start in range(0, rows, tile):
        total = None
        for ref, at in sources:
            value = ref[pl.ds(aligned(at + start), tile), :]
            if len(sources) > 2:
                value = value.astype(F32)
            total = value if total is None else total + value
        target[pl.ds(aligned(offset + start), tile), :] = total.astype(BF)


class WeightSums:
    def __init__(self, grad, res, small, buffers, send, recv, local, small_send, small_recv):
        self.grad, self.res, self.small, self.r = grad, res, small, buffers
        self.send, self.recv, self.local = send, recv, local
        self.small_send, self.small_recv = small_send, small_recv
        self.c = lax.axis_index("section")
        self.dp = lax.axis_index("dp")
        self.z = lax.axis_index("seq")
        self.x = lax.rem(self.dp, 2)
        self.y = self.dp // 2
        z = self.z
        self.upper = z // 2
        self.end = jnp.logical_or(z == 0, z == 3)
        self.mid = jnp.logical_not(self.end)
        self.dp_x = self.dp + 1 - 2 * self.x
        self.dp_y = lax.rem(self.dp + 2, 4)
        self.px = (self.c, self.dp_x, z)
        self.py = (self.c, self.dp_y, z)
        self.pair = (self.c, self.dp, 1 - z + 4 * self.upper)
        self.other = (self.c, self.dp, jnp.clip(3 - z, 1, 2))

    def copy(self, kind, g, source, target, to):
        j = KINDS.index(kind)
        return pltpu.make_async_remote_copy(
            src_ref=source, dst_ref=target, send_sem=self.send.at[j], recv_sem=self.recv.at[g, j],
            device_id=to, device_id_type=MESH)

    def square(self, g):
        odd = lax.rem(g, 2)
        u = jnp.where(odd == 0, self.x, self.y)
        v = jnp.where(odd == 0, self.y, self.x)
        to_u = (self.c, jnp.where(odd == 0, self.dp_x, self.dp_y), self.z)
        to_v = (self.c, jnp.where(odd == 0, self.dp_y, self.dp_x), self.z)
        base = g * ROWS
        own_half = base + u * HALF
        own = own_half + v * QUARTER
        beside = own_half + (1 - v) * QUARTER
        return base, u, v, to_u, to_v, own, beside

    def square_copy(self, kind, g):
        base, u, v, to_u, to_v, own, beside = self.square(g)
        grad, res, r = self.grad, self.res, self.r
        final = r["fl"].at[g]
        if kind == "ru":
            return self.copy(kind, g, part(grad, base + (1 - u) * HALF, HALF), r["ru"].at[g], to_u)
        if kind == "rv":
            return self.copy(kind, g, part(grad, beside, QUARTER), r["rv"].at[g], to_v)
        if kind == "za":
            return self.copy(kind, g, part(grad, own, QUARTER), r["za"].at[g], self.pair)
        if kind == "zb":
            return self.copy(kind, g, part(grad, own, QUARTER), r["zb"].at[g], self.other)
        if kind == "zc":
            return self.copy(kind, g, final, final, self.pair)
        if kind == "av":
            return self.copy(kind, g, final, part(res, own, QUARTER), to_v)
        if kind == "au":
            return self.copy(kind, g, final, part(res, own, QUARTER), to_u)
        if kind == "aw":
            return self.copy(kind, g, part(res, beside, QUARTER), part(res, beside, QUARTER), to_u)
        return pltpu.make_async_copy(final, part(res, own, QUARTER), self.local.at[0])

    def square_level(self, g, level):
        base, u, v, to_u, to_v, own, beside = self.square(g)
        grad, r = self.grad, self.r
        copy = functools.partial(self.square_copy, g=g)
        if level == 0:
            copy("ru").start()
        elif level == 1:
            copy("ru").wait_recv()
            added(grad, beside, [(grad, beside), (r["ru"].at[g], (1 - v) * QUARTER)], QUARTER)
            copy("rv").start()
            added(grad, own, [(grad, own), (r["ru"].at[g], v * QUARTER)], QUARTER)
        elif level == 2:
            copy("rv").wait_recv()
            added(grad, own, [(grad, own), (r["rv"].at[g], 0)], QUARTER)

            @pl.when(self.end)
            def _():
                copy("za").start()
        elif level == 3:

            @pl.when(self.mid)
            def _():
                copy("za").wait_recv()
                added(grad, own, [(grad, own), (r["za"].at[g], 0)], QUARTER)
                copy("zb").start()
        elif level == 4:

            @pl.when(self.mid)
            def _():
                copy("zb").wait_recv()
                added(r["fl"].at[g], 0, [(grad, own), (r["zb"].at[g], 0)], QUARTER)
                copy("zc").start()
                copy("av").start()
                copy("au").start()
                copy("fl").start()
        elif level == 5:

            @pl.when(self.end)
            def _():
                copy("zc").wait_recv()
                copy("av").start()
                copy("au").start()
                copy("fl").start()
        elif level == 6:
            copy("av").wait_recv()
            copy("aw").start()
        elif level == 7:
            copy("au").wait_recv()
            copy("aw").wait_recv()

    def line(self, g):
        base = g * ROWS + LROWS
        upper = self.upper
        three = base + CHUNK * (1 - upper)
        far = base + 2 * CHUNK * (1 - upper)
        near = base + 2 * CHUNK * upper
        outer = base + 3 * CHUNK * upper
        own = base + CHUNK * self.z
        return three, far, near, outer, own

    def line_copy(self, kind, g):
        three, far, near, outer, own = self.line(g)
        grad, res, r = self.grad, self.res, self.r
        base = g * ROWS + LROWS
        final = r["fz"].at[g]
        here = part(res, own, CHUNK)
        if kind == "ze":
            return self.copy(kind, g, part(grad, three, 3 * CHUNK), r["ze"].at[g], self.pair)
        if kind == "zm":
            return self.copy(kind, g, part(grad, far, 2 * CHUNK), r["zm"].at[g], self.other)
        if kind == "zo":
            return self.copy(kind, g, part(grad, outer, CHUNK), r["zo"].at[g], self.pair)
        if kind == "ex":
            return self.copy(kind, g, part(grad, own, CHUNK), r["ex"].at[g], self.px)
        if kind == "ey":
            return self.copy(kind, g, r["tx"].at[g], r["ey"].at[g], self.py)
        if kind in ("ge", "gd"):
            return self.copy(kind, g, final, here, self.pair)
        if kind == "gn":
            return self.copy(kind, g, final, here, self.other)
        if kind == "gf":
            rows = part(res, outer, CHUNK)
            return self.copy(kind, g, rows, rows, self.other)
        if kind == "gp":
            rows = part(res, base + CHUNK * (3 - self.z), CHUNK)
            return self.copy(kind, g, rows, rows, self.pair)
        if kind == "gq":
            rows = part(res, base + 3 * CHUNK * (1 - self.upper), CHUNK)
            return self.copy(kind, g, rows, rows, self.pair)
        return pltpu.make_async_copy(final, here, self.local.at[1])

    def line_level(self, g, level):
        three, far, near, outer, own = self.line(g)
        grad, r = self.grad, self.r
        copy = functools.partial(self.line_copy, g=g)
        if level == 0:

            @pl.when(self.end)
            def _():
                copy("ze").start()
        elif level == 1:

            @pl.when(self.mid)
            def _():
                copy("ze").wait_recv()
                added(grad, far, [(grad, far), (r["ze"].at[g], far - three)], 2 * CHUNK)
                copy("zm").start()
        elif level == 2:

            @pl.when(self.mid)
            def _():
                copy("zm").wait_recv()
                added(grad, outer, [(grad, outer), (r["zm"].at[g], outer - near)], CHUNK)
                copy("zo").start()
                added(grad, own, [(grad, own), (r["ze"].at[g], own - three), (r["zm"].at[g], own - near)], CHUNK)
                copy("ex").start()
        elif level == 3:

            @pl.when(self.end)
            def _():
                copy("zo").wait_recv()
                added(grad, own, [(grad, own), (r["zo"].at[g], 0)], CHUNK)
                copy("ex").start()
        elif level == 4:
            copy("ex").wait_recv()
            added(r["tx"].at[g], 0, [(grad, own), (r["ex"].at[g], 0)], CHUNK)
            copy("ey").start()
        elif level == 5:
            copy("ey").wait_recv()
            added(r["fz"].at[g], 0, [(r["tx"].at[g], 0), (r["ey"].at[g], 0)], CHUNK)
            copy("fz").start()

            @pl.when(self.end)
            def _():
                copy("ge").start()

            @pl.when(self.mid)
            def _():
                copy("gn").start()
                copy("gd").start()
        elif level == 6:

            @pl.when(self.mid)
            def _():
                copy("ge").wait_recv()
                copy("gf").start()
                copy("gn").wait_recv()
                copy("gp").start()
        elif level == 7:

            @pl.when(self.mid)
            def _():
                copy("gf").wait_recv()
                copy("gq").start()
        elif level == 8:

            @pl.when(self.end)
            def _():
                copy("gd").wait_recv()
                copy("gp").wait_recv()
                copy("gq").wait_recv()

    def small_copy(self, kind):
        j = SMALL_KINDS.index(kind)
        s = self.small
        source, target, to = dict(
            sx=(s.at[0], s.at[5], self.px),
            sy=(s.at[1], s.at[6], self.py),
            sa=(s.at[2], s.at[7], self.pair),
            sb=(s.at[3], s.at[8], self.other),
            sc=(s.at[4], s.at[4], self.pair),
        )[kind]
        return pltpu.make_async_remote_copy(
            src_ref=source, dst_ref=target, send_sem=self.small_send.at[j], recv_sem=self.small_recv.at[j],
            device_id=to, device_id_type=MESH)

    def small_level(self, level):
        copy, s = self.small_copy, self.small
        if level == 0:
            copy("sx").start()
        elif level == 1:
            copy("sx").wait_recv()
            s[1] = s[0] + s[5]
            copy("sy").start()
        elif level == 2:
            copy("sy").wait_recv()
            s[2] = s[1] + s[6]

            @pl.when(self.end)
            def _():
                copy("sa").start()
        elif level == 3:

            @pl.when(self.mid)
            def _():
                copy("sa").wait_recv()
                s[3] = s[2] + s[7]
                copy("sb").start()
        elif level == 4:

            @pl.when(self.mid)
            def _():
                copy("sb").wait_recv()
                s[4] = s[3] + s[8]
                copy("sc").start()
        elif level == 5:

            @pl.when(self.end)
            def _():
                copy("sc").wait_recv()

    def tick(self, t, begins, small_begin):
        for level in reversed(range(Z_LEVELS)):
            for kind, stride, late, act in (
                (0, L_STRIDE, 0, self.square_level),
                (1, Z_STRIDE, Z_LATE, self.line_level),
            ):
                if kind == 0 and level >= L_LEVELS:
                    continue
                step = t - late - stride * level
                g = jnp.int32(-1)
                for j, begin in enumerate(begins):
                    g = jnp.where(step == begin, j, g)

                @pl.when(g >= 0)
                def _():
                    act(g, level)

        for level in range(6):

            @pl.when(t == small_begin + level)
            def _():
                self.small_level(level)

    def all_sent(self, kind, rows):
        everything = self.grad.at[pl.ds(0, GROUPS * rows)]
        pltpu.make_async_remote_copy(
            src_ref=everything, dst_ref=everything, send_sem=self.send.at[KINDS.index(kind)],
            recv_sem=self.recv.at[0, 0], device_id=self.px, device_id_type=MESH).wait_send()

    def drain(self):
        for j, rows in ((0, QUARTER), (1, CHUNK)):
            everything = self.grad.at[pl.ds(0, GROUPS * rows)]
            pltpu.make_async_copy(everything, self.res.at[pl.ds(0, GROUPS * rows)], self.local.at[j]).wait()
        self.all_sent("ru", HALF)
        for kind in ("rv", "av", "au", "aw"):
            self.all_sent(kind, QUARTER)
        for kind in ("ex", "ey"):
            self.all_sent(kind, CHUNK)

        @pl.when(self.end)
        def _():
            self.all_sent("za", QUARTER)
            self.all_sent("ze", 3 * CHUNK)
            self.all_sent("ge", CHUNK)

        @pl.when(self.mid)
        def _():
            self.all_sent("zb", QUARTER)
            self.all_sent("zc", QUARTER)
            self.all_sent("zm", 2 * CHUNK)
            for kind in ("zo", "gn", "gd", "gf", "gp", "gq"):
                self.all_sent(kind, CHUNK)

        self.small_copy("sx").wait_send()
        self.small_copy("sy").wait_send()

        @pl.when(self.end)
        def _():
            self.small_copy("sa").wait_send()

        @pl.when(self.mid)
        def _():
            self.small_copy("sb").wait_send()
            self.small_copy("sc").wait_send()


def normed(value):
    mean = jnp.mean(value, axis=-1, keepdims=True)
    centred = value - mean
    spread = jnp.mean(centred * centred, axis=-1, keepdims=True)
    scale = lax.rsqrt(spread + EPS)
    return centred * scale, mean, scale, spread


def gelu(w):
    t = jnp.tanh(w * (2.0 * GELU_A + (8.0 * GELU_B) * (w * w)))
    return w + w * t


def gelu_slope(w):
    square = w * w
    t = jnp.tanh(w * (2.0 * GELU_A + (8.0 * GELU_B) * square))
    q = w * (GELU_A + (12.0 * GELU_B) * square)
    return (0.5 + q) + t * (0.5 - q * t)


def norm_gelu_back(grad, n, scale, gain, half_gain, half_shift):
    dv = grad * gelu_slope(n * half_gain + half_shift)
    terms = dv * n
    dn = dv * gain
    first = jnp.mean(dn, axis=-1, keepdims=True)
    second = jnp.mean(terms * gain, axis=-1, keepdims=True)
    return dv, terms, scale * (dn - first - n * second)


def fold(value):
    rows, width = value.shape
    return jnp.sum(value.reshape(rows // 8, 8, width), axis=0)


def nn(a, b):
    return jnp.dot(a, b, preferred_element_type=F32)


def nt(a, b):
    return lax.dot_general(a, b, (((1,), (1,)), ((), ())), preferred_element_type=F32)


def tn(a, b):
    return lax.dot_general(a, b, (((0,), (0,)), ((), ())), preferred_element_type=F32)


def blocks_kernel(
    names, with_sums, last,
    ends, lengths, outer_gain, inner_gains, outer_biases, inner_biases, down_hbm, conv_hbm, up_hbm,
    ends_out, res, small_out,
    down, conv, up, X, GY, HA, CW, HC, GCW, GP, NB, NC, ST, XS, wide, handing, taps, lhs, oacc, iacc, grad, small,
    *rest,
):
    buffers = dict(zip(names, rest[: len(names)]))
    send, recv, local, small_send, small_recv, load, hand_send, hand_recv, halo_send, halo_recv, store = rest[len(names) :]
    micro, rows, width = X.shape
    inner = down.shape[1]
    section = lax.axis_index("section")
    dp = lax.axis_index("dp")
    z = lax.axis_index("seq")
    first = section == 0
    second = section == 1
    has_left = z > 0
    has_right = z < last
    across = (1 - section, dp, z)
    left = (section, dp, jnp.maximum(z - 1, 0))
    right = (section, dp, jnp.minimum(z + 1, last))
    sums = WeightSums(grad, res, small, buffers, send, recv, local, small_send, small_recv)

    def when(condition, act):
        pl.when(condition)(lambda: act() and None)

    def weight_load(j):
        return pltpu.make_async_copy((down_hbm, conv_hbm, up_hbm)[j], (down, conv, up)[j], load.at[micro + j])

    def end_load(mb, target):
        return pltpu.make_async_copy(ends.at[mb], target.at[mb], load.at[mb])

    @pl.when(first)
    def _():
        end_load(0, X).start()
        weight_load(0).start()

    barrier = pltpu.get_barrier_semaphore()

    def greet(to):
        pl.semaphore_signal(barrier, inc=1, device_id=to, device_id_type=MESH)

    greet(across)
    when(has_left, lambda: greet(left))
    when(has_right, lambda: greet(right))
    if with_sums:
        greet(sums.px)
        greet(sums.py)

    def met():
        peers = (3 if with_sums else 1) + has_left.astype(jnp.int32) + has_right.astype(jnp.int32)
        pl.semaphore_wait(barrier, peers)

    XS[...] = jnp.zeros_like(XS)
    oacc[...] = jnp.zeros_like(oacc)
    iacc[...] = jnp.zeros_like(iacc)
    edge = jnp.zeros((rows, inner), BF)
    for mb in range(micro):

        @pl.when(jnp.logical_not(has_left))
        def _():
            CW[mb, 0:rows, :] = edge
            GCW[mb, 0:rows, :] = edge

        @pl.when(jnp.logical_not(has_right))
        def _():
            CW[mb, 2 * rows : 3 * rows, :] = edge
            GCW[mb, 2 * rows : 3 * rows, :] = edge

    @pl.when(first)
    def _():
        end_load(0, X).wait()
        weight_load(0).wait()
        weight_load(1).start()
        weight_load(2).start()
        for mb in range(1, micro):
            end_load(mb, X).start()

    @pl.when(second)
    def _():
        for j in range(3):
            weight_load(j).start()
        for mb in range(micro):
            end_load(mb, GY).start()

    def halo_copies(ref, which, mb):
        def make(side, count):
            if side == 0:
                source, target, to = ref.at[mb, pl.ds(2 * rows - count, count)], ref.at[mb, pl.ds(rows - count, count)], right
            else:
                source, target, to = ref.at[mb, pl.ds(rows, count)], ref.at[mb, pl.ds(2 * rows, count)], left
            return pltpu.make_async_remote_copy(
                src_ref=source, dst_ref=target, send_sem=halo_send.at[which, mb, side],
                recv_sem=halo_recv.at[which, mb, side], device_id=to, device_id_type=MESH)

        return make

    def halo(ref, which, mb, act_right, act_left):
        make = halo_copies(ref, which, mb)
        for mine, count in ((first, EDGE), (second, rows)):

            @pl.when(mine)
            def _():
                when(act_right[0], lambda: act_right[1](make(0, count)))
                when(act_left[0], lambda: act_left[1](make(1, count)))

    def halo_start(ref, which, mb):
        go = lambda c: c.start()
        halo(ref, which, mb, (has_right, go), (has_left, go))

    def halo_arrived(ref, which, mb):
        go = lambda c: c.wait_recv()
        halo(ref, which, mb, (has_left, go), (has_right, go))

    def halo_sent(ref, which, mb):
        go = lambda c: c.wait_send()
        halo(ref, which, mb, (has_right, go), (has_left, go))

    def shifted(ref, mb, k, sign, target, at, column):
        shift = sign * (k - REACH)

        @pl.when(first)
        def _():
            target[at : at + rows, column : column + inner] = ref[mb, pl.ds(rows + shift * FIRST_DILATION, rows), :]

        @pl.when(second)
        def _():
            target[at : at + rows, column : column + inner] = ref[mb, pl.ds(rows + shift * SECOND_DILATION, rows), :]

    def all_shifted(ref, mb, sign):
        for mine, dilation in ((first, FIRST_DILATION), (second, SECOND_DILATION)):

            @pl.when(mine)
            def _():
                for k in range(FILTER_TAPS):
                    at = rows + sign * (k - REACH) * dilation
                    taps[:, k * inner : (k + 1) * inner] = ref[mb, pl.ds(at, rows), :]

    def hand_over(mb, target):
        slot = lax.rem(mb, 2)
        return pltpu.make_async_remote_copy(
            src_ref=handing.at[slot], dst_ref=target.at[mb], send_sem=hand_send.at[mb], recv_sem=hand_recv.at[mb],
            device_id=across, device_id_type=MESH)

    def store_end(mb):
        return pltpu.make_async_copy(wide.at[lax.rem(mb, 2)], ends_out.at[mb], store.at[mb])

    own = pl.ds(rows, rows)
    outer_shift, inner_shift_b, inner_shift_c = 0.5 * outer_biases[0:1, :], 0.5 * inner_biases[0:1, :], 0.5 * inner_biases[1:2, :]
    outer_half, inner_half_b, inner_half_c = 0.5 * outer_gain[...], 0.5 * inner_gains[0:1, :], 0.5 * inner_gains[1:2, :]

    def valid_of(mb):
        position = z * rows + lax.broadcasted_iota(jnp.int32, (rows, 1), 0)
        return (position < lengths[mb]).astype(F32)

    def forward_a(mb):
        when(jnp.logical_and(first, mb > 0), lambda: end_load(mb, X).wait())
        when(second, lambda: hand_over(mb, X).wait_recv())
        when(jnp.logical_and(second, mb == 0), lambda: weight_load(0).wait())
        n, mean, scale, spread = normed(X[mb].astype(F32))
        XS[...] += (spread + mean * mean) * valid_of(mb)
        ST[mb, :, 0:1] = mean
        ST[mb, :, 1:2] = scale
        hidden = gelu(n * outer_half + outer_shift).astype(BF)
        HA[mb] = hidden
        n, _, scale, _ = normed(nn(hidden, down[...]) + inner_biases[2:3, :])
        NB[mb] = n
        ST[mb, :, 2:3] = scale
        CW[mb, own, :] = (gelu(n * inner_half_b + inner_shift_b) * valid_of(mb)).astype(BF)
        when(jnp.logical_and(first, mb == 0), met)
        halo_start(CW, 0, mb)

    def forward_b(mb):
        slot = lax.rem(mb, 2)
        halo_arrived(CW, 0, mb)

        @pl.when(mb == 0)
        def _():
            weight_load(1).wait()
            weight_load(2).wait()

        @pl.when(mb >= 2)
        def _():
            when(first, lambda: hand_over(mb - 2, X).wait_send())
            when(second, lambda: store_end(mb - 2).wait())

        all_shifted(CW, mb, 1)
        n, _, scale, _ = normed(nn(taps[...], conv[...]) + inner_biases[3:4, :])
        NC[mb] = n
        ST[mb, :, 3:4] = scale
        valid = valid_of(mb)
        hidden = (gelu(n * inner_half_c + inner_shift_c) * valid).astype(BF)
        HC[mb] = hidden
        branch = (nn(hidden, up[...]) + outer_biases[1:2, :]) * valid
        oacc[3] += fold(branch * branch)
        value = X[mb].astype(F32) + branch
        wide[slot] = value
        handing[slot] = value.astype(BF)
        when(first, lambda: hand_over(mb, X).start())
        when(second, lambda: store_end(mb).start())

    def backward_a(mb):
        when(jnp.logical_and(first, mb < micro - 1), lambda: hand_over(mb, GY).wait_recv())

        @pl.when(jnp.logical_and(second, mb == 0))
        def _():
            for k in range(micro):
                end_load(k, GY).wait()

        valid = valid_of(mb)
        oacc[2] += fold(GY[mb].astype(F32) * valid)
        dv, terms, dz = norm_gelu_back(
            nt(GY[mb], up[...]) * valid, NC[mb], ST[mb, :, 3:4], inner_gains[1:2, :], inner_half_c, inner_shift_c
        )
        iacc[3] += fold(terms)
        iacc[4] += fold(dv)
        iacc[5] += fold(dz)
        GCW[mb, own, :] = dz.astype(BF)
        halo_start(GCW, 1, mb)

    def backward_b(mb):
        slot = lax.rem(mb, 2)
        halo_arrived(GCW, 1, mb)

        @pl.when(mb < 2)
        def _():
            when(first, lambda: hand_over(mb + micro - 2, X).wait_send())
            when(second, lambda: store_end(mb + micro - 2).wait())

        @pl.when(mb >= 2)
        def _():
            when(second, lambda: hand_over(mb - 2, GY).wait_send())
            when(first, lambda: store_end(mb - 2).wait())

        all_shifted(GCW, mb, -1)
        total = nt(taps[:, 0:inner], conv[0:inner, :])
        for k in range(1, FILTER_TAPS):
            total = total + nt(taps[:, k * inner : (k + 1) * inner], conv[k * inner : (k + 1) * inner, :])
        dv, terms, dz = norm_gelu_back(
            total * valid_of(mb), NB[mb], ST[mb, :, 2:3], inner_gains[0:1, :], inner_half_b, inner_shift_b
        )
        iacc[0] += fold(terms)
        iacc[1] += fold(dv)
        iacc[2] += fold(dz)
        low = dz.astype(BF)
        GP[mb] = low
        scale = ST[mb, :, 1:2]
        n = (X[mb].astype(F32) - ST[mb, :, 0:1]) * scale
        dv, terms, dz = norm_gelu_back(nt(low, down[...]), n, scale, outer_gain[...], outer_half, outer_shift)
        oacc[0] += fold(terms)
        oacc[1] += fold(dv)
        value = GY[mb].astype(F32) + dz
        wide[slot] = value
        handing[slot] = value.astype(BF)
        when(second, lambda: hand_over(mb, GY).start())
        when(first, lambda: store_end(mb).start())

    def weight_up():
        when(first, lambda: hand_over(micro - 1, GY).wait_recv())
        c = HC[...].reshape(micro * rows, inner)
        for h in range(UP_BLOCKS):
            y = GY[:, :, h * inner : (h + 1) * inner].reshape(micro * rows, inner)
            grad[h * BLOCK : (h + 1) * BLOCK, :] = tn(c, y).astype(BF)

    def weight_tap(tap):
        for k in range(FILTER_TAPS):

            @pl.when(tap == k)
            def _():
                for mb in range(micro):
                    shifted(CW, mb, k, 1, lhs, mb * rows, 0)

        y = GCW[:, own, :].reshape(micro * rows, inner)
        at = pl.multiple_of((UP_BLOCKS + tap) * BLOCK, BLOCK)
        grad[pl.ds(at, BLOCK), :] = tn(lhs[...], y).astype(BF)

    def weight_down():
        y = GP[...].reshape(micro * rows, inner)
        for h in range(BLOCKS - DOWN_AT):
            at = (DOWN_AT + h) * BLOCK
            a = HA[:, :, h * inner : (h + 1) * inner].reshape(micro * rows, inner)
            grad[at : at + BLOCK, :] = tn(a, y).astype(BF)

    def row(value):
        return jnp.sum(value, axis=0, keepdims=True)

    def smalls():
        place = 0

        def put(value):
            nonlocal place
            for at in range(0, value.shape[1], inner):
                small[0, place : place + 1, :] = value[:, at : at + inner]
                place += 1

        small[0] = jnp.zeros_like(small[0])
        for ref, j in ((oacc, 0), (iacc, 0), (iacc, 3), (oacc, 1), (oacc, 2), (iacc, 1), (iacc, 4), (iacc, 2), (iacc, 5)):
            put(row(ref[j]))
        lane = lax.broadcasted_iota(jnp.int32, (1, inner), 1)
        put(jnp.where(lane == 0, row(XS[...]) * width, 0.0))
        value = row(oacc[3])
        put(value[:, :inner] + value[:, inner:])
        count = jnp.float32(0)
        for mb in range(micro):
            count += jnp.clip(lengths[mb] - z * rows, 0, rows).astype(F32)
        put(jnp.zeros((1, inner), F32) + count)

    when(second, met)
    plans = [[(p * 8 + k) * 8 + steps for p, k, steps in plan] for plan in (FIRST_PLAN, SECOND_PLAN)]
    begins = [jnp.where(first, a, b) for a, b in zip(begins_of(FIRST_PLAN), begins_of(SECOND_PLAN))]
    ticks = jnp.where(first, steps_of(FIRST_PLAN), steps_of(SECOND_PLAN))

    def tick(t, carry):
        sums.tick(t, begins, begins[-1])
        return carry

    def step(i, t):
        entry = jnp.int32(0)
        for j, (a, b) in enumerate(zip(*plans)):
            entry = jnp.where(i == j, jnp.where(first, a, b), entry)
        what, k = entry // 64, lax.rem(entry // 8, 8)
        for p, act in ((FA, forward_a), (FB, forward_b), (BA, backward_a), (BB, backward_b), (WC, weight_tap)):
            when(what == p, functools.partial(act, k))
        when(what == WU, weight_up)

        @pl.when(what == WD)
        def _():
            smalls()
            weight_down()

        then = t + lax.rem(entry, 8)
        if with_sums:
            lax.fori_loop(t, then, tick, 0)
        return then

    t = lax.fori_loop(0, len(FIRST_PLAN), step, jnp.int32(0))

    if with_sums:
        lax.fori_loop(t, ticks, tick, 0)
        sums.drain()
        done = pltpu.make_async_copy(small.at[4], small_out, load.at[0])
        done.start()
        done.wait()
    else:
        done = pltpu.make_async_copy(small.at[0], small_out, load.at[0])
        done.start()
        done.wait()
        done = pltpu.make_async_copy(grad, res, load.at[1])
        done.start()
        done.wait()
    for mb in range(micro):
        if mb >= micro - 2:
            when(first, functools.partial(lambda m: store_end(m).wait(), mb))
            when(second, functools.partial(lambda m: hand_over(m, GY).wait_send(), mb))
        halo_sent(CW, 0, mb)
        halo_sent(GCW, 1, mb)


def run_blocks(mesh_shape, ends, lengths, outer_gain, inner_gains, outer_biases, inner_biases, down, conv, up):
    micro, rows, width = ends.shape
    inner = down.shape[1]
    taps = FILTER_TAPS
    with_sums = (mesh_shape["dp"], mesh_shape["seq"]) == (4, 4)
    buffers = {k: pltpu.VMEM((GROUPS, n, BLOCK), BF) for k, n in RECEIVE.items()} if with_sums else {}
    names = tuple(buffers)
    total = BLOCKS * BLOCK
    anywhere = pl.BlockSpec(memory_space=pl.ANY)
    vmem = pl.BlockSpec(memory_space=pltpu.VMEM)
    dma = pltpu.SemaphoreType.DMA
    scratch = [
        pltpu.VMEM(down.shape, BF),
        pltpu.VMEM(conv.shape, BF),
        pltpu.VMEM(up.shape, BF),
        pltpu.VMEM((micro, rows, width), BF),
        pltpu.VMEM((micro, rows, width), BF),
        pltpu.VMEM((micro, rows, width), BF),
        pltpu.VMEM((micro, 3 * rows, inner), BF),
        pltpu.VMEM((micro, rows, inner), BF),
        pltpu.VMEM((micro, 3 * rows, inner), BF),
        pltpu.VMEM((micro, rows, inner), BF),
        pltpu.VMEM((micro, rows, inner), F32),
        pltpu.VMEM((micro, rows, inner), F32),
        pltpu.VMEM((micro, rows, 128), F32),
        pltpu.VMEM((rows, 1), F32),
        pltpu.VMEM((2, rows, width), F32),
        pltpu.VMEM((2, rows, width), BF),
        pltpu.VMEM((rows, taps * inner), BF),
        pltpu.VMEM((micro * rows, inner), BF),
        pltpu.VMEM((4, 8, width), F32),
        pltpu.VMEM((6, 8, inner), F32),
        pltpu.VMEM((total, BLOCK), BF),
        pltpu.VMEM((9, 16, inner), F32),
        *[buffers[k] for k in names],
        dma((len(KINDS),)),
        dma((GROUPS, len(KINDS))),
        dma((2,)),
        dma((len(SMALL_KINDS),)),
        dma((len(SMALL_KINDS),)),
        dma((micro + 3,)),
        dma((micro,)),
        dma((micro,)),
        dma((2, micro, 2)),
        dma((2, micro, 2)),
        dma((micro,)),
    ]
    flops = 2 * 3 * micro * rows * (2 * width * inner + taps * inner * inner)
    return pl.pallas_call(
        functools.partial(blocks_kernel, names, with_sums, mesh_shape["seq"] - 1),
        name="two_blocks",
        out_shape=(
            jax.ShapeDtypeStruct((micro, rows, width), F32),
            jax.ShapeDtypeStruct((total, BLOCK), BF),
            jax.ShapeDtypeStruct((16, inner), F32),
        ),
        in_specs=[anywhere, pl.BlockSpec(memory_space=pltpu.SMEM), vmem, vmem, vmem, vmem, anywhere, anywhere, anywhere],
        out_specs=[anywhere] * 3,
        scratch_shapes=scratch,
        cost_estimate=pl.CostEstimate(flops=flops, bytes_accessed=40 * 2**20, transcendentals=0),
        compiler_params=pltpu.CompilerParams(collective_id=1, has_side_effects=True, vmem_limit_bytes=62 * 2**20),
    )(ends, lengths, outer_gain, inner_gains, outer_biases, inner_biases, down, conv, up)


def finish_kernel(
    ends, rows, small, ends_out, outer_gain, inner_gains, outer_biases, inner_biases, down, conv, up, rms, raw, full, held,
    ends_load, ends_store, load, store,
):
    micro, width = ends.shape[0], ends.shape[2]
    into = [pltpu.make_async_copy(ends.at[mb], held.at[mb], ends_load.at[mb]) for mb in range(micro)]
    out = [pltpu.make_async_copy(held.at[mb], ends_out.at[0, mb, 0], ends_store.at[mb]) for mb in range(micro)]
    loads = [
        pltpu.make_async_copy(rows.at[pl.ds(g * BLOCK, BLOCK)], raw.at[g], load.at[g]) for g in range(BLOCKS)
    ]
    for copy in into + loads:
        copy.start()
    outer_gain[0:1, 0:BLOCK] = small[0:1, :]
    outer_gain[0:1, BLOCK:] = small[1:2, :]
    inner_gains[0] = small[2:4, :]
    for j in range(2):
        outer_biases[0, j : j + 1, 0:BLOCK] = small[4 + 2 * j : 5 + 2 * j, :]
        outer_biases[0, j : j + 1, BLOCK:] = small[5 + 2 * j : 6 + 2 * j, :]
    inner_biases[0] = small[8:12, :]
    squares = jnp.sum(small[12:14, :], axis=1, keepdims=True)
    roots = jnp.sqrt(squares / (small[14:15, 0:1] * width))
    rms[0:1, 0:1] = roots[0:1, :]
    rms[0:1, 1:2] = roots[1:2, :]
    places = [up.at[0, :, pl.ds(h * BLOCK, BLOCK)] for h in range(UP_BLOCKS)]
    places += [conv.at[0, k] for k in range(FILTER_TAPS)]
    places += [down.at[0, pl.ds(h * BLOCK, BLOCK)] for h in range(BLOCKS - DOWN_AT)]
    stores = []
    for mb in range(micro):
        into[mb].wait()
        out[mb].start()
    for g in range(BLOCKS):
        loads[g].wait()
        full[g] = raw[g].astype(F32)
        stores.append(pltpu.make_async_copy(full.at[g], places[g], store.at[g]))
        stores[-1].start()
    for copy in out + stores:
        copy.wait()


def finish(shapes, ends, rows, small):
    anywhere = pl.BlockSpec(memory_space=pl.ANY)
    vmem = pl.BlockSpec(memory_space=pltpu.VMEM)
    dma = pltpu.SemaphoreType.DMA
    return pl.pallas_call(
        finish_kernel,
        name="outputs",
        out_shape=tuple(jax.ShapeDtypeStruct(shape, F32) for shape in shapes),
        in_specs=[anywhere, anywhere, vmem],
        out_specs=[anywhere, vmem, vmem, vmem, vmem, anywhere, anywhere, anywhere, vmem],
        scratch_shapes=[
            pltpu.VMEM((BLOCKS, BLOCK, BLOCK), BF),
            pltpu.VMEM((BLOCKS, BLOCK, BLOCK), F32),
            pltpu.VMEM(ends.shape, F32),
            dma((ends.shape[0],)),
            dma((ends.shape[0],)),
            dma((BLOCKS,)),
            dma((BLOCKS,)),
        ],
        compiler_params=pltpu.CompilerParams(vmem_limit_bytes=60 * 2**20),
    )(ends, rows, small)


def body(
    mesh_shape, ends_in, lengths, outer_gain, inner_gains, outer_biases, inner_biases, down_in, conv_weight, up_out
):
    width = ends_in.shape[-1]
    ends, rows, small = run_blocks(
        mesh_shape, ends_in.reshape(ends_in.shape[1], -1, width), lengths.reshape(-1), outer_gain, inner_gains[0],
        outer_biases[0], inner_biases[0], down_in[0], conv_weight[0].reshape(-1, conv_weight.shape[-1]), up_out[0],
    )
    if (mesh_shape["dp"], mesh_shape["seq"]) == (4, 4):
        weights = (outer_gain, inner_gains, outer_biases, inner_biases, down_in, conv_weight, up_out)
        return finish((ends_in.shape, *(w.shape for w in weights), (1, 2)), ends, rows, small)
    rows, small = lax.psum((rows.astype(F32), small), ("dp", "seq"))
    up = jnp.concatenate([rows[:BLOCK], rows[BLOCK : 2 * BLOCK]], axis=1)
    conv = rows[UP_BLOCKS * BLOCK : DOWN_AT * BLOCK].reshape(conv_weight.shape[1:])
    down = rows[DOWN_AT * BLOCK :]
    rms = jnp.sqrt(jnp.sum(small[12:14], axis=1) / (small[14, 0] * width))
    return (
        ends.reshape(ends_in.shape),
        small[0:2].reshape(1, -1),
        small[None, 2:4],
        small[4:8].reshape(1, 2, -1),
        small[None, 8:12],
        down[None],
        conv[None],
        up[None],
        rms[None],
    )


def solution(mesh):
    in_specs = (
        P("section", None, "dp", "seq", None),
        P(None, "dp"),
        P("section", None),
        P("section", None, None),
        P("section", None, None),
        P("section", None, None),
        P("section", None, None),
        P("section", None, None, None),
        P("section", None, None),
    )
    out_specs = (
        P("section", None, "dp", "seq", None),
        P("section", None),
        P("section", None, None),
        P("section", None, None),
        P("section", None, None),
        P("section", None, None),
        P("section", None, None, None),
        P("section", None, None),
        P("section", None),
    )
    return jax.shard_map(
        functools.partial(body, dict(mesh.shape)), mesh=mesh, in_specs=in_specs, out_specs=out_specs, check_vma=False
    )
```

```python
import functools
import math

import jax
import jax.numpy as jnp
from jax import lax
from jax.experimental import pallas as pl
from jax.experimental.pallas import tpu as pltpu
from jax.sharding import PartitionSpec as P

MESH = pl.DeviceIdType.MESH
BF = jnp.bfloat16
F32 = jnp.float32
FILTER_TAPS = 5
FIRST_DILATION = 2
SECOND_DILATION = 128
REACH = FILTER_TAPS // 2
EPS = 1e-05
GELU_A = math.sqrt(2.0 / math.pi)
GELU_B = GELU_A * 0.044715
EDGE = 16

BLOCK = 640
UP_BLOCKS = 2
DOWN_AT = UP_BLOCKS + FILTER_TAPS
BLOCKS = DOWN_AT + 2
GROUPS = 10
ROWS = BLOCKS * BLOCK // GROUPS
LROWS = 384
HALF = LROWS // 2
QUARTER = LROWS // 4
CHUNK = (ROWS - LROWS) // 4
KINDS = (
    "ru", "rv", "za", "zb", "zc", "av", "au", "aw",
    "ze", "zm", "zo", "ex", "ey", "ge", "gn", "gd", "gf", "gp", "gq",
)
ARRIVES = dict(ru=0, rv=1, av=2, au=3, aw=4, ex=5, ey=6, za=7, zb=8, ze=9, zm=10, ge=11, gn=12, gf=13,
               zc=7, zo=8, gd=9, gp=10, gq=11)
SMALL_KINDS = ("sx", "sy", "sa", "sb", "sc")
RECEIVE = dict(ru=HALF, rv=QUARTER, za=QUARTER, zb=QUARTER, fl=QUARTER, ze=3 * CHUNK, zm=2 * CHUNK,
               zo=CHUNK, ex=CHUNK, ey=CHUNK, tx=CHUNK, fz=CHUNK)
L_LEVELS = 8
Z_LEVELS = 9
L_STRIDE, Z_STRIDE, Z_LATE, GAP = 2, 2, 0, 1
FA, FB, WU, BA, BB, BC, WC, WD = range(1, 9)
FIRST_PLAN = (
    (FA, 0, 0), (FA, 1, 0), (FB, 0, 0), (FA, 2, 0), (FB, 1, 0), (FA, 3, 0), (FB, 2, 0), (FB, 3, 0), (BA, 0, 0), (BA, 1, 0), (BB, 0, 0), (BC, 0, 0), (BA, 2, 0), (BB, 1, 0), (BC, 1, 0), (WU, 0, 0), (BA, 3, 1), (BB, 2, 0), (BC, 2, 1), (BB, 3, 0), (BC, 3, 1), (WC, 0, 0), (WC, 1, 0), (WC, 2, 3), (WC, 3, 3), (WC, 4, 1), (WD, 0, 0),
)
SECOND_PLAN = (
    (FA, 0, 0), (FA, 1, 0), (FB, 0, 0), (FA, 2, 0), (FB, 1, 0), (FA, 3, 0), (FB, 2, 0), (BA, 0, 0), (FB, 3, 0), (WU, 0, 1), (BA, 1, 0), (BB, 0, 0), (BC, 0, 1), (BA, 2, 1), (BB, 1, 0), (BC, 1, 1), (BA, 3, 1), (BB, 2, 0), (BC, 2, 1), (WC, 0, 1), (WC, 1, 1), (BB, 3, 0), (BC, 3, 1), (WC, 2, 1), (WC, 3, 1), (WC, 4, 1), (WD, 0, 1),
)


def begins_of(plan):
    ready, steps = {}, 0
    for what, k, count in plan:
        for block in {WU: range(UP_BLOCKS), WC: (UP_BLOCKS + k,), WD: range(DOWN_AT, BLOCKS)}.get(what, ()):
            ready[block] = steps
        steps += count
    begins = []
    for g in range(GROUPS):
        there = max(ready[block] for block in range(g * ROWS // BLOCK, ((g + 1) * ROWS - 1) // BLOCK + 1))
        begins.append(max(there, begins[-1] + GAP) if begins else there)
    return begins


def steps_of(plan):
    return begins_of(plan)[-1] + max(L_STRIDE * (L_LEVELS - 1), Z_LATE + Z_STRIDE * (Z_LEVELS - 1)) + 1


def aligned(offset):
    return offset if isinstance(offset, int) else pl.multiple_of(offset, 16)


def part(ref, offset, rows):
    return ref.at[pl.ds(aligned(offset), rows)]


def added(target, offset, sources, rows, tile=16):
    for start in range(0, rows, tile):
        total = None
        for ref, at in sources:
            value = ref[pl.ds(aligned(at + start), tile), :]
            if len(sources) > 2:
                value = value.astype(F32)
            total = value if total is None else total + value
        target[pl.ds(aligned(offset + start), tile), :] = total.astype(BF)


class WeightSums:
    def __init__(self, grad, res, small, buffers, send, recv, local, small_send, small_recv):
        self.grad, self.res, self.small, self.r = grad, res, small, buffers
        self.send, self.recv, self.local = send, recv, local
        self.small_send, self.small_recv = small_send, small_recv
        self.c = lax.axis_index("section")
        self.dp = lax.axis_index("dp")
        self.z = lax.axis_index("seq")
        self.x = lax.rem(self.dp, 2)
        self.y = self.dp // 2
        z = self.z
        self.upper = z // 2
        self.end = jnp.logical_or(z == 0, z == 3)
        self.mid = jnp.logical_not(self.end)
        self.dp_x = self.dp + 1 - 2 * self.x
        self.dp_y = lax.rem(self.dp + 2, 4)
        self.px = (self.c, self.dp_x, z)
        self.py = (self.c, self.dp_y, z)
        self.pair = (self.c, self.dp, 1 - z + 4 * self.upper)
        self.other = (self.c, self.dp, jnp.clip(3 - z, 1, 2))

    def copy(self, kind, g, source, target, to):
        j = KINDS.index(kind)
        return pltpu.make_async_remote_copy(
            src_ref=source, dst_ref=target, send_sem=self.send.at[j], recv_sem=self.recv.at[g, ARRIVES[kind]],
            device_id=to, device_id_type=MESH)

    def square(self, g):
        odd = lax.rem(g, 2)
        u = jnp.where(odd == 0, self.x, self.y)
        v = jnp.where(odd == 0, self.y, self.x)
        to_u = (self.c, jnp.where(odd == 0, self.dp_x, self.dp_y), self.z)
        to_v = (self.c, jnp.where(odd == 0, self.dp_y, self.dp_x), self.z)
        base = g * ROWS
        own_half = base + u * HALF
        own = own_half + v * QUARTER
        beside = own_half + (1 - v) * QUARTER
        return base, u, v, to_u, to_v, own, beside

    def square_copy(self, kind, g):
        base, u, v, to_u, to_v, own, beside = self.square(g)
        grad, res, r = self.grad, self.res, self.r
        final = r["fl"].at[g]
        if kind == "ru":
            return self.copy(kind, g, part(grad, base + (1 - u) * HALF, HALF), r["ru"].at[g], to_u)
        if kind == "rv":
            return self.copy(kind, g, part(grad, beside, QUARTER), r["rv"].at[g], to_v)
        if kind == "za":
            return self.copy(kind, g, part(grad, own, QUARTER), r["za"].at[g], self.pair)
        if kind == "zb":
            return self.copy(kind, g, part(grad, own, QUARTER), r["zb"].at[g], self.other)
        if kind == "zc":
            return self.copy(kind, g, final, final, self.pair)
        if kind == "av":
            return self.copy(kind, g, final, part(res, own, QUARTER), to_v)
        if kind == "au":
            return self.copy(kind, g, final, part(res, own, QUARTER), to_u)
        if kind == "aw":
            return self.copy(kind, g, part(res, beside, QUARTER), part(res, beside, QUARTER), to_u)
        return pltpu.make_async_copy(final, part(res, own, QUARTER), self.local.at[0])

    def square_level(self, g, level):
        base, u, v, to_u, to_v, own, beside = self.square(g)
        grad, r = self.grad, self.r
        copy = functools.partial(self.square_copy, g=g)
        if level == 0:
            copy("ru").start()
        elif level == 1:
            copy("ru").wait_recv()
            added(grad, beside, [(grad, beside), (r["ru"].at[g], (1 - v) * QUARTER)], QUARTER)
            copy("rv").start()
            added(grad, own, [(grad, own), (r["ru"].at[g], v * QUARTER)], QUARTER)
        elif level == 2:
            copy("rv").wait_recv()
            added(grad, own, [(grad, own), (r["rv"].at[g], 0)], QUARTER)

            @pl.when(self.end)
            def _():
                copy("za").start()
        elif level == 3:

            @pl.when(self.mid)
            def _():
                copy("za").wait_recv()
                added(grad, own, [(grad, own), (r["za"].at[g], 0)], QUARTER)
                copy("zb").start()
        elif level == 4:

            @pl.when(self.mid)
            def _():
                copy("zb").wait_recv()
                added(r["fl"].at[g], 0, [(grad, own), (r["zb"].at[g], 0)], QUARTER)
                copy("zc").start()
                copy("av").start()
                copy("au").start()
                copy("fl").start()
        elif level == 5:

            @pl.when(self.end)
            def _():
                copy("zc").wait_recv()
                copy("av").start()
                copy("au").start()
                copy("fl").start()
        elif level == 6:
            copy("av").wait_recv()
            copy("aw").start()
        elif level == 7:
            copy("au").wait_recv()
            copy("aw").wait_recv()

    def line(self, g):
        base = g * ROWS + LROWS
        upper = self.upper
        three = base + CHUNK * (1 - upper)
        far = base + 2 * CHUNK * (1 - upper)
        near = base + 2 * CHUNK * upper
        outer = base + 3 * CHUNK * upper
        own = base + CHUNK * self.z
        return three, far, near, outer, own

    def line_copy(self, kind, g):
        three, far, near, outer, own = self.line(g)
        grad, res, r = self.grad, self.res, self.r
        base = g * ROWS + LROWS
        final = r["fz"].at[g]
        here = part(res, own, CHUNK)
        if kind == "ze":
            return self.copy(kind, g, part(grad, three, 3 * CHUNK), r["ze"].at[g], self.pair)
        if kind == "zm":
            return self.copy(kind, g, part(grad, far, 2 * CHUNK), r["zm"].at[g], self.other)
        if kind == "zo":
            return self.copy(kind, g, part(grad, outer, CHUNK), r["zo"].at[g], self.pair)
        if kind == "ex":
            return self.copy(kind, g, part(grad, own, CHUNK), r["ex"].at[g], self.px)
        if kind == "ey":
            return self.copy(kind, g, r["tx"].at[g], r["ey"].at[g], self.py)
        if kind in ("ge", "gd"):
            return self.copy(kind, g, final, here, self.pair)
        if kind == "gn":
            return self.copy(kind, g, final, here, self.other)
        if kind == "gf":
            rows = part(res, outer, CHUNK)
            return self.copy(kind, g, rows, rows, self.other)
        if kind == "gp":
            rows = part(res, base + CHUNK * (3 - self.z), CHUNK)
            return self.copy(kind, g, rows, rows, self.pair)
        if kind == "gq":
            rows = part(res, base + 3 * CHUNK * (1 - self.upper), CHUNK)
            return self.copy(kind, g, rows, rows, self.pair)
        return pltpu.make_async_copy(final, here, self.local.at[1])

    def line_level(self, g, level):
        three, far, near, outer, own = self.line(g)
        grad, r = self.grad, self.r
        copy = functools.partial(self.line_copy, g=g)
        if level == 0:

            @pl.when(self.end)
            def _():
                copy("ze").start()
        elif level == 1:

            @pl.when(self.mid)
            def _():
                copy("ze").wait_recv()
                added(grad, far, [(grad, far), (r["ze"].at[g], far - three)], 2 * CHUNK)
                copy("zm").start()
        elif level == 2:

            @pl.when(self.mid)
            def _():
                copy("zm").wait_recv()
                added(grad, outer, [(grad, outer), (r["zm"].at[g], outer - near)], CHUNK)
                copy("zo").start()
                added(grad, own, [(grad, own), (r["ze"].at[g], own - three), (r["zm"].at[g], own - near)], CHUNK)
                copy("ex").start()
        elif level == 3:

            @pl.when(self.end)
            def _():
                copy("zo").wait_recv()
                added(grad, own, [(grad, own), (r["zo"].at[g], 0)], CHUNK)
                copy("ex").start()
        elif level == 4:
            copy("ex").wait_recv()
            added(r["tx"].at[g], 0, [(grad, own), (r["ex"].at[g], 0)], CHUNK)
            copy("ey").start()
        elif level == 5:
            copy("ey").wait_recv()
            added(r["fz"].at[g], 0, [(r["tx"].at[g], 0), (r["ey"].at[g], 0)], CHUNK)
            copy("fz").start()

            @pl.when(self.end)
            def _():
                copy("ge").start()

            @pl.when(self.mid)
            def _():
                copy("gn").start()
                copy("gd").start()
        elif level == 6:

            @pl.when(self.mid)
            def _():
                copy("ge").wait_recv()
                copy("gf").start()
                copy("gn").wait_recv()
                copy("gp").start()
        elif level == 7:

            @pl.when(self.mid)
            def _():
                copy("gf").wait_recv()
                copy("gq").start()
        elif level == 8:

            @pl.when(self.end)
            def _():
                copy("gd").wait_recv()
                copy("gp").wait_recv()
                copy("gq").wait_recv()

    def small_copy(self, kind):
        j = SMALL_KINDS.index(kind)
        s = self.small
        source, target, to = dict(
            sx=(s.at[0], s.at[5], self.px),
            sy=(s.at[1], s.at[6], self.py),
            sa=(s.at[2], s.at[7], self.pair),
            sb=(s.at[3], s.at[8], self.other),
            sc=(s.at[4], s.at[4], self.pair),
        )[kind]
        return pltpu.make_async_remote_copy(
            src_ref=source, dst_ref=target, send_sem=self.small_send.at[j], recv_sem=self.small_recv.at[j],
            device_id=to, device_id_type=MESH)

    def small_level(self, level):
        copy, s = self.small_copy, self.small
        if level == 0:
            copy("sx").start()
        elif level == 1:
            copy("sx").wait_recv()
            s[1] = s[0] + s[5]
            copy("sy").start()
        elif level == 2:
            copy("sy").wait_recv()
            s[2] = s[1] + s[6]

            @pl.when(self.end)
            def _():
                copy("sa").start()
        elif level == 3:

            @pl.when(self.mid)
            def _():
                copy("sa").wait_recv()
                s[3] = s[2] + s[7]
                copy("sb").start()
        elif level == 4:

            @pl.when(self.mid)
            def _():
                copy("sb").wait_recv()
                s[4] = s[3] + s[8]
                copy("sc").start()
        elif level == 5:

            @pl.when(self.end)
            def _():
                copy("sc").wait_recv()

    def tick(self, t, begins, small_begin):
        for level in reversed(range(Z_LEVELS)):
            for kind, stride, late, act in (
                (0, L_STRIDE, 0, self.square_level),
                (1, Z_STRIDE, Z_LATE, self.line_level),
            ):
                if kind == 0 and level >= L_LEVELS:
                    continue
                step = t - late - stride * level
                g = jnp.int32(-1)
                for j, begin in enumerate(begins):
                    g = jnp.where(step == begin, j, g)

                @pl.when(g >= 0)
                def _():
                    act(g, level)

        for level in range(6):

            @pl.when(t == small_begin + level)
            def _():
                self.small_level(level)

    def all_sent(self, kind, rows):
        everything = self.grad.at[pl.ds(0, GROUPS * rows)]
        pltpu.make_async_remote_copy(
            src_ref=everything, dst_ref=everything, send_sem=self.send.at[KINDS.index(kind)],
            recv_sem=self.recv.at[0, 0], device_id=self.px, device_id_type=MESH).wait_send()

    def drain(self):
        for j, rows in ((0, QUARTER), (1, CHUNK)):
            everything = self.grad.at[pl.ds(0, GROUPS * rows)]
            pltpu.make_async_copy(everything, self.res.at[pl.ds(0, GROUPS * rows)], self.local.at[j]).wait()
        self.all_sent("ru", HALF)
        for kind in ("rv", "av", "au", "aw"):
            self.all_sent(kind, QUARTER)
        for kind in ("ex", "ey"):
            self.all_sent(kind, CHUNK)

        @pl.when(self.end)
        def _():
            self.all_sent("za", QUARTER)
            self.all_sent("ze", 3 * CHUNK)
            self.all_sent("ge", CHUNK)

        @pl.when(self.mid)
        def _():
            self.all_sent("zb", QUARTER)
            self.all_sent("zc", QUARTER)
            self.all_sent("zm", 2 * CHUNK)
            for kind in ("zo", "gn", "gd", "gf", "gp", "gq"):
                self.all_sent(kind, CHUNK)

        self.small_copy("sx").wait_send()
        self.small_copy("sy").wait_send()

        @pl.when(self.end)
        def _():
            self.small_copy("sa").wait_send()

        @pl.when(self.mid)
        def _():
            self.small_copy("sb").wait_send()
            self.small_copy("sc").wait_send()


def normed(value):
    mean = jnp.mean(value, axis=-1, keepdims=True)
    centred = value - mean
    spread = jnp.mean(centred * centred, axis=-1, keepdims=True)
    scale = lax.rsqrt(spread + EPS)
    return centred * scale, mean, scale, spread


def gelu(w):
    t = jnp.tanh(w * (2.0 * GELU_A + (8.0 * GELU_B) * (w * w)))
    return w + w * t


def gelu_slope(w):
    square = w * w
    t = jnp.tanh(w * (2.0 * GELU_A + (8.0 * GELU_B) * square))
    q = w * (GELU_A + (12.0 * GELU_B) * square)
    return (0.5 + q) + t * (0.5 - q * t)


def norm_gelu_back(grad, n, scale, gain, half_gain, half_shift):
    dv = grad * gelu_slope(n * half_gain + half_shift)
    terms = dv * n
    dn = dv * gain
    first = jnp.mean(dn, axis=-1, keepdims=True)
    second = jnp.mean(terms * gain, axis=-1, keepdims=True)
    return dv, terms, scale * (dn - first - n * second)


def fold(value):
    rows, width = value.shape
    return jnp.sum(value.reshape(rows // 8, 8, width), axis=0)


def nn(a, b):
    return jnp.dot(a, b, preferred_element_type=F32)


def nt(a, b):
    return lax.dot_general(a, b, (((1,), (1,)), ((), ())), preferred_element_type=F32)


def tn(a, b):
    return lax.dot_general(a, b, (((0,), (0,)), ((), ())), preferred_element_type=F32)


def blocks_kernel(
    names, with_sums, last,
    ends, lengths, outer_gain, inner_gains, outer_biases, inner_biases, down_hbm, conv_hbm, up_hbm,
    ends_out, res, small_out,
    down, conv, up, X, GY, HA, CW, HC, GCW, GP, NB, NC, ST, XS, wide, handing, taps, lhs, oacc, iacc, grad, small,
    *rest,
):
    buffers = dict(zip(names, rest[: len(names)]))
    send, recv, local, small_send, small_recv, load, hand_send, hand_recv, halo_send, halo_recv, store = rest[len(names) :]
    micro, rows, width = X.shape
    inner = down.shape[1]
    section = lax.axis_index("section")
    dp = lax.axis_index("dp")
    z = lax.axis_index("seq")
    first = section == 0
    second = section == 1
    has_left = z > 0
    has_right = z < last
    across = (1 - section, dp, z)
    left = (section, dp, jnp.maximum(z - 1, 0))
    right = (section, dp, jnp.minimum(z + 1, last))
    sums = WeightSums(grad, res, small, buffers, send, recv, local, small_send, small_recv)

    def when(condition, act):
        pl.when(condition)(lambda: act() and None)

    def weight_load(j):
        return pltpu.make_async_copy((down_hbm, conv_hbm, up_hbm)[j], (down, conv, up)[j], load.at[micro + j])

    def end_load(mb, target):
        return pltpu.make_async_copy(ends.at[mb], target.at[mb], load.at[mb])

    @pl.when(first)
    def _():
        end_load(0, X).start()
        weight_load(0).start()

    barrier = pltpu.get_barrier_semaphore()

    def greet(to):
        pl.semaphore_signal(barrier, inc=1, device_id=to, device_id_type=MESH)

    greet(across)
    when(has_left, lambda: greet(left))
    when(has_right, lambda: greet(right))
    if with_sums:
        greet(sums.px)
        greet(sums.py)

    def met():
        peers = (3 if with_sums else 1) + has_left.astype(jnp.int32) + has_right.astype(jnp.int32)
        pl.semaphore_wait(barrier, peers)

    XS[...] = jnp.zeros_like(XS)
    oacc[...] = jnp.zeros_like(oacc)
    iacc[...] = jnp.zeros_like(iacc)
    edge = jnp.zeros((rows, inner), BF)
    for mb in range(micro):

        @pl.when(jnp.logical_not(has_left))
        def _():
            CW[mb, 0:rows, :] = edge
            GCW[mb, 0:rows, :] = edge

        @pl.when(jnp.logical_not(has_right))
        def _():
            CW[mb, 2 * rows : 3 * rows, :] = edge
            GCW[mb, 2 * rows : 3 * rows, :] = edge

    @pl.when(first)
    def _():
        end_load(0, X).wait()
        weight_load(0).wait()
        weight_load(1).start()
        weight_load(2).start()
        for mb in range(1, micro):
            end_load(mb, X).start()

    @pl.when(second)
    def _():
        for j in range(3):
            weight_load(j).start()
        for mb in range(micro):
            end_load(mb, GY).start()

    def halo_copies(ref, which, mb):
        def make(side, count):
            if side == 0:
                source, target, to = ref.at[mb, pl.ds(2 * rows - count, count)], ref.at[mb, pl.ds(rows - count, count)], right
            else:
                source, target, to = ref.at[mb, pl.ds(rows, count)], ref.at[mb, pl.ds(2 * rows, count)], left
            return pltpu.make_async_remote_copy(
                src_ref=source, dst_ref=target, send_sem=halo_send.at[which, mb, side],
                recv_sem=halo_recv.at[which, mb, side], device_id=to, device_id_type=MESH)

        return make

    def halo(ref, which, mb, act_right, act_left):
        make = halo_copies(ref, which, mb)
        for mine, count in ((first, EDGE), (second, rows)):

            @pl.when(mine)
            def _():
                when(act_right[0], lambda: act_right[1](make(0, count)))
                when(act_left[0], lambda: act_left[1](make(1, count)))

    def halo_start(ref, which, mb):
        go = lambda c: c.start()
        halo(ref, which, mb, (has_right, go), (has_left, go))

    def halo_arrived(ref, which, mb):
        go = lambda c: c.wait_recv()
        halo(ref, which, mb, (has_left, go), (has_right, go))

    def halo_sent(ref, which, mb):
        go = lambda c: c.wait_send()
        halo(ref, which, mb, (has_right, go), (has_left, go))

    def shifted(ref, mb, k, sign, target, at, column):
        shift = sign * (k - REACH)

        @pl.when(first)
        def _():
            target[at : at + rows, column : column + inner] = ref[mb, pl.ds(rows + shift * FIRST_DILATION, rows), :]

        @pl.when(second)
        def _():
            target[at : at + rows, column : column + inner] = ref[mb, pl.ds(rows + shift * SECOND_DILATION, rows), :]

    def all_shifted(ref, mb, sign):
        for mine, dilation in ((first, FIRST_DILATION), (second, SECOND_DILATION)):

            @pl.when(mine)
            def _():
                for k in range(FILTER_TAPS):
                    at = rows + sign * (k - REACH) * dilation
                    taps[:, k * inner : (k + 1) * inner] = ref[mb, pl.ds(at, rows), :]

    def hand_over(mb, target):
        slot = lax.rem(mb, 2)
        return pltpu.make_async_remote_copy(
            src_ref=handing.at[slot], dst_ref=target.at[mb], send_sem=hand_send.at[mb], recv_sem=hand_recv.at[mb],
            device_id=across, device_id_type=MESH)

    def store_end(mb):
        return pltpu.make_async_copy(wide.at[lax.rem(mb, 2)], ends_out.at[mb], store.at[mb])

    own = pl.ds(rows, rows)
    outer_shift, inner_shift_b, inner_shift_c = 0.5 * outer_biases[0:1, :], 0.5 * inner_biases[0:1, :], 0.5 * inner_biases[1:2, :]
    outer_half, inner_half_b, inner_half_c = 0.5 * outer_gain[...], 0.5 * inner_gains[0:1, :], 0.5 * inner_gains[1:2, :]

    def valid_of(mb):
        position = z * rows + lax.broadcasted_iota(jnp.int32, (rows, 1), 0)
        return (position < lengths[mb]).astype(F32)

    def forward_a(mb):
        when(jnp.logical_and(first, mb > 0), lambda: end_load(mb, X).wait())
        when(second, lambda: hand_over(mb, X).wait_recv())
        when(jnp.logical_and(second, mb == 0), lambda: weight_load(0).wait())
        n, mean, scale, spread = normed(X[mb].astype(F32))
        XS[...] += (spread + mean * mean) * valid_of(mb)
        ST[mb, :, 0:1] = mean
        ST[mb, :, 1:2] = scale
        hidden = gelu(n * outer_half + outer_shift).astype(BF)
        HA[mb] = hidden
        n, _, scale, _ = normed(nn(hidden, down[...]) + inner_biases[2:3, :])
        NB[mb] = n
        ST[mb, :, 2:3] = scale
        CW[mb, own, :] = (gelu(n * inner_half_b + inner_shift_b) * valid_of(mb)).astype(BF)
        when(jnp.logical_and(first, mb == 0), met)
        halo_start(CW, 0, mb)

    halves = [slice(h * (rows // 2), (h + 1) * (rows // 2)) for h in range(2)]

    def forward_b(mb):
        slot = lax.rem(mb, 2)
        halo_arrived(CW, 0, mb)

        @pl.when(mb == 0)
        def _():
            weight_load(1).wait()
            weight_load(2).wait()

        @pl.when(mb >= 2)
        def _():
            when(first, lambda: hand_over(mb - 2, X).wait_send())
            when(second, lambda: store_end(mb - 2).wait())

        all_shifted(CW, mb, 1)

        def norm_c(half, product):
            n, _, scale, _ = normed(product + inner_biases[3:4, :])
            NC[mb, half, :] = n
            ST[mb, half, 3:4] = scale
            hidden = (gelu(n * inner_half_c + inner_shift_c) * valid_of(mb)[half, :]).astype(BF)
            HC[mb, half, :] = hidden
            return hidden

        def close(half, product):
            branch = (product + outer_biases[1:2, :]) * valid_of(mb)[half, :]
            oacc[3] += fold(branch * branch)
            value = X[mb, half, :].astype(F32) + branch
            wide[slot, half, :] = value
            handing[slot, half, :] = value.astype(BF)

        lower = nn(taps[halves[0], :], conv[...])
        upper = nn(taps[halves[1], :], conv[...])
        hidden = norm_c(halves[0], lower)
        lower = nn(hidden, up[...])
        hidden = norm_c(halves[1], upper)
        upper = nn(hidden, up[...])
        close(halves[0], lower)
        close(halves[1], upper)
        when(first, lambda: hand_over(mb, X).start())
        when(second, lambda: store_end(mb).start())

    def backward_a(mb):
        when(jnp.logical_and(first, mb < micro - 1), lambda: hand_over(mb, GY).wait_recv())

        @pl.when(jnp.logical_and(second, mb == 0))
        def _():
            for k in range(micro):
                end_load(k, GY).wait()

        valid = valid_of(mb)
        oacc[2] += fold(GY[mb].astype(F32) * valid)
        dv, terms, dz = norm_gelu_back(
            nt(GY[mb], up[...]) * valid, NC[mb], ST[mb, :, 3:4], inner_gains[1:2, :], inner_half_c, inner_shift_c
        )
        iacc[3] += fold(terms)
        iacc[4] += fold(dv)
        iacc[5] += fold(dz)
        GCW[mb, own, :] = dz.astype(BF)
        halo_start(GCW, 1, mb)

    def backward_b(mb):
        halo_arrived(GCW, 1, mb)
        all_shifted(GCW, mb, -1)
        total = nt(taps[:, 0:inner], conv[0:inner, :])
        for k in range(1, FILTER_TAPS):
            total = total + nt(taps[:, k * inner : (k + 1) * inner], conv[k * inner : (k + 1) * inner, :])
        dv, terms, dz = norm_gelu_back(
            total * valid_of(mb), NB[mb], ST[mb, :, 2:3], inner_gains[0:1, :], inner_half_b, inner_shift_b
        )
        iacc[0] += fold(terms)
        iacc[1] += fold(dv)
        iacc[2] += fold(dz)
        GP[mb] = dz.astype(BF)

    def backward_c(mb):
        slot = lax.rem(mb, 2)

        @pl.when(mb < 2)
        def _():
            when(first, lambda: hand_over(mb + micro - 2, X).wait_send())
            when(second, lambda: store_end(mb + micro - 2).wait())

        @pl.when(mb >= 2)
        def _():
            when(second, lambda: hand_over(mb - 2, GY).wait_send())
            when(first, lambda: store_end(mb - 2).wait())

        scale = ST[mb, :, 1:2]
        n = (X[mb].astype(F32) - ST[mb, :, 0:1]) * scale
        dv, terms, dz = norm_gelu_back(nt(GP[mb], down[...]), n, scale, outer_gain[...], outer_half, outer_shift)
        oacc[0] += fold(terms)
        oacc[1] += fold(dv)
        value = GY[mb].astype(F32) + dz
        wide[slot] = value
        handing[slot] = value.astype(BF)
        when(second, lambda: hand_over(mb, GY).start())
        when(first, lambda: store_end(mb).start())

    def weight_up():
        when(first, lambda: hand_over(micro - 1, GY).wait_recv())
        c = HC[...].reshape(micro * rows, inner)
        for h in range(UP_BLOCKS):
            y = GY[:, :, h * inner : (h + 1) * inner].reshape(micro * rows, inner)
            grad[h * BLOCK : (h + 1) * BLOCK, :] = tn(c, y).astype(BF)

    def weight_tap(tap):
        for k in range(FILTER_TAPS):

            @pl.when(tap == k)
            def _():
                for mb in range(micro):
                    shifted(CW, mb, k, 1, lhs, mb * rows, 0)

        y = GCW[:, own, :].reshape(micro * rows, inner)
        at = pl.multiple_of((UP_BLOCKS + tap) * BLOCK, BLOCK)
        grad[pl.ds(at, BLOCK), :] = tn(lhs[...], y).astype(BF)

    def weight_down():
        y = GP[...].reshape(micro * rows, inner)
        for h in range(BLOCKS - DOWN_AT):
            at = (DOWN_AT + h) * BLOCK
            a = HA[:, :, h * inner : (h + 1) * inner].reshape(micro * rows, inner)
            grad[at : at + BLOCK, :] = tn(a, y).astype(BF)

    def row(value):
        return jnp.sum(value, axis=0, keepdims=True)

    def smalls():
        place = 0

        def put(value):
            nonlocal place
            for at in range(0, value.shape[1], inner):
                small[0, place : place + 1, :] = value[:, at : at + inner]
                place += 1

        small[0] = jnp.zeros_like(small[0])
        for ref, j in ((oacc, 0), (iacc, 0), (iacc, 3), (oacc, 1), (oacc, 2), (iacc, 1), (iacc, 4), (iacc, 2), (iacc, 5)):
            put(row(ref[j]))
        lane = lax.broadcasted_iota(jnp.int32, (1, inner), 1)
        put(jnp.where(lane == 0, row(XS[...]) * width, 0.0))
        value = row(oacc[3])
        put(value[:, :inner] + value[:, inner:])
        count = jnp.float32(0)
        for mb in range(micro):
            count += jnp.clip(lengths[mb] - z * rows, 0, rows).astype(F32)
        put(jnp.zeros((1, inner), F32) + count)

    when(second, met)
    plans = [[(p * 8 + k) * 8 + steps for p, k, steps in plan] for plan in (FIRST_PLAN, SECOND_PLAN)]
    begins = [jnp.where(first, a, b) for a, b in zip(begins_of(FIRST_PLAN), begins_of(SECOND_PLAN))]
    ticks = jnp.where(first, steps_of(FIRST_PLAN), steps_of(SECOND_PLAN))

    def tick(t, carry):
        sums.tick(t, begins, begins[-1])
        return carry

    def step(i, t):
        entry = jnp.int32(0)
        for j, (a, b) in enumerate(zip(*plans)):
            entry = jnp.where(i == j, jnp.where(first, a, b), entry)
        what, k = entry // 64, lax.rem(entry // 8, 8)
        for p, act in ((FA, forward_a), (FB, forward_b), (BA, backward_a), (BB, backward_b), (BC, backward_c), (WC, weight_tap)):
            when(what == p, functools.partial(act, k))
        when(what == WU, weight_up)

        @pl.when(what == WD)
        def _():
            smalls()
            weight_down()

        then = t + lax.rem(entry, 8)
        if with_sums:
            lax.fori_loop(t, then, tick, 0)
        return then

    t = lax.fori_loop(0, len(FIRST_PLAN), step, jnp.int32(0))

    if with_sums:
        lax.fori_loop(t, ticks, tick, 0)
        sums.drain()
        done = pltpu.make_async_copy(small.at[4], small_out, load.at[0])
        done.start()
        done.wait()
    else:
        done = pltpu.make_async_copy(small.at[0], small_out, load.at[0])
        done.start()
        done.wait()
        done = pltpu.make_async_copy(grad, res, load.at[1])
        done.start()
        done.wait()
    for mb in range(micro):
        if mb >= micro - 2:
            when(first, functools.partial(lambda m: store_end(m).wait(), mb))
            when(second, functools.partial(lambda m: hand_over(m, GY).wait_send(), mb))
        halo_sent(CW, 0, mb)
        halo_sent(GCW, 1, mb)


def run_blocks(mesh_shape, ends, lengths, outer_gain, inner_gains, outer_biases, inner_biases, down, conv, up):
    micro, rows, width = ends.shape
    inner = down.shape[1]
    taps = FILTER_TAPS
    with_sums = (mesh_shape["dp"], mesh_shape["seq"]) == (4, 4)
    buffers = {k: pltpu.VMEM((GROUPS, n, BLOCK), BF) for k, n in RECEIVE.items()} if with_sums else {}
    names = tuple(buffers)
    total = BLOCKS * BLOCK
    anywhere = pl.BlockSpec(memory_space=pl.ANY)
    vmem = pl.BlockSpec(memory_space=pltpu.VMEM)
    dma = pltpu.SemaphoreType.DMA
    scratch = [
        pltpu.VMEM(down.shape, BF),
        pltpu.VMEM(conv.shape, BF),
        pltpu.VMEM(up.shape, BF),
        pltpu.VMEM((micro, rows, width), BF),
        pltpu.VMEM((micro, rows, width), BF),
        pltpu.VMEM((micro, rows, width), BF),
        pltpu.VMEM((micro, 3 * rows, inner), BF),
        pltpu.VMEM((micro, rows, inner), BF),
        pltpu.VMEM((micro, 3 * rows, inner), BF),
        pltpu.VMEM((micro, rows, inner), BF),
        pltpu.VMEM((micro, rows, inner), F32),
        pltpu.VMEM((micro, rows, inner), F32),
        pltpu.VMEM((micro, rows, 128), F32),
        pltpu.VMEM((rows, 1), F32),
        pltpu.VMEM((2, rows, width), F32),
        pltpu.VMEM((2, rows, width), BF),
        pltpu.VMEM((rows, taps * inner), BF),
        pltpu.VMEM((micro * rows, inner), BF),
        pltpu.VMEM((4, 8, width), F32),
        pltpu.VMEM((6, 8, inner), F32),
        pltpu.VMEM((total, BLOCK), BF),
        pltpu.VMEM((9, 16, inner), F32),
        *[buffers[k] for k in names],
        dma((len(KINDS),)),
        dma((GROUPS, max(ARRIVES.values()) + 1)),
        dma((2,)),
        dma((len(SMALL_KINDS),)),
        dma((len(SMALL_KINDS),)),
        dma((micro + 3,)),
        dma((micro,)),
        dma((micro,)),
        dma((2, micro, 2)),
        dma((2, micro, 2)),
        dma((micro,)),
    ]
    flops = 2 * 3 * micro * rows * (2 * width * inner + taps * inner * inner)
    return pl.pallas_call(
        functools.partial(blocks_kernel, names, with_sums, mesh_shape["seq"] - 1),
        name="two_blocks",
        out_shape=(
            jax.ShapeDtypeStruct((micro, rows, width), F32),
            jax.ShapeDtypeStruct((total, BLOCK), BF),
            jax.ShapeDtypeStruct((16, inner), F32),
        ),
        in_specs=[anywhere, pl.BlockSpec(memory_space=pltpu.SMEM), vmem, vmem, vmem, vmem, anywhere, anywhere, anywhere],
        out_specs=[anywhere] * 3,
        scratch_shapes=scratch,
        cost_estimate=pl.CostEstimate(flops=flops, bytes_accessed=40 * 2**20, transcendentals=0),
        compiler_params=pltpu.CompilerParams(collective_id=1, has_side_effects=True, vmem_limit_bytes=62 * 2**20),
    )(ends, lengths, outer_gain, inner_gains, outer_biases, inner_biases, down, conv, up)


def finish_kernel(
    ends, rows, small, ends_out, outer_gain, inner_gains, outer_biases, inner_biases, down, conv, up, rms, raw, full, held,
    ends_load, ends_store, load, store,
):
    micro, width = ends.shape[0], ends.shape[2]
    into = [pltpu.make_async_copy(ends.at[mb], held.at[mb], ends_load.at[mb]) for mb in range(micro)]
    out = [pltpu.make_async_copy(held.at[mb], ends_out.at[0, mb, 0], ends_store.at[mb]) for mb in range(micro)]
    loads = [
        pltpu.make_async_copy(rows.at[pl.ds(g * BLOCK, BLOCK)], raw.at[g], load.at[g]) for g in range(BLOCKS)
    ]
    for copy in into + loads:
        copy.start()
    outer_gain[0:1, 0:BLOCK] = small[0:1, :]
    outer_gain[0:1, BLOCK:] = small[1:2, :]
    inner_gains[0] = small[2:4, :]
    for j in range(2):
        outer_biases[0, j : j + 1, 0:BLOCK] = small[4 + 2 * j : 5 + 2 * j, :]
        outer_biases[0, j : j + 1, BLOCK:] = small[5 + 2 * j : 6 + 2 * j, :]
    inner_biases[0] = small[8:12, :]
    squares = jnp.sum(small[12:14, :], axis=1, keepdims=True)
    roots = jnp.sqrt(squares / (small[14:15, 0:1] * width))
    rms[0:1, 0:1] = roots[0:1, :]
    rms[0:1, 1:2] = roots[1:2, :]
    places = [up.at[0, :, pl.ds(h * BLOCK, BLOCK)] for h in range(UP_BLOCKS)]
    places += [conv.at[0, k] for k in range(FILTER_TAPS)]
    places += [down.at[0, pl.ds(h * BLOCK, BLOCK)] for h in range(BLOCKS - DOWN_AT)]
    stores = []
    for mb in range(micro):
        into[mb].wait()
        out[mb].start()
    for g in range(BLOCKS):
        loads[g].wait()
        full[g] = raw[g].astype(F32)
        stores.append(pltpu.make_async_copy(full.at[g], places[g], store.at[g]))
        stores[-1].start()
    for copy in out + stores:
        copy.wait()


def finish(shapes, ends, rows, small):
    anywhere = pl.BlockSpec(memory_space=pl.ANY)
    vmem = pl.BlockSpec(memory_space=pltpu.VMEM)
    dma = pltpu.SemaphoreType.DMA
    return pl.pallas_call(
        finish_kernel,
        name="outputs",
        out_shape=tuple(jax.ShapeDtypeStruct(shape, F32) for shape in shapes),
        in_specs=[anywhere, anywhere, vmem],
        out_specs=[anywhere, vmem, vmem, vmem, vmem, anywhere, anywhere, anywhere, vmem],
        scratch_shapes=[
            pltpu.VMEM((BLOCKS, BLOCK, BLOCK), BF),
            pltpu.VMEM((BLOCKS, BLOCK, BLOCK), F32),
            pltpu.VMEM(ends.shape, F32),
            dma((ends.shape[0],)),
            dma((ends.shape[0],)),
            dma((BLOCKS,)),
            dma((BLOCKS,)),
        ],
        compiler_params=pltpu.CompilerParams(vmem_limit_bytes=60 * 2**20),
    )(ends, rows, small)


def body(
    mesh_shape, ends_in, lengths, outer_gain, inner_gains, outer_biases, inner_biases, down_in, conv_weight, up_out
):
    width = ends_in.shape[-1]
    ends, rows, small = run_blocks(
        mesh_shape, ends_in.reshape(ends_in.shape[1], -1, width), lengths.reshape(-1), outer_gain, inner_gains[0],
        outer_biases[0], inner_biases[0], down_in[0], conv_weight[0].reshape(-1, conv_weight.shape[-1]), up_out[0],
    )
    if (mesh_shape["dp"], mesh_shape["seq"]) == (4, 4):
        weights = (outer_gain, inner_gains, outer_biases, inner_biases, down_in, conv_weight, up_out)
        return finish((ends_in.shape, *(w.shape for w in weights), (1, 2)), ends, rows, small)
    rows, small = lax.psum((rows.astype(F32), small), ("dp", "seq"))
    up = jnp.concatenate([rows[:BLOCK], rows[BLOCK : 2 * BLOCK]], axis=1)
    conv = rows[UP_BLOCKS * BLOCK : DOWN_AT * BLOCK].reshape(conv_weight.shape[1:])
    down = rows[DOWN_AT * BLOCK :]
    rms = jnp.sqrt(jnp.sum(small[12:14], axis=1) / (small[14, 0] * width))
    return (
        ends.reshape(ends_in.shape),
        small[0:2].reshape(1, -1),
        small[None, 2:4],
        small[4:8].reshape(1, 2, -1),
        small[None, 8:12],
        down[None],
        conv[None],
        up[None],
        rms[None],
    )


def solution(mesh):
    in_specs = (
        P("section", None, "dp", "seq", None),
        P(None, "dp"),
        P("section", None),
        P("section", None, None),
        P("section", None, None),
        P("section", None, None),
        P("section", None, None),
        P("section", None, None, None),
        P("section", None, None),
    )
    out_specs = (
        P("section", None, "dp", "seq", None),
        P("section", None),
        P("section", None, None),
        P("section", None, None),
        P("section", None, None),
        P("section", None, None),
        P("section", None, None, None),
        P("section", None, None),
        P("section", None),
    )
    return jax.shard_map(
        functools.partial(body, dict(mesh.shape)), mesh=mesh, in_specs=in_specs, out_specs=out_specs, check_vma=False
    )
```

```python
import functools
import math

import jax
import jax.numpy as jnp
from jax import lax
from jax.experimental import pallas as pl
from jax.experimental.pallas import tpu as pltpu
from jax.sharding import PartitionSpec as P

MESH = pl.DeviceIdType.MESH
BF = jnp.bfloat16
F32 = jnp.float32
FILTER_TAPS = 5
FIRST_DILATION = 2
SECOND_DILATION = 128
REACH = FILTER_TAPS // 2
EPS = 1e-05
GELU_A = math.sqrt(2.0 / math.pi)
GELU_B = GELU_A * 0.044715
EDGE = 16

BLOCK = 640
UP_BLOCKS = 2
DOWN_AT = UP_BLOCKS + FILTER_TAPS
BLOCKS = DOWN_AT + 2
GROUPS = 10
ROWS = BLOCKS * BLOCK // GROUPS
LROWS = 384
HALF = LROWS // 2
QUARTER = LROWS // 4
CHUNK = (ROWS - LROWS) // 4
KINDS = (
    "ru", "rv", "za", "zb", "zc", "av", "au", "aw",
    "ze", "zm", "zo", "ex", "ey", "ge", "gn", "gd", "gf", "gp", "gq",
)
ARRIVES = dict(ru=0, rv=1, av=2, au=3, aw=4, ex=5, ey=6, za=7, zb=8, ze=9, zm=10, ge=11, gn=12, gf=13,
               zc=7, zo=8, gd=9, gp=10, gq=11)
SMALL_KINDS = ("sx", "sy", "sa", "sb", "sc")
RECEIVE = dict(ru=HALF, rv=QUARTER, za=QUARTER, zb=QUARTER, fl=QUARTER, ze=3 * CHUNK, zm=2 * CHUNK,
               zo=CHUNK, ex=CHUNK, ey=CHUNK, tx=CHUNK, fz=CHUNK)
L_LEVELS = 8
Z_LEVELS = 9
FIRST_PACE = (2, 2, 0, 1)
SECOND_PACE = (2, 2, 0, 1)

FA, FB, WU, BA, BB, BC, WC, WD = range(1, 9)
FIRST_PLAN = (
    (FA, 0, 0), (FA, 1, 0), (FB, 0, 0), (FA, 2, 0), (FB, 1, 0), (FA, 3, 0), (FB, 2, 0), (FB, 3, 0), (BA, 0, 0), (BA, 1, 0), (BB, 0, 0), (BC, 0, 0), (BA, 2, 0), (BB, 1, 0), (BC, 1, 0), (WU, 0, 0), (BA, 3, 1), (BB, 2, 0), (BC, 2, 1), (BB, 3, 0), (BC, 3, 1), (WC, 0, 0), (WC, 1, 0), (WC, 2, 3), (WC, 3, 3), (WC, 4, 1), (WD, 0, 0),
)
SECOND_PLAN = (
    (FA, 0, 0), (FA, 1, 0), (FB, 0, 0), (FA, 2, 0), (FB, 1, 0), (FA, 3, 0), (FB, 2, 0), (BA, 0, 0), (FB, 3, 0), (WU, 0, 1), (BA, 1, 0), (BB, 0, 0), (BC, 0, 1), (BA, 2, 1), (BB, 1, 0), (BC, 1, 1), (BA, 3, 1), (BB, 2, 0), (BC, 2, 1), (WC, 0, 1), (WC, 1, 1), (BB, 3, 0), (BC, 3, 1), (WC, 2, 1), (WC, 3, 1), (WC, 4, 1), (WD, 0, 1),
)


def begins_of(plan, pace):
    ready, steps = {}, 0
    for what, k, count in plan:
        for block in {WU: range(UP_BLOCKS), WC: (UP_BLOCKS + k,), WD: range(DOWN_AT, BLOCKS)}.get(what, ()):
            ready[block] = steps
        steps += count
    begins = []
    for g in range(GROUPS):
        there = max(ready[block] for block in range(g * ROWS // BLOCK, ((g + 1) * ROWS - 1) // BLOCK + 1))
        begins.append(max(there, begins[-1] + pace[3]) if begins else there)
    return begins


def planned_steps(plan):
    return sum(entry[2] for entry in plan)


def steps_of(plan, pace):
    square, line, late, _ = pace
    last = begins_of(plan, pace)[-1] + max(square * (L_LEVELS - 1), late + line * (Z_LEVELS - 1))
    return max(last + 1, planned_steps(plan) + 6)


def aligned(offset):
    return offset if isinstance(offset, int) else pl.multiple_of(offset, 16)


def part(ref, offset, rows):
    return ref.at[pl.ds(aligned(offset), rows)]


def added(target, offset, sources, rows, tile=16):
    for start in range(0, rows, tile):
        total = None
        for ref, at in sources:
            value = ref[pl.ds(aligned(at + start), tile), :]
            if len(sources) > 2:
                value = value.astype(F32)
            total = value if total is None else total + value
        target[pl.ds(aligned(offset + start), tile), :] = total.astype(BF)


class WeightSums:
    def __init__(self, grad, res, small, buffers, send, recv, local, small_send, small_recv):
        self.grad, self.res, self.small, self.r = grad, res, small, buffers
        self.send, self.recv, self.local = send, recv, local
        self.small_send, self.small_recv = small_send, small_recv
        self.c = lax.axis_index("section")
        self.dp = lax.axis_index("dp")
        self.z = lax.axis_index("seq")
        self.x = lax.rem(self.dp, 2)
        self.y = self.dp // 2
        z = self.z
        self.upper = z // 2
        self.end = jnp.logical_or(z == 0, z == 3)
        self.mid = jnp.logical_not(self.end)
        self.dp_x = self.dp + 1 - 2 * self.x
        self.dp_y = lax.rem(self.dp + 2, 4)
        self.px = (self.c, self.dp_x, z)
        self.py = (self.c, self.dp_y, z)
        self.pair = (self.c, self.dp, 1 - z + 4 * self.upper)
        self.other = (self.c, self.dp, jnp.clip(3 - z, 1, 2))

    def copy(self, kind, g, source, target, to):
        j = KINDS.index(kind)
        return pltpu.make_async_remote_copy(
            src_ref=source, dst_ref=target, send_sem=self.send.at[j], recv_sem=self.recv.at[g, ARRIVES[kind]],
            device_id=to, device_id_type=MESH)

    def square(self, g):
        odd = lax.rem(g, 2)
        u = jnp.where(odd == 0, self.x, self.y)
        v = jnp.where(odd == 0, self.y, self.x)
        to_u = (self.c, jnp.where(odd == 0, self.dp_x, self.dp_y), self.z)
        to_v = (self.c, jnp.where(odd == 0, self.dp_y, self.dp_x), self.z)
        base = g * ROWS
        own_half = base + u * HALF
        own = own_half + v * QUARTER
        beside = own_half + (1 - v) * QUARTER
        return base, u, v, to_u, to_v, own, beside

    def square_copy(self, kind, g):
        base, u, v, to_u, to_v, own, beside = self.square(g)
        grad, res, r = self.grad, self.res, self.r
        final = r["fl"].at[g]
        if kind == "ru":
            return self.copy(kind, g, part(grad, base + (1 - u) * HALF, HALF), r["ru"].at[g], to_u)
        if kind == "rv":
            return self.copy(kind, g, part(grad, beside, QUARTER), r["rv"].at[g], to_v)
        if kind == "za":
            return self.copy(kind, g, part(grad, own, QUARTER), r["za"].at[g], self.pair)
        if kind == "zb":
            return self.copy(kind, g, part(grad, own, QUARTER), r["zb"].at[g], self.other)
        if kind == "zc":
            return self.copy(kind, g, final, final, self.pair)
        if kind == "av":
            return self.copy(kind, g, final, part(res, own, QUARTER), to_v)
        if kind == "au":
            return self.copy(kind, g, final, part(res, own, QUARTER), to_u)
        if kind == "aw":
            return self.copy(kind, g, part(res, beside, QUARTER), part(res, beside, QUARTER), to_u)
        return pltpu.make_async_copy(final, part(res, own, QUARTER), self.local.at[0])

    def square_level(self, g, level):
        base, u, v, to_u, to_v, own, beside = self.square(g)
        grad, r = self.grad, self.r
        copy = functools.partial(self.square_copy, g=g)
        if level == 0:
            copy("ru").start()
        elif level == 1:
            copy("ru").wait_recv()
            added(grad, beside, [(grad, beside), (r["ru"].at[g], (1 - v) * QUARTER)], QUARTER)
            copy("rv").start()
            added(grad, own, [(grad, own), (r["ru"].at[g], v * QUARTER)], QUARTER)
        elif level == 2:
            copy("rv").wait_recv()
            added(grad, own, [(grad, own), (r["rv"].at[g], 0)], QUARTER)

            @pl.when(self.end)
            def _():
                copy("za").start()
        elif level == 3:

            @pl.when(self.mid)
            def _():
                copy("za").wait_recv()
                added(grad, own, [(grad, own), (r["za"].at[g], 0)], QUARTER)
                copy("zb").start()
        elif level == 4:

            @pl.when(self.mid)
            def _():
                copy("zb").wait_recv()
                added(r["fl"].at[g], 0, [(grad, own), (r["zb"].at[g], 0)], QUARTER)
                copy("zc").start()
                copy("av").start()
                copy("au").start()
                copy("fl").start()
        elif level == 5:

            @pl.when(self.end)
            def _():
                copy("zc").wait_recv()
                copy("av").start()
                copy("au").start()
                copy("fl").start()
        elif level == 6:
            copy("av").wait_recv()
            copy("aw").start()
        elif level == 7:
            copy("au").wait_recv()
            copy("aw").wait_recv()

    def line(self, g):
        base = g * ROWS + LROWS
        upper = self.upper
        three = base + CHUNK * (1 - upper)
        far = base + 2 * CHUNK * (1 - upper)
        near = base + 2 * CHUNK * upper
        outer = base + 3 * CHUNK * upper
        own = base + CHUNK * self.z
        return three, far, near, outer, own

    def line_copy(self, kind, g):
        three, far, near, outer, own = self.line(g)
        grad, res, r = self.grad, self.res, self.r
        base = g * ROWS + LROWS
        final = r["fz"].at[g]
        here = part(res, own, CHUNK)
        if kind == "ze":
            return self.copy(kind, g, part(grad, three, 3 * CHUNK), r["ze"].at[g], self.pair)
        if kind == "zm":
            return self.copy(kind, g, part(grad, far, 2 * CHUNK), r["zm"].at[g], self.other)
        if kind == "zo":
            return self.copy(kind, g, part(grad, outer, CHUNK), r["zo"].at[g], self.pair)
        if kind == "ex":
            return self.copy(kind, g, part(grad, own, CHUNK), r["ex"].at[g], self.px)
        if kind == "ey":
            return self.copy(kind, g, r["tx"].at[g], r["ey"].at[g], self.py)
        if kind in ("ge", "gd"):
            return self.copy(kind, g, final, here, self.pair)
        if kind == "gn":
            return self.copy(kind, g, final, here, self.other)
        if kind == "gf":
            rows = part(res, outer, CHUNK)
            return self.copy(kind, g, rows, rows, self.other)
        if kind == "gp":
            rows = part(res, base + CHUNK * (3 - self.z), CHUNK)
            return self.copy(kind, g, rows, rows, self.pair)
        if kind == "gq":
            rows = part(res, base + 3 * CHUNK * (1 - self.upper), CHUNK)
            return self.copy(kind, g, rows, rows, self.pair)
        return pltpu.make_async_copy(final, here, self.local.at[1])

    def line_level(self, g, level):
        three, far, near, outer, own = self.line(g)
        grad, r = self.grad, self.r
        copy = functools.partial(self.line_copy, g=g)
        if level == 0:

            @pl.when(self.end)
            def _():
                copy("ze").start()
        elif level == 1:

            @pl.when(self.mid)
            def _():
                copy("ze").wait_recv()
                added(grad, far, [(grad, far), (r["ze"].at[g], far - three)], 2 * CHUNK)
                copy("zm").start()
        elif level == 2:

            @pl.when(self.mid)
            def _():
                copy("zm").wait_recv()
                added(grad, outer, [(grad, outer), (r["zm"].at[g], outer - near)], CHUNK)
                copy("zo").start()
                added(grad, own, [(grad, own), (r["ze"].at[g], own - three), (r["zm"].at[g], own - near)], CHUNK)
                copy("ex").start()
        elif level == 3:

            @pl.when(self.end)
            def _():
                copy("zo").wait_recv()
                added(grad, own, [(grad, own), (r["zo"].at[g], 0)], CHUNK)
                copy("ex").start()
        elif level == 4:
            copy("ex").wait_recv()
            added(r["tx"].at[g], 0, [(grad, own), (r["ex"].at[g], 0)], CHUNK)
            copy("ey").start()
        elif level == 5:
            copy("ey").wait_recv()
            added(r["fz"].at[g], 0, [(r["tx"].at[g], 0), (r["ey"].at[g], 0)], CHUNK)
            copy("fz").start()

            @pl.when(self.end)
            def _():
                copy("ge").start()

            @pl.when(self.mid)
            def _():
                copy("gn").start()
                copy("gd").start()
        elif level == 6:

            @pl.when(self.mid)
            def _():
                copy("ge").wait_recv()
                copy("gf").start()
                copy("gn").wait_recv()
                copy("gp").start()
        elif level == 7:

            @pl.when(self.mid)
            def _():
                copy("gf").wait_recv()
                copy("gq").start()
        elif level == 8:

            @pl.when(self.end)
            def _():
                copy("gd").wait_recv()
                copy("gp").wait_recv()
                copy("gq").wait_recv()

    def small_copy(self, kind):
        j = SMALL_KINDS.index(kind)
        s = self.small
        source, target, to = dict(
            sx=(s.at[0], s.at[5], self.px),
            sy=(s.at[1], s.at[6], self.py),
            sa=(s.at[2], s.at[7], self.pair),
            sb=(s.at[3], s.at[8], self.other),
            sc=(s.at[4], s.at[4], self.pair),
        )[kind]
        return pltpu.make_async_remote_copy(
            src_ref=source, dst_ref=target, send_sem=self.small_send.at[j], recv_sem=self.small_recv.at[j],
            device_id=to, device_id_type=MESH)

    def small_level(self, level):
        copy, s = self.small_copy, self.small
        if level == 0:
            copy("sx").start()
        elif level == 1:
            copy("sx").wait_recv()
            s[1] = s[0] + s[5]
            copy("sy").start()
        elif level == 2:
            copy("sy").wait_recv()
            s[2] = s[1] + s[6]

            @pl.when(self.end)
            def _():
                copy("sa").start()
        elif level == 3:

            @pl.when(self.mid)
            def _():
                copy("sa").wait_recv()
                s[3] = s[2] + s[7]
                copy("sb").start()
        elif level == 4:

            @pl.when(self.mid)
            def _():
                copy("sb").wait_recv()
                s[4] = s[3] + s[8]
                copy("sc").start()
        elif level == 5:

            @pl.when(self.end)
            def _():
                copy("sc").wait_recv()

    def tick(self, t, begins, pace, small_begin):
        square, line, late = pace

        def beginning(step):
            g = jnp.int32(-1)
            for j, begin in enumerate(begins):
                g = jnp.where(step == begin, j, g)
            return g

        for level in reversed(range(Z_LEVELS)):
            g = beginning(t - late - line * level)
            if level < L_LEVELS:
                same = square is line and isinstance(late, int) and late == 0
                g_square = g if same else beginning(t - square * level)

                @pl.when(g_square >= 0)
                def _():
                    self.square_level(g_square, level)

            @pl.when(g >= 0)
            def _():
                self.line_level(g, level)

        for level in range(6):

            @pl.when(t == small_begin + level)
            def _():
                self.small_level(level)

    def all_sent(self, kind, rows):
        everything = self.grad.at[pl.ds(0, GROUPS * rows)]
        pltpu.make_async_remote_copy(
            src_ref=everything, dst_ref=everything, send_sem=self.send.at[KINDS.index(kind)],
            recv_sem=self.recv.at[0, 0], device_id=self.px, device_id_type=MESH).wait_send()

    def drain(self):
        for j, rows in ((0, QUARTER), (1, CHUNK)):
            everything = self.grad.at[pl.ds(0, GROUPS * rows)]
            pltpu.make_async_copy(everything, self.res.at[pl.ds(0, GROUPS * rows)], self.local.at[j]).wait()
        self.all_sent("ru", HALF)
        for kind in ("rv", "av", "au", "aw"):
            self.all_sent(kind, QUARTER)
        for kind in ("ex", "ey"):
            self.all_sent(kind, CHUNK)

        @pl.when(self.end)
        def _():
            self.all_sent("za", QUARTER)
            self.all_sent("ze", 3 * CHUNK)
            self.all_sent("ge", CHUNK)

        @pl.when(self.mid)
        def _():
            self.all_sent("zb", QUARTER)
            self.all_sent("zc", QUARTER)
            self.all_sent("zm", 2 * CHUNK)
            for kind in ("zo", "gn", "gd", "gf", "gp", "gq"):
                self.all_sent(kind, CHUNK)

        self.small_copy("sx").wait_send()
        self.small_copy("sy").wait_send()

        @pl.when(self.end)
        def _():
            self.small_copy("sa").wait_send()

        @pl.when(self.mid)
        def _():
            self.small_copy("sb").wait_send()
            self.small_copy("sc").wait_send()


def normed(value):
    mean = jnp.mean(value, axis=-1, keepdims=True)
    centred = value - mean
    spread = jnp.mean(centred * centred, axis=-1, keepdims=True)
    scale = lax.rsqrt(spread + EPS)
    return centred * scale, mean, scale, spread


def gelu(w):
    t = jnp.tanh(w * (2.0 * GELU_A + (8.0 * GELU_B) * (w * w)))
    return w + w * t


def gelu_slope(w):
    square = w * w
    t = jnp.tanh(w * (2.0 * GELU_A + (8.0 * GELU_B) * square))
    q = w * (GELU_A + (12.0 * GELU_B) * square)
    return (0.5 + q) + t * (0.5 - q * t)


def norm_gelu_back(grad, n, scale, gain, half_gain, half_shift):
    dv = grad * gelu_slope(n * half_gain + half_shift)
    terms = dv * n
    dn = dv * gain
    first = jnp.mean(dn, axis=-1, keepdims=True)
    second = jnp.mean(terms * gain, axis=-1, keepdims=True)
    return dv, terms, scale * (dn - first - n * second)


def fold(value):
    rows, width = value.shape
    return jnp.sum(value.reshape(rows // 8, 8, width), axis=0)


def nn(a, b):
    return jnp.dot(a, b, preferred_element_type=F32)


def nt(a, b):
    return lax.dot_general(a, b, (((1,), (1,)), ((), ())), preferred_element_type=F32)


def tn(a, b):
    return lax.dot_general(a, b, (((0,), (0,)), ((), ())), preferred_element_type=F32)


def blocks_kernel(
    names, with_sums, last,
    ends, lengths, outer_gain, inner_gains, outer_biases, inner_biases, down_hbm, conv_hbm, up_hbm,
    ends_out, res, small_out,
    down, conv, up, X, GY, HA, CW, HC, GCW, GP, NB, NC, ST, XS, handing, taps, lhs, oacc, iacc, grad, small,
    *rest,
):
    buffers = dict(zip(names, rest[: len(names)]))
    send, recv, local, small_send, small_recv, load, hand_send, hand_recv, halo_send, halo_recv, store = rest[len(names) :]
    micro, rows, width = X.shape
    inner = down.shape[1]
    section = lax.axis_index("section")
    dp = lax.axis_index("dp")
    z = lax.axis_index("seq")
    first = section == 0
    second = section == 1
    has_left = z > 0
    has_right = z < last
    across = (1 - section, dp, z)
    left = (section, dp, jnp.maximum(z - 1, 0))
    right = (section, dp, jnp.minimum(z + 1, last))
    sums = WeightSums(grad, res, small, buffers, send, recv, local, small_send, small_recv)

    def when(condition, act):
        pl.when(condition)(lambda: act() and None)

    def weight_load(j):
        return pltpu.make_async_copy((down_hbm, conv_hbm, up_hbm)[j], (down, conv, up)[j], load.at[micro + j])

    def end_load(mb, target):
        return pltpu.make_async_copy(ends.at[mb], target.at[mb], load.at[mb])

    @pl.when(first)
    def _():
        end_load(0, X).start()
        weight_load(0).start()

    barrier = pltpu.get_barrier_semaphore()

    def greet(to):
        pl.semaphore_signal(barrier, inc=1, device_id=to, device_id_type=MESH)

    greet(across)
    when(has_left, lambda: greet(left))
    when(has_right, lambda: greet(right))
    if with_sums:
        greet(sums.px)
        greet(sums.py)

    def met():
        peers = (3 if with_sums else 1) + has_left.astype(jnp.int32) + has_right.astype(jnp.int32)
        pl.semaphore_wait(barrier, peers)

    XS[...] = jnp.zeros_like(XS)
    oacc[...] = jnp.zeros_like(oacc)
    iacc[...] = jnp.zeros_like(iacc)
    edge = jnp.zeros((rows, inner), BF)
    for mb in range(micro):

        @pl.when(jnp.logical_not(has_left))
        def _():
            CW[mb, 0:rows, :] = edge
            GCW[mb, 0:rows, :] = edge

        @pl.when(jnp.logical_not(has_right))
        def _():
            CW[mb, 2 * rows : 3 * rows, :] = edge
            GCW[mb, 2 * rows : 3 * rows, :] = edge

    @pl.when(first)
    def _():
        end_load(0, X).wait()
        weight_load(0).wait()
        weight_load(1).start()
        weight_load(2).start()
        for mb in range(1, micro):
            end_load(mb, X).start()

    @pl.when(second)
    def _():
        for j in range(3):
            weight_load(j).start()
        for mb in range(micro):
            end_load(mb, GY).start()

    def halo_copies(ref, which, mb):
        def make(side, count):
            if side == 0:
                source, target, to = ref.at[mb, pl.ds(2 * rows - count, count)], ref.at[mb, pl.ds(rows - count, count)], right
            else:
                source, target, to = ref.at[mb, pl.ds(rows, count)], ref.at[mb, pl.ds(2 * rows, count)], left
            return pltpu.make_async_remote_copy(
                src_ref=source, dst_ref=target, send_sem=halo_send.at[which, mb, side],
                recv_sem=halo_recv.at[which, mb, side], device_id=to, device_id_type=MESH)

        return make

    def halo(ref, which, mb, act_right, act_left):
        make = halo_copies(ref, which, mb)
        for mine, count in ((first, EDGE), (second, rows)):

            @pl.when(mine)
            def _():
                when(act_right[0], lambda: act_right[1](make(0, count)))
                when(act_left[0], lambda: act_left[1](make(1, count)))

    def halo_start(ref, which, mb):
        go = lambda c: c.start()
        halo(ref, which, mb, (has_right, go), (has_left, go))

    def halo_arrived(ref, which, mb):
        go = lambda c: c.wait_recv()
        halo(ref, which, mb, (has_left, go), (has_right, go))

    def halo_sent(ref, which, mb):
        go = lambda c: c.wait_send()
        halo(ref, which, mb, (has_right, go), (has_left, go))

    def shifted(ref, mb, k, sign, target, at, column):
        shift = sign * (k - REACH)

        @pl.when(first)
        def _():
            target[at : at + rows, column : column + inner] = ref[mb, pl.ds(rows + shift * FIRST_DILATION, rows), :]

        @pl.when(second)
        def _():
            target[at : at + rows, column : column + inner] = ref[mb, pl.ds(rows + shift * SECOND_DILATION, rows), :]

    def all_shifted(ref, mb, sign):
        for mine, dilation in ((first, FIRST_DILATION), (second, SECOND_DILATION)):

            @pl.when(mine)
            def _():
                for k in range(FILTER_TAPS):
                    at = rows + sign * (k - REACH) * dilation
                    taps[:, k * inner : (k + 1) * inner] = ref[mb, pl.ds(at, rows), :]

    def hand_over(mb, target):
        slot = lax.rem(mb, 2)
        return pltpu.make_async_remote_copy(
            src_ref=handing.at[slot], dst_ref=target.at[mb], send_sem=hand_send.at[mb], recv_sem=hand_recv.at[mb],
            device_id=across, device_id_type=MESH)

    def store_end(mb):
        return pltpu.make_async_copy(handing.at[lax.rem(mb, 2)], ends_out.at[mb], store.at[mb])

    own = pl.ds(rows, rows)
    outer_shift, inner_shift_b, inner_shift_c = 0.5 * outer_biases[0:1, :], 0.5 * inner_biases[0:1, :], 0.5 * inner_biases[1:2, :]
    outer_half, inner_half_b, inner_half_c = 0.5 * outer_gain[...], 0.5 * inner_gains[0:1, :], 0.5 * inner_gains[1:2, :]

    def valid_of(mb):
        position = z * rows + lax.broadcasted_iota(jnp.int32, (rows, 1), 0)
        return (position < lengths[mb]).astype(F32)

    def forward_a(mb):
        when(jnp.logical_and(first, mb > 0), lambda: end_load(mb, X).wait())
        when(second, lambda: hand_over(mb, X).wait_recv())
        when(jnp.logical_and(second, mb == 0), lambda: weight_load(0).wait())
        n, mean, scale, spread = normed(X[mb].astype(F32))
        XS[...] += (spread + mean * mean) * valid_of(mb)
        ST[mb, :, 0:1] = mean
        ST[mb, :, 1:2] = scale
        hidden = gelu(n * outer_half + outer_shift).astype(BF)
        HA[mb] = hidden
        n, _, scale, _ = normed(nn(hidden, down[...]) + inner_biases[2:3, :])
        NB[mb] = n
        ST[mb, :, 2:3] = scale
        CW[mb, own, :] = (gelu(n * inner_half_b + inner_shift_b) * valid_of(mb)).astype(BF)
        when(jnp.logical_and(first, mb == 0), met)
        halo_start(CW, 0, mb)

    halves = [slice(h * (rows // 2), (h + 1) * (rows // 2)) for h in range(2)]

    def forward_b(mb):
        slot = lax.rem(mb, 2)
        halo_arrived(CW, 0, mb)

        @pl.when(mb == 0)
        def _():
            weight_load(1).wait()
            weight_load(2).wait()

        @pl.when(mb >= 2)
        def _():
            when(first, lambda: hand_over(mb - 2, X).wait_send())
            when(second, lambda: store_end(mb - 2).wait())

        all_shifted(CW, mb, 1)

        def norm_c(half, product):
            n, _, scale, _ = normed(product + inner_biases[3:4, :])
            NC[mb, half, :] = n
            ST[mb, half, 3:4] = scale
            hidden = (gelu(n * inner_half_c + inner_shift_c) * valid_of(mb)[half, :]).astype(BF)
            HC[mb, half, :] = hidden
            return hidden

        def close(half, product):
            branch = (product + outer_biases[1:2, :]) * valid_of(mb)[half, :]
            oacc[3] += fold(branch * branch)
            value = X[mb, half, :].astype(F32) + branch
            handing[slot, half, :] = value.astype(BF)

        lower = nn(taps[halves[0], :], conv[...])
        upper = nn(taps[halves[1], :], conv[...])
        hidden = norm_c(halves[0], lower)
        lower = nn(hidden, up[...])
        hidden = norm_c(halves[1], upper)
        upper = nn(hidden, up[...])
        close(halves[0], lower)
        close(halves[1], upper)
        when(first, lambda: hand_over(mb, X).start())
        when(second, lambda: store_end(mb).start())

    def backward_a(mb):
        when(jnp.logical_and(first, mb < micro - 1), lambda: hand_over(mb, GY).wait_recv())

        @pl.when(jnp.logical_and(second, mb == 0))
        def _():
            for k in range(micro):
                end_load(k, GY).wait()

        valid = valid_of(mb)
        oacc[2] += fold(GY[mb].astype(F32) * valid)
        dv, terms, dz = norm_gelu_back(
            nt(GY[mb], up[...]) * valid, NC[mb], ST[mb, :, 3:4], inner_gains[1:2, :], inner_half_c, inner_shift_c
        )
        iacc[3] += fold(terms)
        iacc[4] += fold(dv)
        iacc[5] += fold(dz)
        GCW[mb, own, :] = dz.astype(BF)
        halo_start(GCW, 1, mb)

    def backward_b(mb):
        halo_arrived(GCW, 1, mb)
        all_shifted(GCW, mb, -1)
        total = nt(taps[:, 0:inner], conv[0:inner, :])
        for k in range(1, FILTER_TAPS):
            total = total + nt(taps[:, k * inner : (k + 1) * inner], conv[k * inner : (k + 1) * inner, :])
        dv, terms, dz = norm_gelu_back(
            total * valid_of(mb), NB[mb], ST[mb, :, 2:3], inner_gains[0:1, :], inner_half_b, inner_shift_b
        )
        iacc[0] += fold(terms)
        iacc[1] += fold(dv)
        iacc[2] += fold(dz)
        GP[mb] = dz.astype(BF)

    def backward_c(mb):
        slot = lax.rem(mb, 2)

        @pl.when(mb < 2)
        def _():
            when(first, lambda: hand_over(mb + micro - 2, X).wait_send())
            when(second, lambda: store_end(mb + micro - 2).wait())

        @pl.when(mb >= 2)
        def _():
            when(second, lambda: hand_over(mb - 2, GY).wait_send())
            when(first, lambda: store_end(mb - 2).wait())

        scale = ST[mb, :, 1:2]
        n = (X[mb].astype(F32) - ST[mb, :, 0:1]) * scale
        dv, terms, dz = norm_gelu_back(nt(GP[mb], down[...]), n, scale, outer_gain[...], outer_half, outer_shift)
        oacc[0] += fold(terms)
        oacc[1] += fold(dv)
        value = GY[mb].astype(F32) + dz
        handing[slot] = value.astype(BF)
        when(second, lambda: hand_over(mb, GY).start())
        when(first, lambda: store_end(mb).start())

    def weight_up():
        when(first, lambda: hand_over(micro - 1, GY).wait_recv())
        total = tn(HC[...].reshape(micro * rows, inner), GY[...].reshape(micro * rows, width)).astype(BF)
        for h in range(UP_BLOCKS):
            grad[h * BLOCK : (h + 1) * BLOCK, :] = total[:, h * inner : (h + 1) * inner]

    def weight_tap(tap):
        for k in range(FILTER_TAPS):

            @pl.when(tap == k)
            def _():
                for mb in range(micro):
                    shifted(CW, mb, k, 1, lhs, mb * rows, 0)

        y = GCW[:, own, :].reshape(micro * rows, inner)
        at = pl.multiple_of((UP_BLOCKS + tap) * BLOCK, BLOCK)
        grad[pl.ds(at, BLOCK), :] = tn(lhs[...], y).astype(BF)

    def weight_down():
        y = GP[...].reshape(micro * rows, inner)
        for h in range(BLOCKS - DOWN_AT):
            at = (DOWN_AT + h) * BLOCK
            a = HA[:, :, h * inner : (h + 1) * inner].reshape(micro * rows, inner)
            grad[at : at + BLOCK, :] = tn(a, y).astype(BF)

    def row(value):
        return jnp.sum(value, axis=0, keepdims=True)

    def smalls():
        place = 0

        def put(value):
            nonlocal place
            for at in range(0, value.shape[1], inner):
                small[0, place : place + 1, :] = value[:, at : at + inner]
                place += 1

        small[0] = jnp.zeros_like(small[0])
        for ref, j in ((oacc, 0), (iacc, 0), (iacc, 3), (oacc, 1), (oacc, 2), (iacc, 1), (iacc, 4), (iacc, 2), (iacc, 5)):
            put(row(ref[j]))
        lane = lax.broadcasted_iota(jnp.int32, (1, inner), 1)
        put(jnp.where(lane == 0, row(XS[...]) * width, 0.0))
        value = row(oacc[3])
        put(value[:, :inner] + value[:, inner:])
        count = jnp.float32(0)
        for mb in range(micro):
            count += jnp.clip(lengths[mb] - z * rows, 0, rows).astype(F32)
        put(jnp.zeros((1, inner), F32) + count)

    when(second, met)
    plans = [[(p * 8 + k) * 8 + steps for p, k, steps in plan] for plan in (FIRST_PLAN, SECOND_PLAN)]
    def mine(a, b):
        return a if a == b else jnp.where(first, a, b)

    begins = [mine(a, b) for a, b in zip(begins_of(FIRST_PLAN, FIRST_PACE), begins_of(SECOND_PLAN, SECOND_PACE))]
    square, line, late = (mine(a, b) for a, b in zip(FIRST_PACE[:3], SECOND_PACE[:3]))
    same = FIRST_PACE[0] == FIRST_PACE[1] and SECOND_PACE[0] == SECOND_PACE[1]
    pace = (line if same else square, line, late)
    planned = mine(planned_steps(FIRST_PLAN), planned_steps(SECOND_PLAN))
    ticks = mine(steps_of(FIRST_PLAN, FIRST_PACE), steps_of(SECOND_PLAN, SECOND_PACE))

    def tick(t, carry):
        sums.tick(t, begins, pace, planned)
        return carry

    def step(i, t):
        entry = jnp.int32(0)
        for j, (a, b) in enumerate(zip(*plans)):
            entry = jnp.where(i == j, jnp.where(first, a, b), entry)
        what, k = entry // 64, lax.rem(entry // 8, 8)
        for p, act in ((FA, forward_a), (FB, forward_b), (BA, backward_a), (BB, backward_b), (BC, backward_c), (WC, weight_tap)):
            when(what == p, functools.partial(act, k))
        when(what == WU, weight_up)
        when(what == WD, weight_down)
        then = t + lax.rem(entry, 8)
        if with_sums:
            lax.fori_loop(t, then, tick, 0)
        return then

    t = lax.fori_loop(0, len(FIRST_PLAN), step, jnp.int32(0))
    smalls()

    if with_sums:
        lax.fori_loop(t, ticks, tick, 0)
        sums.drain()
        done = pltpu.make_async_copy(small.at[4], small_out, load.at[0])
        done.start()
        done.wait()
    else:
        done = pltpu.make_async_copy(small.at[0], small_out, load.at[0])
        done.start()
        done.wait()
        done = pltpu.make_async_copy(grad, res, load.at[1])
        done.start()
        done.wait()
    for mb in range(micro):
        if mb >= micro - 2:
            when(first, functools.partial(lambda m: store_end(m).wait(), mb))
            when(second, functools.partial(lambda m: hand_over(m, GY).wait_send(), mb))
        halo_sent(CW, 0, mb)
        halo_sent(GCW, 1, mb)


def run_blocks(mesh_shape, ends, lengths, outer_gain, inner_gains, outer_biases, inner_biases, down, conv, up):
    micro, rows, width = ends.shape
    inner = down.shape[1]
    taps = FILTER_TAPS
    with_sums = (mesh_shape["dp"], mesh_shape["seq"]) == (4, 4)
    buffers = {k: pltpu.VMEM((GROUPS, n, BLOCK), BF) for k, n in RECEIVE.items()} if with_sums else {}
    names = tuple(buffers)
    total = BLOCKS * BLOCK
    anywhere = pl.BlockSpec(memory_space=pl.ANY)
    vmem = pl.BlockSpec(memory_space=pltpu.VMEM)
    dma = pltpu.SemaphoreType.DMA
    scratch = [
        pltpu.VMEM(down.shape, BF),
        pltpu.VMEM(conv.shape, BF),
        pltpu.VMEM(up.shape, BF),
        pltpu.VMEM((micro, rows, width), BF),
        pltpu.VMEM((micro, rows, width), BF),
        pltpu.VMEM((micro, rows, width), BF),
        pltpu.VMEM((micro, 3 * rows, inner), BF),
        pltpu.VMEM((micro, rows, inner), BF),
        pltpu.VMEM((micro, 3 * rows, inner), BF),
        pltpu.VMEM((micro, rows, inner), BF),
        pltpu.VMEM((micro, rows, inner), F32),
        pltpu.VMEM((micro, rows, inner), F32),
        pltpu.VMEM((micro, rows, 128), F32),
        pltpu.VMEM((rows, 1), F32),
        pltpu.VMEM((2, rows, width), BF),
        pltpu.VMEM((rows, taps * inner), BF),
        pltpu.VMEM((micro * rows, inner), BF),
        pltpu.VMEM((4, 8, width), F32),
        pltpu.VMEM((6, 8, inner), F32),
        pltpu.VMEM((total, BLOCK), BF),
        pltpu.VMEM((9, 16, inner), F32),
        *[buffers[k] for k in names],
        dma((len(KINDS),)),
        dma((GROUPS, max(ARRIVES.values()) + 1)),
        dma((2,)),
        dma((len(SMALL_KINDS),)),
        dma((len(SMALL_KINDS),)),
        dma((micro + 3,)),
        dma((micro,)),
        dma((micro,)),
        dma((2, micro, 2)),
        dma((2, micro, 2)),
        dma((micro,)),
    ]
    flops = 2 * 3 * micro * rows * (2 * width * inner + taps * inner * inner)
    return pl.pallas_call(
        functools.partial(blocks_kernel, names, with_sums, mesh_shape["seq"] - 1),
        name="two_blocks",
        out_shape=(
            jax.ShapeDtypeStruct((micro, rows, width), BF),
            jax.ShapeDtypeStruct((total, BLOCK), BF),
            jax.ShapeDtypeStruct((16, inner), F32),
        ),
        in_specs=[anywhere, pl.BlockSpec(memory_space=pltpu.SMEM), vmem, vmem, vmem, vmem, anywhere, anywhere, anywhere],
        out_specs=[anywhere] * 3,
        scratch_shapes=scratch,
        cost_estimate=pl.CostEstimate(flops=flops, bytes_accessed=40 * 2**20, transcendentals=0),
        compiler_params=pltpu.CompilerParams(collective_id=1, has_side_effects=True, vmem_limit_bytes=62 * 2**20),
    )(ends, lengths, outer_gain, inner_gains, outer_biases, inner_biases, down, conv, up)


AHEAD = 6


def finish_kernel(
    ends, rows, small, ends_out, outer_gain, inner_gains, outer_biases, inner_biases, down, conv, up, rms,
    raw, full, held, wide, load, store,
):
    micro, width = ends.shape[0], ends.shape[2]
    places = [up.at[0, :, pl.ds(h * BLOCK, BLOCK)] for h in range(UP_BLOCKS)]
    places += [conv.at[0, k] for k in range(FILTER_TAPS)]
    places += [down.at[0, pl.ds(h * BLOCK, BLOCK)] for h in range(BLOCKS - DOWN_AT)]
    moves = [(rows.at[pl.ds(g * BLOCK, BLOCK)], raw.at[g], full.at[g], places[g]) for g in range(BLOCKS)]
    moves += [(ends.at[mb], held.at[mb], wide.at[mb], ends_out.at[0, mb, 0]) for mb in range(micro)]
    loads = [pltpu.make_async_copy(m[0], m[1], load.at[i]) for i, m in enumerate(moves)]
    stores = [pltpu.make_async_copy(m[2], m[3], store.at[i]) for i, m in enumerate(moves)]
    for copy in loads[:AHEAD]:
        copy.start()
    outer_gain[0:1, 0:BLOCK] = small[0:1, :]
    outer_gain[0:1, BLOCK:] = small[1:2, :]
    inner_gains[0] = small[2:4, :]
    for j in range(2):
        outer_biases[0, j : j + 1, 0:BLOCK] = small[4 + 2 * j : 5 + 2 * j, :]
        outer_biases[0, j : j + 1, BLOCK:] = small[5 + 2 * j : 6 + 2 * j, :]
    inner_biases[0] = small[8:12, :]
    squares = jnp.sum(small[12:14, :], axis=1, keepdims=True)
    roots = jnp.sqrt(squares / (small[14:15, 0:1] * width))
    rms[0:1, 0:1] = roots[0:1, :]
    rms[0:1, 1:2] = roots[1:2, :]
    for i, (_, source, target, _) in enumerate(moves):
        loads[i].wait()
        if i + AHEAD < len(moves):
            loads[i + AHEAD].start()
        target[...] = source[...].astype(F32)
        stores[i].start()
    for copy in stores:
        copy.wait()


def finish(shapes, ends, rows, small):
    anywhere = pl.BlockSpec(memory_space=pl.ANY)
    vmem = pl.BlockSpec(memory_space=pltpu.VMEM)
    dma = pltpu.SemaphoreType.DMA
    return pl.pallas_call(
        finish_kernel,
        name="outputs",
        out_shape=tuple(jax.ShapeDtypeStruct(shape, F32) for shape in shapes),
        in_specs=[anywhere, anywhere, vmem],
        out_specs=[anywhere, vmem, vmem, vmem, vmem, anywhere, anywhere, anywhere, vmem],
        scratch_shapes=[
            pltpu.VMEM((BLOCKS, BLOCK, BLOCK), BF),
            pltpu.VMEM((BLOCKS, BLOCK, BLOCK), F32),
            pltpu.VMEM(ends.shape, BF),
            pltpu.VMEM(ends.shape, F32),
            dma((BLOCKS + ends.shape[0],)),
            dma((BLOCKS + ends.shape[0],)),
        ],
        compiler_params=pltpu.CompilerParams(vmem_limit_bytes=60 * 2**20),
    )(ends, rows, small)


def body(
    mesh_shape, ends_in, lengths, outer_gain, inner_gains, outer_biases, inner_biases, down_in, conv_weight, up_out
):
    width = ends_in.shape[-1]
    ends, rows, small = run_blocks(
        mesh_shape, ends_in.reshape(ends_in.shape[1], -1, width), lengths.reshape(-1), outer_gain, inner_gains[0],
        outer_biases[0], inner_biases[0], down_in[0], conv_weight[0].reshape(-1, conv_weight.shape[-1]), up_out[0],
    )
    if (mesh_shape["dp"], mesh_shape["seq"]) == (4, 4):
        weights = (outer_gain, inner_gains, outer_biases, inner_biases, down_in, conv_weight, up_out)
        return finish((ends_in.shape, *(w.shape for w in weights), (1, 2)), ends, rows, small)
    rows, small = lax.psum((rows.astype(F32), small), ("dp", "seq"))
    up = jnp.concatenate([rows[:BLOCK], rows[BLOCK : 2 * BLOCK]], axis=1)
    conv = rows[UP_BLOCKS * BLOCK : DOWN_AT * BLOCK].reshape(conv_weight.shape[1:])
    down = rows[DOWN_AT * BLOCK :]
    rms = jnp.sqrt(jnp.sum(small[12:14], axis=1) / (small[14, 0] * width))
    return (
        ends.astype(F32).reshape(ends_in.shape),
        small[0:2].reshape(1, -1),
        small[None, 2:4],
        small[4:8].reshape(1, 2, -1),
        small[None, 8:12],
        down[None],
        conv[None],
        up[None],
        rms[None],
    )


def solution(mesh):
    in_specs = (
        P("section", None, "dp", "seq", None),
        P(None, "dp"),
        P("section", None),
        P("section", None, None),
        P("section", None, None),
        P("section", None, None),
        P("section", None, None),
        P("section", None, None, None),
        P("section", None, None),
    )
    out_specs = (
        P("section", None, "dp", "seq", None),
        P("section", None),
        P("section", None, None),
        P("section", None, None),
        P("section", None, None),
        P("section", None, None),
        P("section", None, None, None),
        P("section", None, None),
        P("section", None),
    )
    return jax.shard_map(
        functools.partial(body, dict(mesh.shape)), mesh=mesh, in_specs=in_specs, out_specs=out_specs, check_vma=False
    )
```

```python
import functools
import math

import jax
import jax.numpy as jnp
from jax import lax
from jax.experimental import pallas as pl
from jax.experimental.pallas import tpu as pltpu
from jax.sharding import PartitionSpec as P

MESH = pl.DeviceIdType.MESH
BF = jnp.bfloat16
F32 = jnp.float32
FILTER_TAPS = 5
FIRST_DILATION = 2
SECOND_DILATION = 128
REACH = FILTER_TAPS // 2
EPS = 1e-05
GELU_A = math.sqrt(2.0 / math.pi)
GELU_B = GELU_A * 0.044715
EDGE = 16

BLOCK = 640
UP_BLOCKS = 2
DOWN_AT = UP_BLOCKS + FILTER_TAPS
BLOCKS = DOWN_AT + 2
GROUPS = 10
ROWS = BLOCKS * BLOCK // GROUPS
LROWS = 384
HALF = LROWS // 2
QUARTER = LROWS // 4
CHUNK = (ROWS - LROWS) // 4
KINDS = (
    "ru", "rv", "za", "zb", "zc", "av", "au", "aw",
    "ze", "zm", "zo", "ex", "ey", "ge", "gn", "gd", "gf", "gp", "gq",
)
ARRIVES = dict(ru=0, rv=1, av=2, au=3, aw=4, ex=5, ey=6, za=7, zb=8, ze=9, zm=10, ge=11, gn=12, gf=13,
               zc=7, zo=8, gd=9, gp=10, gq=11)
SMALL_KINDS = ("sx", "sy", "sa", "sb", "sc")
RECEIVE = dict(ru=HALF, rv=QUARTER, za=QUARTER, zb=QUARTER, fl=QUARTER, ze=3 * CHUNK, zm=2 * CHUNK,
               zo=CHUNK, ex=CHUNK, ey=CHUNK, tx=CHUNK, fz=CHUNK)
L_LEVELS = 8
Z_LEVELS = 9
FIRST_PACE = (2, 2, 0, 1)
SECOND_PACE = (2, 2, 0, 1)

FA, FB, WU, BA, BB, BC, WC, WD = range(1, 9)
FIRST_PLAN = (
    (FA, 0, 0), (FA, 1, 0), (FB, 0, 0), (FA, 2, 0), (FB, 1, 0), (FA, 3, 0), (FB, 2, 0), (FB, 3, 0), (BA, 0, 0), (BA, 1, 0), (BB, 0, 0), (BC, 0, 0), (BA, 2, 0), (BB, 1, 0), (BC, 1, 0), (BB, 2, 0), (WU, 0, 0), (BA, 3, 1), (BC, 2, 3), (BB, 3, 0), (BC, 3, 1), (WC, 0, 0), (WC, 1, 0), (WC, 2, 3), (WC, 3, 2), (WC, 4, 1), (WD, 0, 0),
)
SECOND_PLAN = (
    (FA, 0, 0), (FA, 1, 0), (FB, 0, 0), (FA, 2, 0), (FB, 1, 0), (FA, 3, 0), (FB, 2, 0), (BA, 0, 0), (FB, 3, 0), (WU, 0, 1), (BA, 1, 0), (BB, 0, 0), (BC, 0, 1), (BA, 2, 1), (BB, 1, 0), (BC, 1, 1), (BA, 3, 1), (BB, 2, 0), (BC, 2, 1), (WC, 0, 1), (WC, 1, 0), (BB, 3, 1), (WC, 2, 1), (BC, 3, 0), (WC, 3, 1), (WC, 4, 1), (WD, 0, 1),
)


def begins_of(plan, pace):
    ready, steps = {}, 0
    for what, k, count in plan:
        for block in {WU: range(UP_BLOCKS), WC: (UP_BLOCKS + k,), WD: range(DOWN_AT, BLOCKS)}.get(what, ()):
            ready[block] = steps
        steps += count
    begins = []
    for g in range(GROUPS):
        there = max(ready[block] for block in range(g * ROWS // BLOCK, ((g + 1) * ROWS - 1) // BLOCK + 1))
        begins.append(max(there, begins[-1] + pace[3]) if begins else there)
    return begins


def planned_steps(plan):
    return sum(entry[2] for entry in plan)


def steps_of(plan, pace):
    square, line, late, _ = pace
    last = begins_of(plan, pace)[-1] + max(square * (L_LEVELS - 1), late + line * (Z_LEVELS - 1))
    return max(last + 1, planned_steps(plan) + 6)


def aligned(offset):
    return offset if isinstance(offset, int) else pl.multiple_of(offset, 16)


def part(ref, offset, rows):
    return ref.at[pl.ds(aligned(offset), rows)]


def added(target, offset, sources, rows, tile=16):
    for start in range(0, rows, tile):
        total = None
        for ref, at in sources:
            value = ref[pl.ds(aligned(at + start), tile), :]
            if len(sources) > 2:
                value = value.astype(F32)
            total = value if total is None else total + value
        target[pl.ds(aligned(offset + start), tile), :] = total.astype(BF)


class WeightSums:
    def __init__(self, grad, res, small, buffers, send, recv, local, small_send, small_recv):
        self.grad, self.res, self.small, self.r = grad, res, small, buffers
        self.send, self.recv, self.local = send, recv, local
        self.small_send, self.small_recv = small_send, small_recv
        self.c = lax.axis_index("section")
        self.dp = lax.axis_index("dp")
        self.z = lax.axis_index("seq")
        self.x = lax.rem(self.dp, 2)
        self.y = self.dp // 2
        z = self.z
        self.upper = z // 2
        self.end = jnp.logical_or(z == 0, z == 3)
        self.mid = jnp.logical_not(self.end)
        self.dp_x = self.dp + 1 - 2 * self.x
        self.dp_y = lax.rem(self.dp + 2, 4)
        self.px = (self.c, self.dp_x, z)
        self.py = (self.c, self.dp_y, z)
        self.pair = (self.c, self.dp, 1 - z + 4 * self.upper)
        self.other = (self.c, self.dp, jnp.clip(3 - z, 1, 2))

    def copy(self, kind, g, source, target, to):
        j = KINDS.index(kind)
        return pltpu.make_async_remote_copy(
            src_ref=source, dst_ref=target, send_sem=self.send.at[j], recv_sem=self.recv.at[g, ARRIVES[kind]],
            device_id=to, device_id_type=MESH)

    def square(self, g):
        odd = lax.rem(g, 2)
        u = jnp.where(odd == 0, self.x, self.y)
        v = jnp.where(odd == 0, self.y, self.x)
        to_u = (self.c, jnp.where(odd == 0, self.dp_x, self.dp_y), self.z)
        to_v = (self.c, jnp.where(odd == 0, self.dp_y, self.dp_x), self.z)
        base = g * ROWS
        own_half = base + u * HALF
        own = own_half + v * QUARTER
        beside = own_half + (1 - v) * QUARTER
        return base, u, v, to_u, to_v, own, beside

    def square_copy(self, kind, g):
        base, u, v, to_u, to_v, own, beside = self.square(g)
        grad, res, r = self.grad, self.res, self.r
        final = r["fl"].at[g]
        if kind == "ru":
            return self.copy(kind, g, part(grad, base + (1 - u) * HALF, HALF), r["ru"].at[g], to_u)
        if kind == "rv":
            return self.copy(kind, g, part(grad, beside, QUARTER), r["rv"].at[g], to_v)
        if kind == "za":
            return self.copy(kind, g, part(grad, own, QUARTER), r["za"].at[g], self.pair)
        if kind == "zb":
            return self.copy(kind, g, part(grad, own, QUARTER), r["zb"].at[g], self.other)
        if kind == "zc":
            return self.copy(kind, g, final, final, self.pair)
        if kind == "av":
            return self.copy(kind, g, final, part(res, own, QUARTER), to_v)
        if kind == "au":
            return self.copy(kind, g, final, part(res, own, QUARTER), to_u)
        if kind == "aw":
            return self.copy(kind, g, part(res, beside, QUARTER), part(res, beside, QUARTER), to_u)
        return pltpu.make_async_copy(final, part(res, own, QUARTER), self.local.at[0])

    def square_level(self, g, level):
        base, u, v, to_u, to_v, own, beside = self.square(g)
        grad, r = self.grad, self.r
        copy = functools.partial(self.square_copy, g=g)
        if level == 0:
            copy("ru").start()
        elif level == 1:
            copy("ru").wait_recv()
            added(grad, beside, [(grad, beside), (r["ru"].at[g], (1 - v) * QUARTER)], QUARTER)
            copy("rv").start()
            added(grad, own, [(grad, own), (r["ru"].at[g], v * QUARTER)], QUARTER)
        elif level == 2:
            copy("rv").wait_recv()
            added(grad, own, [(grad, own), (r["rv"].at[g], 0)], QUARTER)

            @pl.when(self.end)
            def _():
                copy("za").start()
        elif level == 3:

            @pl.when(self.mid)
            def _():
                copy("za").wait_recv()
                added(grad, own, [(grad, own), (r["za"].at[g], 0)], QUARTER)
                copy("zb").start()
        elif level == 4:

            @pl.when(self.mid)
            def _():
                copy("zb").wait_recv()
                added(r["fl"].at[g], 0, [(grad, own), (r["zb"].at[g], 0)], QUARTER)
                copy("zc").start()
                copy("av").start()
                copy("au").start()
                copy("fl").start()
        elif level == 5:

            @pl.when(self.end)
            def _():
                copy("zc").wait_recv()
                copy("av").start()
                copy("au").start()
                copy("fl").start()
        elif level == 6:
            copy("av").wait_recv()
            copy("aw").start()
        elif level == 7:
            copy("au").wait_recv()
            copy("aw").wait_recv()

    def line(self, g):
        base = g * ROWS + LROWS
        upper = self.upper
        three = base + CHUNK * (1 - upper)
        far = base + 2 * CHUNK * (1 - upper)
        near = base + 2 * CHUNK * upper
        outer = base + 3 * CHUNK * upper
        own = base + CHUNK * self.z
        return three, far, near, outer, own

    def line_copy(self, kind, g):
        three, far, near, outer, own = self.line(g)
        grad, res, r = self.grad, self.res, self.r
        base = g * ROWS + LROWS
        final = r["fz"].at[g]
        here = part(res, own, CHUNK)
        if kind == "ze":
            return self.copy(kind, g, part(grad, three, 3 * CHUNK), r["ze"].at[g], self.pair)
        if kind == "zm":
            return self.copy(kind, g, part(grad, far, 2 * CHUNK), r["zm"].at[g], self.other)
        if kind == "zo":
            return self.copy(kind, g, part(grad, outer, CHUNK), r["zo"].at[g], self.pair)
        if kind == "ex":
            return self.copy(kind, g, part(grad, own, CHUNK), r["ex"].at[g], self.px)
        if kind == "ey":
            return self.copy(kind, g, r["tx"].at[g], r["ey"].at[g], self.py)
        if kind in ("ge", "gd"):
            return self.copy(kind, g, final, here, self.pair)
        if kind == "gn":
            return self.copy(kind, g, final, here, self.other)
        if kind == "gf":
            rows = part(res, outer, CHUNK)
            return self.copy(kind, g, rows, rows, self.other)
        if kind == "gp":
            rows = part(res, base + CHUNK * (3 - self.z), CHUNK)
            return self.copy(kind, g, rows, rows, self.pair)
        if kind == "gq":
            rows = part(res, base + 3 * CHUNK * (1 - self.upper), CHUNK)
            return self.copy(kind, g, rows, rows, self.pair)
        return pltpu.make_async_copy(final, here, self.local.at[1])

    def line_level(self, g, level):
        three, far, near, outer, own = self.line(g)
        grad, r = self.grad, self.r
        copy = functools.partial(self.line_copy, g=g)
        if level == 0:

            @pl.when(self.end)
            def _():
                copy("ze").start()
        elif level == 1:

            @pl.when(self.mid)
            def _():
                copy("ze").wait_recv()
                added(grad, far, [(grad, far), (r["ze"].at[g], far - three)], 2 * CHUNK)
                copy("zm").start()
        elif level == 2:

            @pl.when(self.mid)
            def _():
                copy("zm").wait_recv()
                added(grad, outer, [(grad, outer), (r["zm"].at[g], outer - near)], CHUNK)
                copy("zo").start()
                added(grad, own, [(grad, own), (r["ze"].at[g], own - three), (r["zm"].at[g], own - near)], CHUNK)
                copy("ex").start()
        elif level == 3:

            @pl.when(self.end)
            def _():
                copy("zo").wait_recv()
                added(grad, own, [(grad, own), (r["zo"].at[g], 0)], CHUNK)
                copy("ex").start()
        elif level == 4:
            copy("ex").wait_recv()
            added(r["tx"].at[g], 0, [(grad, own), (r["ex"].at[g], 0)], CHUNK)
            copy("ey").start()
        elif level == 5:
            copy("ey").wait_recv()
            added(r["fz"].at[g], 0, [(r["tx"].at[g], 0), (r["ey"].at[g], 0)], CHUNK)
            copy("fz").start()

            @pl.when(self.end)
            def _():
                copy("ge").start()

            @pl.when(self.mid)
            def _():
                copy("gn").start()
                copy("gd").start()
        elif level == 6:

            @pl.when(self.mid)
            def _():
                copy("ge").wait_recv()
                copy("gf").start()
                copy("gn").wait_recv()
                copy("gp").start()
        elif level == 7:

            @pl.when(self.mid)
            def _():
                copy("gf").wait_recv()
                copy("gq").start()
        elif level == 8:

            @pl.when(self.end)
            def _():
                copy("gd").wait_recv()
                copy("gp").wait_recv()
                copy("gq").wait_recv()

    def small_copy(self, kind):
        j = SMALL_KINDS.index(kind)
        s = self.small
        source, target, to = dict(
            sx=(s.at[0], s.at[5], self.px),
            sy=(s.at[1], s.at[6], self.py),
            sa=(s.at[2], s.at[7], self.pair),
            sb=(s.at[3], s.at[8], self.other),
            sc=(s.at[4], s.at[4], self.pair),
        )[kind]
        return pltpu.make_async_remote_copy(
            src_ref=source, dst_ref=target, send_sem=self.small_send.at[j], recv_sem=self.small_recv.at[j],
            device_id=to, device_id_type=MESH)

    def small_level(self, level):
        copy, s = self.small_copy, self.small
        if level == 0:
            copy("sx").start()
        elif level == 1:
            copy("sx").wait_recv()
            s[1] = s[0] + s[5]
            copy("sy").start()
        elif level == 2:
            copy("sy").wait_recv()
            s[2] = s[1] + s[6]

            @pl.when(self.end)
            def _():
                copy("sa").start()
        elif level == 3:

            @pl.when(self.mid)
            def _():
                copy("sa").wait_recv()
                s[3] = s[2] + s[7]
                copy("sb").start()
        elif level == 4:

            @pl.when(self.mid)
            def _():
                copy("sb").wait_recv()
                s[4] = s[3] + s[8]
                copy("sc").start()
        elif level == 5:

            @pl.when(self.end)
            def _():
                copy("sc").wait_recv()

    def tick(self, t, begins, pace, small_begin):
        square, line, late = pace

        def beginning(step):
            g = jnp.int32(-1)
            for j, begin in enumerate(begins):
                g = jnp.where(step == begin, j, g)
            return g

        for level in reversed(range(Z_LEVELS)):
            g = beginning(t - late - line * level)
            if level < L_LEVELS:
                same = square is line and isinstance(late, int) and late == 0
                g_square = g if same else beginning(t - square * level)

                @pl.when(g_square >= 0)
                def _():
                    self.square_level(g_square, level)

            @pl.when(g >= 0)
            def _():
                self.line_level(g, level)

        for level in range(6):

            @pl.when(t == small_begin + level)
            def _():
                self.small_level(level)

    def all_sent(self, kind, rows):
        everything = self.grad.at[pl.ds(0, GROUPS * rows)]
        pltpu.make_async_remote_copy(
            src_ref=everything, dst_ref=everything, send_sem=self.send.at[KINDS.index(kind)],
            recv_sem=self.recv.at[0, 0], device_id=self.px, device_id_type=MESH).wait_send()

    def drain(self):
        for j, rows in ((0, QUARTER), (1, CHUNK)):
            everything = self.grad.at[pl.ds(0, GROUPS * rows)]
            pltpu.make_async_copy(everything, self.res.at[pl.ds(0, GROUPS * rows)], self.local.at[j]).wait()
        self.all_sent("ru", HALF)
        for kind in ("rv", "av", "au", "aw"):
            self.all_sent(kind, QUARTER)
        for kind in ("ex", "ey"):
            self.all_sent(kind, CHUNK)

        @pl.when(self.end)
        def _():
            self.all_sent("za", QUARTER)
            self.all_sent("ze", 3 * CHUNK)
            self.all_sent("ge", CHUNK)

        @pl.when(self.mid)
        def _():
            self.all_sent("zb", QUARTER)
            self.all_sent("zc", QUARTER)
            self.all_sent("zm", 2 * CHUNK)
            for kind in ("zo", "gn", "gd", "gf", "gp", "gq"):
                self.all_sent(kind, CHUNK)

        self.small_copy("sx").wait_send()
        self.small_copy("sy").wait_send()

        @pl.when(self.end)
        def _():
            self.small_copy("sa").wait_send()

        @pl.when(self.mid)
        def _():
            self.small_copy("sb").wait_send()
            self.small_copy("sc").wait_send()


def normed(value):
    mean = jnp.mean(value, axis=-1, keepdims=True)
    centred = value - mean
    spread = jnp.mean(centred * centred, axis=-1, keepdims=True)
    scale = lax.rsqrt(spread + EPS)
    return centred * scale, mean, scale, spread


def gelu(w):
    t = jnp.tanh(w * (2.0 * GELU_A + (8.0 * GELU_B) * (w * w)))
    return w + w * t


def gelu_slope(w):
    square = w * w
    t = jnp.tanh(w * (2.0 * GELU_A + (8.0 * GELU_B) * square))
    q = w * (GELU_A + (12.0 * GELU_B) * square)
    return (0.5 + q) + t * (0.5 - q * t)


def norm_gelu_back(grad, n, scale, gain, half_gain, half_shift):
    dv = grad * gelu_slope(n * half_gain + half_shift)
    terms = dv * n
    dn = dv * gain
    first = jnp.mean(dn, axis=-1, keepdims=True)
    second = jnp.mean(terms * gain, axis=-1, keepdims=True)
    return dv, terms, scale * (dn - first - n * second)


def fold(value):
    rows, width = value.shape
    return jnp.sum(value.reshape(rows // 8, 8, width), axis=0)


def nn(a, b):
    return jnp.dot(a, b, preferred_element_type=F32)


def nt(a, b):
    return lax.dot_general(a, b, (((1,), (1,)), ((), ())), preferred_element_type=F32)


def tn(a, b):
    return lax.dot_general(a, b, (((0,), (0,)), ((), ())), preferred_element_type=F32)


def blocks_kernel(
    names, with_sums, last,
    ends, lengths, outer_gain, inner_gains, outer_biases, inner_biases, down_hbm, conv_hbm, up_hbm,
    ends_out, res, small_out,
    down, conv, up, X, GY, HA, CW, HC, GCW, GP, NB, NC, ST, XS, handing, taps, lhs, oacc, iacc, grad, small,
    *rest,
):
    buffers = dict(zip(names, rest[: len(names)]))
    send, recv, local, small_send, small_recv, load, hand_send, hand_recv, halo_send, halo_recv, store = rest[len(names) :]
    micro, rows, width = X.shape
    inner = down.shape[1]
    section = lax.axis_index("section")
    dp = lax.axis_index("dp")
    z = lax.axis_index("seq")
    first = section == 0
    second = section == 1
    has_left = z > 0
    has_right = z < last
    across = (1 - section, dp, z)
    left = (section, dp, jnp.maximum(z - 1, 0))
    right = (section, dp, jnp.minimum(z + 1, last))
    sums = WeightSums(grad, res, small, buffers, send, recv, local, small_send, small_recv)

    def when(condition, act):
        pl.when(condition)(lambda: act() and None)

    def weight_load(j):
        return pltpu.make_async_copy((down_hbm, conv_hbm, up_hbm)[j], (down, conv, up)[j], load.at[micro + j])

    def end_load(mb, target):
        return pltpu.make_async_copy(ends.at[mb], target.at[mb], load.at[mb])

    @pl.when(first)
    def _():
        end_load(0, X).start()
        weight_load(0).start()

    barrier = pltpu.get_barrier_semaphore()

    def greet(to):
        pl.semaphore_signal(barrier, inc=1, device_id=to, device_id_type=MESH)

    greet(across)
    when(has_left, lambda: greet(left))
    when(has_right, lambda: greet(right))
    if with_sums:
        greet(sums.px)
        greet(sums.py)

    def met():
        peers = (3 if with_sums else 1) + has_left.astype(jnp.int32) + has_right.astype(jnp.int32)
        pl.semaphore_wait(barrier, peers)

    XS[...] = jnp.zeros_like(XS)
    oacc[...] = jnp.zeros_like(oacc)
    iacc[...] = jnp.zeros_like(iacc)
    edge = jnp.zeros((rows, inner), BF)
    for mb in range(micro):

        @pl.when(jnp.logical_not(has_left))
        def _():
            CW[mb, 0:rows, :] = edge
            GCW[mb, 0:rows, :] = edge

        @pl.when(jnp.logical_not(has_right))
        def _():
            CW[mb, 2 * rows : 3 * rows, :] = edge
            GCW[mb, 2 * rows : 3 * rows, :] = edge

    @pl.when(first)
    def _():
        end_load(0, X).wait()
        weight_load(0).wait()
        weight_load(1).start()
        weight_load(2).start()
        for mb in range(1, micro):
            end_load(mb, X).start()

    @pl.when(second)
    def _():
        for j in range(3):
            weight_load(j).start()
        for mb in range(micro):
            end_load(mb, GY).start()

    def halo_copies(ref, which, mb):
        def make(side, count):
            if side == 0:
                source, target, to = ref.at[mb, pl.ds(2 * rows - count, count)], ref.at[mb, pl.ds(rows - count, count)], right
            else:
                source, target, to = ref.at[mb, pl.ds(rows, count)], ref.at[mb, pl.ds(2 * rows, count)], left
            return pltpu.make_async_remote_copy(
                src_ref=source, dst_ref=target, send_sem=halo_send.at[which, mb, side],
                recv_sem=halo_recv.at[which, mb, side], device_id=to, device_id_type=MESH)

        return make

    def halo(ref, which, mb, act_right, act_left):
        make = halo_copies(ref, which, mb)
        for mine, count in ((first, EDGE), (second, rows)):

            @pl.when(mine)
            def _():
                when(act_right[0], lambda: act_right[1](make(0, count)))
                when(act_left[0], lambda: act_left[1](make(1, count)))

    def halo_start(ref, which, mb):
        go = lambda c: c.start()
        halo(ref, which, mb, (has_right, go), (has_left, go))

    def halo_arrived(ref, which, mb):
        go = lambda c: c.wait_recv()
        halo(ref, which, mb, (has_left, go), (has_right, go))

    def halo_sent(ref, which, mb):
        go = lambda c: c.wait_send()
        halo(ref, which, mb, (has_right, go), (has_left, go))

    def shifted(ref, mb, k, sign, target, at, column):
        shift = sign * (k - REACH)

        @pl.when(first)
        def _():
            target[at : at + rows, column : column + inner] = ref[mb, pl.ds(rows + shift * FIRST_DILATION, rows), :]

        @pl.when(second)
        def _():
            target[at : at + rows, column : column + inner] = ref[mb, pl.ds(rows + shift * SECOND_DILATION, rows), :]

    def all_shifted(ref, mb, sign):
        for mine, dilation in ((first, FIRST_DILATION), (second, SECOND_DILATION)):

            @pl.when(mine)
            def _():
                for k in range(FILTER_TAPS):
                    at = rows + sign * (k - REACH) * dilation
                    taps[:, k * inner : (k + 1) * inner] = ref[mb, pl.ds(at, rows), :]

    def hand_over(mb, target):
        slot = lax.rem(mb, 2)
        return pltpu.make_async_remote_copy(
            src_ref=handing.at[slot], dst_ref=target.at[mb], send_sem=hand_send.at[mb], recv_sem=hand_recv.at[mb],
            device_id=across, device_id_type=MESH)

    def store_end(mb):
        return pltpu.make_async_copy(handing.at[lax.rem(mb, 2)], ends_out.at[mb], store.at[mb])

    own = pl.ds(rows, rows)
    outer_shift, inner_shift_b, inner_shift_c = 0.5 * outer_biases[0:1, :], 0.5 * inner_biases[0:1, :], 0.5 * inner_biases[1:2, :]
    outer_half, inner_half_b, inner_half_c = 0.5 * outer_gain[...], 0.5 * inner_gains[0:1, :], 0.5 * inner_gains[1:2, :]

    def valid_of(mb):
        position = z * rows + lax.broadcasted_iota(jnp.int32, (rows, 1), 0)
        return (position < lengths[mb]).astype(F32)

    def forward_a(mb):
        when(jnp.logical_and(first, mb > 0), lambda: end_load(mb, X).wait())
        when(second, lambda: hand_over(mb, X).wait_recv())
        when(jnp.logical_and(second, mb == 0), lambda: weight_load(0).wait())
        n, mean, scale, spread = normed(X[mb].astype(F32))
        XS[...] += (spread + mean * mean) * valid_of(mb)
        ST[mb, :, 0:1] = mean
        ST[mb, :, 1:2] = scale
        hidden = gelu(n * outer_half + outer_shift).astype(BF)
        HA[mb] = hidden
        n, _, scale, _ = normed(nn(hidden, down[...]) + inner_biases[2:3, :])
        NB[mb] = n
        ST[mb, :, 2:3] = scale
        CW[mb, own, :] = (gelu(n * inner_half_b + inner_shift_b) * valid_of(mb)).astype(BF)
        when(jnp.logical_and(first, mb == 0), met)
        halo_start(CW, 0, mb)

    halves = [slice(h * (rows // 2), (h + 1) * (rows // 2)) for h in range(2)]

    def forward_b(mb):
        slot = lax.rem(mb, 2)
        halo_arrived(CW, 0, mb)

        @pl.when(mb == 0)
        def _():
            weight_load(1).wait()
            weight_load(2).wait()

        @pl.when(mb >= 2)
        def _():
            when(first, lambda: hand_over(mb - 2, X).wait_send())
            when(second, lambda: store_end(mb - 2).wait())

        all_shifted(CW, mb, 1)

        def norm_c(half, product):
            n, _, scale, _ = normed(product + inner_biases[3:4, :])
            NC[mb, half, :] = n
            ST[mb, half, 3:4] = scale
            hidden = (gelu(n * inner_half_c + inner_shift_c) * valid_of(mb)[half, :]).astype(BF)
            HC[mb, half, :] = hidden
            return hidden

        def close(half, product):
            branch = (product + outer_biases[1:2, :]) * valid_of(mb)[half, :]
            oacc[3] += fold(branch * branch)
            value = X[mb, half, :].astype(F32) + branch
            handing[slot, half, :] = value.astype(BF)

        lower = nn(taps[halves[0], :], conv[...])
        upper = nn(taps[halves[1], :], conv[...])
        hidden = norm_c(halves[0], lower)
        lower = nn(hidden, up[...])
        hidden = norm_c(halves[1], upper)
        upper = nn(hidden, up[...])
        close(halves[0], lower)
        close(halves[1], upper)
        when(first, lambda: hand_over(mb, X).start())
        when(second, lambda: store_end(mb).start())

    def backward_a(mb):
        when(jnp.logical_and(first, mb < micro - 1), lambda: hand_over(mb, GY).wait_recv())

        @pl.when(jnp.logical_and(second, mb == 0))
        def _():
            for k in range(micro):
                end_load(k, GY).wait()

        valid = valid_of(mb)
        oacc[2] += fold(GY[mb].astype(F32) * valid)
        dv, terms, dz = norm_gelu_back(
            nt(GY[mb], up[...]) * valid, NC[mb], ST[mb, :, 3:4], inner_gains[1:2, :], inner_half_c, inner_shift_c
        )
        iacc[3] += fold(terms)
        iacc[4] += fold(dv)
        iacc[5] += fold(dz)
        GCW[mb, own, :] = dz.astype(BF)
        halo_start(GCW, 1, mb)

    def backward_b(mb):
        halo_arrived(GCW, 1, mb)
        all_shifted(GCW, mb, -1)
        total = nt(taps[:, 0:inner], conv[0:inner, :])
        for k in range(1, FILTER_TAPS):
            total = total + nt(taps[:, k * inner : (k + 1) * inner], conv[k * inner : (k + 1) * inner, :])
        dv, terms, dz = norm_gelu_back(
            total * valid_of(mb), NB[mb], ST[mb, :, 2:3], inner_gains[0:1, :], inner_half_b, inner_shift_b
        )
        iacc[0] += fold(terms)
        iacc[1] += fold(dv)
        iacc[2] += fold(dz)
        GP[mb] = dz.astype(BF)

    def backward_c(mb):
        slot = lax.rem(mb, 2)

        @pl.when(mb < 2)
        def _():
            when(first, lambda: hand_over(mb + micro - 2, X).wait_send())
            when(second, lambda: store_end(mb + micro - 2).wait())

        @pl.when(mb >= 2)
        def _():
            when(second, lambda: hand_over(mb - 2, GY).wait_send())
            when(first, lambda: store_end(mb - 2).wait())

        scale = ST[mb, :, 1:2]
        n = (X[mb].astype(F32) - ST[mb, :, 0:1]) * scale
        dv, terms, dz = norm_gelu_back(nt(GP[mb], down[...]), n, scale, outer_gain[...], outer_half, outer_shift)
        oacc[0] += fold(terms)
        oacc[1] += fold(dv)
        value = GY[mb].astype(F32) + dz
        handing[slot] = value.astype(BF)
        when(second, lambda: hand_over(mb, GY).start())
        when(first, lambda: store_end(mb).start())

    def weight_up():
        when(first, lambda: hand_over(micro - 1, GY).wait_recv())
        total = tn(HC[...].reshape(micro * rows, inner), GY[...].reshape(micro * rows, width)).astype(BF)
        for h in range(UP_BLOCKS):
            grad[h * BLOCK : (h + 1) * BLOCK, :] = total[:, h * inner : (h + 1) * inner]

    def weight_tap(tap):
        for k in range(FILTER_TAPS):

            @pl.when(tap == k)
            def _():
                for mb in range(micro):
                    shifted(CW, mb, k, 1, lhs, mb * rows, 0)

        y = GCW[:, own, :].reshape(micro * rows, inner)
        at = pl.multiple_of((UP_BLOCKS + tap) * BLOCK, BLOCK)
        grad[pl.ds(at, BLOCK), :] = tn(lhs[...], y).astype(BF)

    def weight_down():
        y = GP[...].reshape(micro * rows, inner)
        for h in range(BLOCKS - DOWN_AT):
            at = (DOWN_AT + h) * BLOCK
            a = HA[:, :, h * inner : (h + 1) * inner].reshape(micro * rows, inner)
            grad[at : at + BLOCK, :] = tn(a, y).astype(BF)

    def row(value):
        return jnp.sum(value, axis=0, keepdims=True)

    def smalls():
        place = 0

        def put(value):
            nonlocal place
            for at in range(0, value.shape[1], inner):
                small[0, place : place + 1, :] = value[:, at : at + inner]
                place += 1

        small[0] = jnp.zeros_like(small[0])
        for ref, j in ((oacc, 0), (iacc, 0), (iacc, 3), (oacc, 1), (oacc, 2), (iacc, 1), (iacc, 4), (iacc, 2), (iacc, 5)):
            put(row(ref[j]))
        lane = lax.broadcasted_iota(jnp.int32, (1, inner), 1)
        put(jnp.where(lane == 0, row(XS[...]) * width, 0.0))
        value = row(oacc[3])
        put(value[:, :inner] + value[:, inner:])
        count = jnp.float32(0)
        for mb in range(micro):
            count += jnp.clip(lengths[mb] - z * rows, 0, rows).astype(F32)
        put(jnp.zeros((1, inner), F32) + count)

    when(second, met)
    plans = [[(p * 8 + k) * 8 + steps for p, k, steps in plan] for plan in (FIRST_PLAN, SECOND_PLAN)]
    def mine(a, b):
        return a if a == b else jnp.where(first, a, b)

    begins = [mine(a, b) for a, b in zip(begins_of(FIRST_PLAN, FIRST_PACE), begins_of(SECOND_PLAN, SECOND_PACE))]
    square, line, late = (mine(a, b) for a, b in zip(FIRST_PACE[:3], SECOND_PACE[:3]))
    same = FIRST_PACE[0] == FIRST_PACE[1] and SECOND_PACE[0] == SECOND_PACE[1]
    pace = (line if same else square, line, late)
    planned = mine(planned_steps(FIRST_PLAN), planned_steps(SECOND_PLAN))
    ticks = mine(steps_of(FIRST_PLAN, FIRST_PACE), steps_of(SECOND_PLAN, SECOND_PACE))

    def tick(t, carry):
        sums.tick(t, begins, pace, planned)
        return carry

    def step(i, t):
        entry = jnp.int32(0)
        for j, (a, b) in enumerate(zip(*plans)):
            entry = jnp.where(i == j, jnp.where(first, a, b), entry)
        what, k = entry // 64, lax.rem(entry // 8, 8)
        for p, act in ((FA, forward_a), (FB, forward_b), (BA, backward_a), (BB, backward_b), (BC, backward_c), (WC, weight_tap)):
            when(what == p, functools.partial(act, k))
        when(what == WU, weight_up)
        when(what == WD, weight_down)
        then = t + lax.rem(entry, 8)
        if with_sums:
            lax.fori_loop(t, then, tick, 0)
        return then

    t = lax.fori_loop(0, len(FIRST_PLAN), step, jnp.int32(0))
    smalls()

    if with_sums:
        lax.fori_loop(t, ticks, tick, 0)
        sums.drain()
        done = pltpu.make_async_copy(small.at[4], small_out, load.at[0])
        done.start()
        done.wait()
    else:
        done = pltpu.make_async_copy(small.at[0], small_out, load.at[0])
        done.start()
        done.wait()
        done = pltpu.make_async_copy(grad, res, load.at[1])
        done.start()
        done.wait()
    for mb in range(micro):
        if mb >= micro - 2:
            when(first, functools.partial(lambda m: store_end(m).wait(), mb))
            when(second, functools.partial(lambda m: hand_over(m, GY).wait_send(), mb))
        halo_sent(CW, 0, mb)
        halo_sent(GCW, 1, mb)


def run_blocks(mesh_shape, ends, lengths, outer_gain, inner_gains, outer_biases, inner_biases, down, conv, up):
    micro, rows, width = ends.shape
    inner = down.shape[1]
    taps = FILTER_TAPS
    with_sums = (mesh_shape["dp"], mesh_shape["seq"]) == (4, 4)
    buffers = {k: pltpu.VMEM((GROUPS, n, BLOCK), BF) for k, n in RECEIVE.items()} if with_sums else {}
    names = tuple(buffers)
    total = BLOCKS * BLOCK
    anywhere = pl.BlockSpec(memory_space=pl.ANY)
    vmem = pl.BlockSpec(memory_space=pltpu.VMEM)
    dma = pltpu.SemaphoreType.DMA
    scratch = [
        pltpu.VMEM(down.shape, BF),
        pltpu.VMEM(conv.shape, BF),
        pltpu.VMEM(up.shape, BF),
        pltpu.VMEM((micro, rows, width), BF),
        pltpu.VMEM((micro, rows, width), BF),
        pltpu.VMEM((micro, rows, width), BF),
        pltpu.VMEM((micro, 3 * rows, inner), BF),
        pltpu.VMEM((micro, rows, inner), BF),
        pltpu.VMEM((micro, 3 * rows, inner), BF),
        pltpu.VMEM((micro, rows, inner), BF),
        pltpu.VMEM((micro, rows, inner), F32),
        pltpu.VMEM((micro, rows, inner), F32),
        pltpu.VMEM((micro, rows, 128), F32),
        pltpu.VMEM((rows, 1), F32),
        pltpu.VMEM((2, rows, width), BF),
        pltpu.VMEM((rows, taps * inner), BF),
        pltpu.VMEM((micro * rows, inner), BF),
        pltpu.VMEM((4, 8, width), F32),
        pltpu.VMEM((6, 8, inner), F32),
        pltpu.VMEM((total, BLOCK), BF),
        pltpu.VMEM((9, 16, inner), F32),
        *[buffers[k] for k in names],
        dma((len(KINDS),)),
        dma((GROUPS, max(ARRIVES.values()) + 1)),
        dma((2,)),
        dma((len(SMALL_KINDS),)),
        dma((len(SMALL_KINDS),)),
        dma((micro + 3,)),
        dma((micro,)),
        dma((micro,)),
        dma((2, micro, 2)),
        dma((2, micro, 2)),
        dma((micro,)),
    ]
    flops = 2 * 3 * micro * rows * (2 * width * inner + taps * inner * inner)
    return pl.pallas_call(
        functools.partial(blocks_kernel, names, with_sums, mesh_shape["seq"] - 1),
        name="two_blocks",
        out_shape=(
            jax.ShapeDtypeStruct((micro, rows, width), BF),
            jax.ShapeDtypeStruct((total, BLOCK), BF),
            jax.ShapeDtypeStruct((16, inner), F32),
        ),
        in_specs=[anywhere, pl.BlockSpec(memory_space=pltpu.SMEM), vmem, vmem, vmem, vmem, anywhere, anywhere, anywhere],
        out_specs=[anywhere] * 3,
        scratch_shapes=scratch,
        cost_estimate=pl.CostEstimate(flops=flops, bytes_accessed=40 * 2**20, transcendentals=0),
        compiler_params=pltpu.CompilerParams(collective_id=1, has_side_effects=True, vmem_limit_bytes=62 * 2**20),
    )(ends, lengths, outer_gain, inner_gains, outer_biases, inner_biases, down, conv, up)


AHEAD = 6


def finish_kernel(
    ends, rows, small, ends_out, outer_gain, inner_gains, outer_biases, inner_biases, down, conv, up, rms,
    raw, full, held, wide, load, store,
):
    micro, width = ends.shape[0], ends.shape[2]
    places = [up.at[0, :, pl.ds(h * BLOCK, BLOCK)] for h in range(UP_BLOCKS)]
    places += [conv.at[0, k] for k in range(FILTER_TAPS)]
    places += [down.at[0, pl.ds(h * BLOCK, BLOCK)] for h in range(BLOCKS - DOWN_AT)]
    moves = [(rows.at[pl.ds(g * BLOCK, BLOCK)], raw.at[g], full.at[g], places[g]) for g in range(BLOCKS)]
    moves += [(ends.at[mb], held.at[mb], wide.at[mb], ends_out.at[0, mb, 0]) for mb in range(micro)]
    loads = [pltpu.make_async_copy(m[0], m[1], load.at[i]) for i, m in enumerate(moves)]
    stores = [pltpu.make_async_copy(m[2], m[3], store.at[i]) for i, m in enumerate(moves)]
    for copy in loads[:AHEAD]:
        copy.start()
    outer_gain[0:1, 0:BLOCK] = small[0:1, :]
    outer_gain[0:1, BLOCK:] = small[1:2, :]
    inner_gains[0] = small[2:4, :]
    for j in range(2):
        outer_biases[0, j : j + 1, 0:BLOCK] = small[4 + 2 * j : 5 + 2 * j, :]
        outer_biases[0, j : j + 1, BLOCK:] = small[5 + 2 * j : 6 + 2 * j, :]
    inner_biases[0] = small[8:12, :]
    squares = jnp.sum(small[12:14, :], axis=1, keepdims=True)
    roots = jnp.sqrt(squares / (small[14:15, 0:1] * width))
    rms[0:1, 0:1] = roots[0:1, :]
    rms[0:1, 1:2] = roots[1:2, :]
    for i, (_, source, target, _) in enumerate(moves):
        loads[i].wait()
        if i + AHEAD < len(moves):
            loads[i + AHEAD].start()
        target[...] = source[...].astype(F32)
        stores[i].start()
    for copy in stores:
        copy.wait()


def finish(shapes, ends, rows, small):
    anywhere = pl.BlockSpec(memory_space=pl.ANY)
    vmem = pl.BlockSpec(memory_space=pltpu.VMEM)
    dma = pltpu.SemaphoreType.DMA
    return pl.pallas_call(
        finish_kernel,
        name="outputs",
        out_shape=tuple(jax.ShapeDtypeStruct(shape, F32) for shape in shapes),
        in_specs=[anywhere, anywhere, vmem],
        out_specs=[anywhere, vmem, vmem, vmem, vmem, anywhere, anywhere, anywhere, vmem],
        scratch_shapes=[
            pltpu.VMEM((BLOCKS, BLOCK, BLOCK), BF),
            pltpu.VMEM((BLOCKS, BLOCK, BLOCK), F32),
            pltpu.VMEM(ends.shape, BF),
            pltpu.VMEM(ends.shape, F32),
            dma((BLOCKS + ends.shape[0],)),
            dma((BLOCKS + ends.shape[0],)),
        ],
        compiler_params=pltpu.CompilerParams(vmem_limit_bytes=60 * 2**20),
    )(ends, rows, small)


def body(
    mesh_shape, ends_in, lengths, outer_gain, inner_gains, outer_biases, inner_biases, down_in, conv_weight, up_out
):
    width = ends_in.shape[-1]
    ends, rows, small = run_blocks(
        mesh_shape, ends_in.reshape(ends_in.shape[1], -1, width), lengths.reshape(-1), outer_gain, inner_gains[0],
        outer_biases[0], inner_biases[0], down_in[0], conv_weight[0].reshape(-1, conv_weight.shape[-1]), up_out[0],
    )
    if (mesh_shape["dp"], mesh_shape["seq"]) == (4, 4):
        weights = (outer_gain, inner_gains, outer_biases, inner_biases, down_in, conv_weight, up_out)
        return finish((ends_in.shape, *(w.shape for w in weights), (1, 2)), ends, rows, small)
    rows, small = lax.psum((rows.astype(F32), small), ("dp", "seq"))
    up = jnp.concatenate([rows[:BLOCK], rows[BLOCK : 2 * BLOCK]], axis=1)
    conv = rows[UP_BLOCKS * BLOCK : DOWN_AT * BLOCK].reshape(conv_weight.shape[1:])
    down = rows[DOWN_AT * BLOCK :]
    rms = jnp.sqrt(jnp.sum(small[12:14], axis=1) / (small[14, 0] * width))
    return (
        ends.astype(F32).reshape(ends_in.shape),
        small[0:2].reshape(1, -1),
        small[None, 2:4],
        small[4:8].reshape(1, 2, -1),
        small[None, 8:12],
        down[None],
        conv[None],
        up[None],
        rms[None],
    )


def solution(mesh):
    in_specs = (
        P("section", None, "dp", "seq", None),
        P(None, "dp"),
        P("section", None),
        P("section", None, None),
        P("section", None, None),
        P("section", None, None),
        P("section", None, None),
        P("section", None, None, None),
        P("section", None, None),
    )
    out_specs = (
        P("section", None, "dp", "seq", None),
        P("section", None),
        P("section", None, None),
        P("section", None, None),
        P("section", None, None),
        P("section", None, None),
        P("section", None, None, None),
        P("section", None, None),
        P("section", None),
    )
    return jax.shard_map(
        functools.partial(body, dict(mesh.shape)), mesh=mesh, in_specs=in_specs, out_specs=out_specs, check_vma=False
    )
```

```python
import functools
import math

import jax
import jax.numpy as jnp
from jax import lax
from jax.experimental import pallas as pl
from jax.experimental.pallas import tpu as pltpu
from jax.sharding import PartitionSpec as P

MESH = pl.DeviceIdType.MESH
BF = jnp.bfloat16
F32 = jnp.float32
FILTER_TAPS = 5
FIRST_DILATION = 2
SECOND_DILATION = 128
REACH = FILTER_TAPS // 2
EPS = 1e-05
GELU_A = math.sqrt(2.0 / math.pi)
GELU_B = GELU_A * 0.044715
EDGE = 16

BLOCK = 640
UP_BLOCKS = 2
DOWN_AT = UP_BLOCKS + FILTER_TAPS
BLOCKS = DOWN_AT + 2
GROUPS = 10
ROWS = BLOCKS * BLOCK // GROUPS
LROWS = 384
HALF = LROWS // 2
QUARTER = LROWS // 4
CHUNK = (ROWS - LROWS) // 4
KINDS = (
    "ru", "rv", "za", "zb", "zc", "av", "au", "aw",
    "ze", "zm", "zo", "ex", "ey", "ge", "gn", "gd", "gf", "gp", "gq",
)
ARRIVES = dict(ru=0, rv=1, av=2, au=3, aw=4, ex=5, ey=6, za=7, zb=8, ze=9, zm=10, ge=11, gn=12, gf=13,
               zc=7, zo=8, gd=9, gp=10, gq=11)
SMALL_KINDS = ("sx", "sy", "sa", "sb", "sc")
RECEIVE = dict(ru=HALF, rv=QUARTER, za=QUARTER, zb=QUARTER, fl=QUARTER, ze=3 * CHUNK, zm=2 * CHUNK,
               zo=CHUNK, ex=CHUNK, ey=CHUNK, tx=CHUNK, fz=CHUNK)
L_LEVELS = 8
Z_LEVELS = 9
FIRST_PACE = (2, 2, 0, 1)
SECOND_PACE = (2, 2, 0, 1)

FA, FB, WU, BA, BB, BC, WC, WD = range(1, 9)
FIRST_PLAN = (
    (FA, 0, 0), (FA, 1, 0), (FB, 0, 0), (FA, 2, 0), (FB, 1, 0), (FA, 3, 0), (FB, 2, 0), (FB, 3, 0), (BA, 0, 0), (BA, 1, 0), (BB, 0, 0), (BC, 0, 0), (BA, 2, 0), (BB, 1, 0), (BC, 1, 0), (BB, 2, 0), (WU, 0, 0), (BA, 3, 1), (BC, 2, 3), (BB, 3, 0), (BC, 3, 2), (WC, 0, 0), (WC, 1, 0), (WC, 2, 3), (WC, 3, 0), (WC, 4, 1), (WD, 0, 0),
)
SECOND_PLAN = (
    (FA, 0, 0), (FA, 1, 0), (FB, 0, 0), (FA, 2, 0), (FB, 1, 0), (FA, 3, 0), (FB, 2, 0), (BA, 0, 0), (FB, 3, 0), (WU, 0, 1), (BA, 1, 0), (BB, 0, 0), (BC, 0, 1), (BA, 2, 1), (BB, 1, 0), (BC, 1, 1), (BA, 3, 1), (BB, 2, 0), (BC, 2, 1), (WC, 0, 1), (WC, 1, 0), (BB, 3, 1), (WC, 2, 1), (BC, 3, 1), (WC, 3, 1), (WC, 4, 1), (WD, 0, 1),
)


def begins_of(plan, pace):
    ready, steps = {}, 0
    for what, k, count in plan:
        for block in {WU: range(UP_BLOCKS), WC: (UP_BLOCKS + k,), WD: range(DOWN_AT, BLOCKS)}.get(what, ()):
            ready[block] = steps
        steps += count
    begins = []
    for g in range(GROUPS):
        there = max(ready[block] for block in range(g * ROWS // BLOCK, ((g + 1) * ROWS - 1) // BLOCK + 1))
        begins.append(max(there, begins[-1] + pace[3]) if begins else there)
    return begins


def planned_steps(plan):
    return sum(entry[2] for entry in plan)


def steps_of(plan, pace):
    square, line, late, _ = pace
    last = begins_of(plan, pace)[-1] + max(square * (L_LEVELS - 1), late + line * (Z_LEVELS - 1))
    return max(last + 1, planned_steps(plan) + 6)


def aligned(offset):
    return offset if isinstance(offset, int) else pl.multiple_of(offset, 16)


def part(ref, offset, rows):
    return ref.at[pl.ds(aligned(offset), rows)]


def added(target, offset, sources, rows, tile=16):
    for start in range(0, rows, tile):
        total = None
        for ref, at in sources:
            value = ref[pl.ds(aligned(at + start), tile), :]
            if len(sources) > 2:
                value = value.astype(F32)
            total = value if total is None else total + value
        target[pl.ds(aligned(offset + start), tile), :] = total.astype(BF)


class WeightSums:
    def __init__(self, grad, res, small, buffers, send, recv, local, small_send, small_recv):
        self.grad, self.res, self.small, self.r = grad, res, small, buffers
        self.send, self.recv, self.local = send, recv, local
        self.small_send, self.small_recv = small_send, small_recv
        self.c = lax.axis_index("section")
        self.dp = lax.axis_index("dp")
        self.z = lax.axis_index("seq")
        self.x = lax.rem(self.dp, 2)
        self.y = self.dp // 2
        z = self.z
        self.upper = z // 2
        self.end = jnp.logical_or(z == 0, z == 3)
        self.mid = jnp.logical_not(self.end)
        self.dp_x = self.dp + 1 - 2 * self.x
        self.dp_y = lax.rem(self.dp + 2, 4)
        self.px = (self.c, self.dp_x, z)
        self.py = (self.c, self.dp_y, z)
        self.pair = (self.c, self.dp, 1 - z + 4 * self.upper)
        self.other = (self.c, self.dp, jnp.clip(3 - z, 1, 2))

    def copy(self, kind, g, source, target, to):
        j = KINDS.index(kind)
        return pltpu.make_async_remote_copy(
            src_ref=source, dst_ref=target, send_sem=self.send.at[j], recv_sem=self.recv.at[g, ARRIVES[kind]],
            device_id=to, device_id_type=MESH)

    def square(self, g):
        odd = lax.rem(g, 2)
        u = jnp.where(odd == 0, self.x, self.y)
        v = jnp.where(odd == 0, self.y, self.x)
        to_u = (self.c, jnp.where(odd == 0, self.dp_x, self.dp_y), self.z)
        to_v = (self.c, jnp.where(odd == 0, self.dp_y, self.dp_x), self.z)
        base = g * ROWS
        own_half = base + u * HALF
        own = own_half + v * QUARTER
        beside = own_half + (1 - v) * QUARTER
        return base, u, v, to_u, to_v, own, beside

    def square_copy(self, kind, g):
        base, u, v, to_u, to_v, own, beside = self.square(g)
        grad, res, r = self.grad, self.res, self.r
        final = r["fl"].at[g]
        if kind == "ru":
            return self.copy(kind, g, part(grad, base + (1 - u) * HALF, HALF), r["ru"].at[g], to_u)
        if kind == "rv":
            return self.copy(kind, g, part(grad, beside, QUARTER), r["rv"].at[g], to_v)
        if kind == "za":
            return self.copy(kind, g, part(grad, own, QUARTER), r["za"].at[g], self.pair)
        if kind == "zb":
            return self.copy(kind, g, part(grad, own, QUARTER), r["zb"].at[g], self.other)
        if kind == "zc":
            return self.copy(kind, g, final, final, self.pair)
        if kind == "av":
            return self.copy(kind, g, final, part(res, own, QUARTER), to_v)
        if kind == "au":
            return self.copy(kind, g, final, part(res, own, QUARTER), to_u)
        if kind == "aw":
            return self.copy(kind, g, part(res, beside, QUARTER), part(res, beside, QUARTER), to_u)
        return pltpu.make_async_copy(final, part(res, own, QUARTER), self.local.at[0])

    def square_level(self, g, level):
        base, u, v, to_u, to_v, own, beside = self.square(g)
        grad, r = self.grad, self.r
        copy = functools.partial(self.square_copy, g=g)
        if level == 0:
            copy("ru").start()
        elif level == 1:
            copy("ru").wait_recv()
            added(grad, beside, [(grad, beside), (r["ru"].at[g], (1 - v) * QUARTER)], QUARTER)
            copy("rv").start()
            added(grad, own, [(grad, own), (r["ru"].at[g], v * QUARTER)], QUARTER)
        elif level == 2:
            copy("rv").wait_recv()
            added(grad, own, [(grad, own), (r["rv"].at[g], 0)], QUARTER)

            @pl.when(self.end)
            def _():
                copy("za").start()
        elif level == 3:

            @pl.when(self.mid)
            def _():
                copy("za").wait_recv()
                added(grad, own, [(grad, own), (r["za"].at[g], 0)], QUARTER)
                copy("zb").start()
        elif level == 4:

            @pl.when(self.mid)
            def _():
                copy("zb").wait_recv()
                added(r["fl"].at[g], 0, [(grad, own), (r["zb"].at[g], 0)], QUARTER)
                copy("zc").start()
                copy("av").start()
                copy("au").start()
                copy("fl").start()
        elif level == 5:

            @pl.when(self.end)
            def _():
                copy("zc").wait_recv()
                copy("av").start()
                copy("au").start()
                copy("fl").start()
        elif level == 6:
            copy("av").wait_recv()
            copy("aw").start()
        elif level == 7:
            copy("au").wait_recv()
            copy("aw").wait_recv()

    def line(self, g):
        base = g * ROWS + LROWS
        upper = self.upper
        three = base + CHUNK * (1 - upper)
        far = base + 2 * CHUNK * (1 - upper)
        near = base + 2 * CHUNK * upper
        outer = base + 3 * CHUNK * upper
        own = base + CHUNK * self.z
        return three, far, near, outer, own

    def line_copy(self, kind, g):
        three, far, near, outer, own = self.line(g)
        grad, res, r = self.grad, self.res, self.r
        base = g * ROWS + LROWS
        final = r["fz"].at[g]
        here = part(res, own, CHUNK)
        if kind == "ze":
            return self.copy(kind, g, part(grad, three, 3 * CHUNK), r["ze"].at[g], self.pair)
        if kind == "zm":
            return self.copy(kind, g, part(grad, far, 2 * CHUNK), r["zm"].at[g], self.other)
        if kind == "zo":
            return self.copy(kind, g, part(grad, outer, CHUNK), r["zo"].at[g], self.pair)
        if kind == "ex":
            return self.copy(kind, g, part(grad, own, CHUNK), r["ex"].at[g], self.px)
        if kind == "ey":
            return self.copy(kind, g, r["tx"].at[g], r["ey"].at[g], self.py)
        if kind in ("ge", "gd"):
            return self.copy(kind, g, final, here, self.pair)
        if kind == "gn":
            return self.copy(kind, g, final, here, self.other)
        if kind == "gf":
            rows = part(res, outer, CHUNK)
            return self.copy(kind, g, rows, rows, self.other)
        if kind == "gp":
            rows = part(res, base + CHUNK * (3 - self.z), CHUNK)
            return self.copy(kind, g, rows, rows, self.pair)
        if kind == "gq":
            rows = part(res, base + 3 * CHUNK * (1 - self.upper), CHUNK)
            return self.copy(kind, g, rows, rows, self.pair)
        return pltpu.make_async_copy(final, here, self.local.at[1])

    def line_level(self, g, level):
        three, far, near, outer, own = self.line(g)
        grad, r = self.grad, self.r
        copy = functools.partial(self.line_copy, g=g)
        if level == 0:

            @pl.when(self.end)
            def _():
                copy("ze").start()
        elif level == 1:

            @pl.when(self.mid)
            def _():
                copy("ze").wait_recv()
                added(grad, far, [(grad, far), (r["ze"].at[g], far - three)], 2 * CHUNK)
                copy("zm").start()
        elif level == 2:

            @pl.when(self.mid)
            def _():
                copy("zm").wait_recv()
                added(grad, outer, [(grad, outer), (r["zm"].at[g], outer - near)], CHUNK)
                copy("zo").start()
                added(grad, own, [(grad, own), (r["ze"].at[g], own - three), (r["zm"].at[g], own - near)], CHUNK)
                copy("ex").start()
        elif level == 3:

            @pl.when(self.end)
            def _():
                copy("zo").wait_recv()
                added(grad, own, [(grad, own), (r["zo"].at[g], 0)], CHUNK)
                copy("ex").start()
        elif level == 4:
            copy("ex").wait_recv()
            added(r["tx"].at[g], 0, [(grad, own), (r["ex"].at[g], 0)], CHUNK)
            copy("ey").start()
        elif level == 5:
            copy("ey").wait_recv()
            added(r["fz"].at[g], 0, [(r["tx"].at[g], 0), (r["ey"].at[g], 0)], CHUNK)
            copy("fz").start()

            @pl.when(self.end)
            def _():
                copy("ge").start()

            @pl.when(self.mid)
            def _():
                copy("gn").start()
                copy("gd").start()
        elif level == 6:

            @pl.when(self.mid)
            def _():
                copy("ge").wait_recv()
                copy("gf").start()
                copy("gn").wait_recv()
                copy("gp").start()
        elif level == 7:

            @pl.when(self.mid)
            def _():
                copy("gf").wait_recv()
                copy("gq").start()
        elif level == 8:

            @pl.when(self.end)
            def _():
                copy("gd").wait_recv()
                copy("gp").wait_recv()
                copy("gq").wait_recv()

    def small_copy(self, kind):
        j = SMALL_KINDS.index(kind)
        s = self.small
        source, target, to = dict(
            sx=(s.at[0], s.at[5], self.px),
            sy=(s.at[1], s.at[6], self.py),
            sa=(s.at[2], s.at[7], self.pair),
            sb=(s.at[3], s.at[8], self.other),
            sc=(s.at[4], s.at[4], self.pair),
        )[kind]
        return pltpu.make_async_remote_copy(
            src_ref=source, dst_ref=target, send_sem=self.small_send.at[j], recv_sem=self.small_recv.at[j],
            device_id=to, device_id_type=MESH)

    def small_level(self, level):
        copy, s = self.small_copy, self.small
        if level == 0:
            copy("sx").start()
        elif level == 1:
            copy("sx").wait_recv()
            s[1] = s[0] + s[5]
            copy("sy").start()
        elif level == 2:
            copy("sy").wait_recv()
            s[2] = s[1] + s[6]

            @pl.when(self.end)
            def _():
                copy("sa").start()
        elif level == 3:

            @pl.when(self.mid)
            def _():
                copy("sa").wait_recv()
                s[3] = s[2] + s[7]
                copy("sb").start()
        elif level == 4:

            @pl.when(self.mid)
            def _():
                copy("sb").wait_recv()
                s[4] = s[3] + s[8]
                copy("sc").start()
        elif level == 5:

            @pl.when(self.end)
            def _():
                copy("sc").wait_recv()

    def tick(self, t, begins, pace, small_begin):
        square, line, late = pace

        def beginning(step):
            g = jnp.int32(-1)
            for j, begin in enumerate(begins):
                g = jnp.where(step == begin, j, g)
            return g

        for level in reversed(range(Z_LEVELS)):
            g = beginning(t - late - line * level)
            if level < L_LEVELS:
                same = square is line and isinstance(late, int) and late == 0
                g_square = g if same else beginning(t - square * level)

                @pl.when(g_square >= 0)
                def _():
                    self.square_level(g_square, level)

            @pl.when(g >= 0)
            def _():
                self.line_level(g, level)

        for level in range(6):

            @pl.when(t == small_begin + level)
            def _():
                self.small_level(level)

    def all_sent(self, kind, rows):
        everything = self.grad.at[pl.ds(0, GROUPS * rows)]
        pltpu.make_async_remote_copy(
            src_ref=everything, dst_ref=everything, send_sem=self.send.at[KINDS.index(kind)],
            recv_sem=self.recv.at[0, 0], device_id=self.px, device_id_type=MESH).wait_send()

    def drain(self):
        for j, rows in ((0, QUARTER), (1, CHUNK)):
            everything = self.grad.at[pl.ds(0, GROUPS * rows)]
            pltpu.make_async_copy(everything, self.res.at[pl.ds(0, GROUPS * rows)], self.local.at[j]).wait()
        self.all_sent("ru", HALF)
        for kind in ("rv", "av", "au", "aw"):
            self.all_sent(kind, QUARTER)
        for kind in ("ex", "ey"):
            self.all_sent(kind, CHUNK)

        @pl.when(self.end)
        def _():
            self.all_sent("za", QUARTER)
            self.all_sent("ze", 3 * CHUNK)
            self.all_sent("ge", CHUNK)

        @pl.when(self.mid)
        def _():
            self.all_sent("zb", QUARTER)
            self.all_sent("zc", QUARTER)
            self.all_sent("zm", 2 * CHUNK)
            for kind in ("zo", "gn", "gd", "gf", "gp", "gq"):
                self.all_sent(kind, CHUNK)

        self.small_copy("sx").wait_send()
        self.small_copy("sy").wait_send()

        @pl.when(self.end)
        def _():
            self.small_copy("sa").wait_send()

        @pl.when(self.mid)
        def _():
            self.small_copy("sb").wait_send()
            self.small_copy("sc").wait_send()


def normed(value):
    mean = jnp.mean(value, axis=-1, keepdims=True)
    centred = value - mean
    spread = jnp.mean(centred * centred, axis=-1, keepdims=True)
    scale = lax.rsqrt(spread + EPS)
    return centred * scale, mean, scale, spread


def gelu(w):
    t = jnp.tanh(w * (2.0 * GELU_A + (8.0 * GELU_B) * (w * w)))
    return w + w * t


def gelu_slope(w):
    square = w * w
    t = jnp.tanh(w * (2.0 * GELU_A + (8.0 * GELU_B) * square))
    q = w * (GELU_A + (12.0 * GELU_B) * square)
    return (0.5 + q) + t * (0.5 - q * t)


def norm_gelu_back(grad, n, scale, gain, half_gain, half_shift):
    dv = grad * gelu_slope(n * half_gain + half_shift)
    terms = dv * n
    dn = dv * gain
    first = jnp.mean(dn, axis=-1, keepdims=True)
    second = jnp.mean(terms * gain, axis=-1, keepdims=True)
    return dv, terms, scale * (dn - first - n * second)


def fold(value):
    rows, width = value.shape
    return jnp.sum(value.reshape(rows // 8, 8, width), axis=0)


def nn(a, b):
    return jnp.dot(a, b, preferred_element_type=F32)


def nt(a, b):
    return lax.dot_general(a, b, (((1,), (1,)), ((), ())), preferred_element_type=F32)


def tn(a, b):
    return lax.dot_general(a, b, (((0,), (0,)), ((), ())), preferred_element_type=F32)


def blocks_kernel(
    names, with_sums, last,
    ends, lengths, outer_gain, inner_gains, outer_biases, inner_biases, down_hbm, conv_hbm, up_hbm,
    ends_out, res, small_out,
    down, conv, up, X, GY, HA, CW, HC, GCW, GP, NB, NC, ST, XS, handing, taps, lhs, oacc, iacc, grad, small,
    *rest,
):
    buffers = dict(zip(names, rest[: len(names)]))
    send, recv, local, small_send, small_recv, load, hand_send, hand_recv, halo_send, halo_recv, store = rest[len(names) :]
    micro, rows, width = X.shape
    inner = down.shape[1]
    section = lax.axis_index("section")
    dp = lax.axis_index("dp")
    z = lax.axis_index("seq")
    first = section == 0
    second = section == 1
    has_left = z > 0
    has_right = z < last
    across = (1 - section, dp, z)
    left = (section, dp, jnp.maximum(z - 1, 0))
    right = (section, dp, jnp.minimum(z + 1, last))
    sums = WeightSums(grad, res, small, buffers, send, recv, local, small_send, small_recv)

    def when(condition, act):
        pl.when(condition)(lambda: act() and None)

    def weight_load(j):
        return pltpu.make_async_copy((down_hbm, conv_hbm, up_hbm)[j], (down, conv, up)[j], load.at[micro + j])

    def end_load(mb, target):
        return pltpu.make_async_copy(ends.at[mb], target.at[mb], load.at[mb])

    @pl.when(first)
    def _():
        end_load(0, X).start()
        weight_load(0).start()

    barrier = pltpu.get_barrier_semaphore()

    def greet(to):
        pl.semaphore_signal(barrier, inc=1, device_id=to, device_id_type=MESH)

    greet(across)
    when(has_left, lambda: greet(left))
    when(has_right, lambda: greet(right))
    if with_sums:
        greet(sums.px)
        greet(sums.py)

    def met():
        peers = (3 if with_sums else 1) + has_left.astype(jnp.int32) + has_right.astype(jnp.int32)
        pl.semaphore_wait(barrier, peers)

    XS[...] = jnp.zeros_like(XS)
    oacc[...] = jnp.zeros_like(oacc)
    iacc[...] = jnp.zeros_like(iacc)
    edge = jnp.zeros((rows, inner), BF)
    for mb in range(micro):

        @pl.when(jnp.logical_not(has_left))
        def _():
            CW[mb, 0:rows, :] = edge
            GCW[mb, 0:rows, :] = edge

        @pl.when(jnp.logical_not(has_right))
        def _():
            CW[mb, 2 * rows : 3 * rows, :] = edge
            GCW[mb, 2 * rows : 3 * rows, :] = edge

    @pl.when(first)
    def _():
        end_load(0, X).wait()
        weight_load(0).wait()
        weight_load(1).start()
        weight_load(2).start()
        for mb in range(1, micro):
            end_load(mb, X).start()

    @pl.when(second)
    def _():
        for j in range(3):
            weight_load(j).start()
        for mb in range(micro):
            end_load(mb, GY).start()

    def halo_copies(ref, which, mb):
        def make(side, count):
            if side == 0:
                source, target, to = ref.at[mb, pl.ds(2 * rows - count, count)], ref.at[mb, pl.ds(rows - count, count)], right
            else:
                source, target, to = ref.at[mb, pl.ds(rows, count)], ref.at[mb, pl.ds(2 * rows, count)], left
            return pltpu.make_async_remote_copy(
                src_ref=source, dst_ref=target, send_sem=halo_send.at[which, mb, side],
                recv_sem=halo_recv.at[which, mb, side], device_id=to, device_id_type=MESH)

        return make

    def halo(ref, which, mb, act_right, act_left):
        make = halo_copies(ref, which, mb)
        for mine, count in ((first, EDGE), (second, rows)):

            @pl.when(mine)
            def _():
                when(act_right[0], lambda: act_right[1](make(0, count)))
                when(act_left[0], lambda: act_left[1](make(1, count)))

    def halo_start(ref, which, mb):
        go = lambda c: c.start()
        halo(ref, which, mb, (has_right, go), (has_left, go))

    def halo_arrived(ref, which, mb):
        go = lambda c: c.wait_recv()
        halo(ref, which, mb, (has_left, go), (has_right, go))

    def halo_sent(ref, which, mb):
        go = lambda c: c.wait_send()
        halo(ref, which, mb, (has_right, go), (has_left, go))

    def shifted(ref, mb, k, sign, target, at, column):
        shift = sign * (k - REACH)

        @pl.when(first)
        def _():
            target[at : at + rows, column : column + inner] = ref[mb, pl.ds(rows + shift * FIRST_DILATION, rows), :]

        @pl.when(second)
        def _():
            target[at : at + rows, column : column + inner] = ref[mb, pl.ds(rows + shift * SECOND_DILATION, rows), :]

    def all_shifted(ref, mb, sign):
        for mine, dilation in ((first, FIRST_DILATION), (second, SECOND_DILATION)):

            @pl.when(mine)
            def _():
                for k in range(FILTER_TAPS):
                    at = rows + sign * (k - REACH) * dilation
                    taps[:, k * inner : (k + 1) * inner] = ref[mb, pl.ds(at, rows), :]

    class HandOver:
        def __init__(self, mb, target):
            slot, half = lax.rem(mb, 2), rows // 2
            self.halves = [
                pltpu.make_async_remote_copy(
                    src_ref=handing.at[slot, pl.ds(h * half, half)], dst_ref=target.at[mb, pl.ds(h * half, half)],
                    send_sem=hand_send.at[mb, h], recv_sem=hand_recv.at[mb, h], device_id=across, device_id_type=MESH)
                for h in range(2)
            ]

        def start(self):
            for copy in self.halves:
                copy.start()

        def wait_send(self):
            for copy in self.halves:
                copy.wait_send()

        def wait_recv(self):
            for copy in self.halves:
                copy.wait_recv()

    hand_over = HandOver

    def store_end(mb):
        return pltpu.make_async_copy(handing.at[lax.rem(mb, 2)], ends_out.at[mb], store.at[mb])

    own = pl.ds(rows, rows)
    outer_shift, inner_shift_b, inner_shift_c = 0.5 * outer_biases[0:1, :], 0.5 * inner_biases[0:1, :], 0.5 * inner_biases[1:2, :]
    outer_half, inner_half_b, inner_half_c = 0.5 * outer_gain[...], 0.5 * inner_gains[0:1, :], 0.5 * inner_gains[1:2, :]

    def valid_of(mb):
        position = z * rows + lax.broadcasted_iota(jnp.int32, (rows, 1), 0)
        return (position < lengths[mb]).astype(F32)

    def forward_a(mb):
        when(jnp.logical_and(first, mb > 0), lambda: end_load(mb, X).wait())
        when(second, lambda: hand_over(mb, X).wait_recv())
        when(jnp.logical_and(second, mb == 0), lambda: weight_load(0).wait())
        n, mean, scale, spread = normed(X[mb].astype(F32))
        XS[...] += (spread + mean * mean) * valid_of(mb)
        ST[mb, :, 0:1] = mean
        ST[mb, :, 1:2] = scale
        hidden = gelu(n * outer_half + outer_shift).astype(BF)
        HA[mb] = hidden
        n, _, scale, _ = normed(nn(hidden, down[...]) + inner_biases[2:3, :])
        NB[mb] = n
        ST[mb, :, 2:3] = scale
        CW[mb, own, :] = (gelu(n * inner_half_b + inner_shift_b) * valid_of(mb)).astype(BF)
        when(jnp.logical_and(first, mb == 0), met)
        halo_start(CW, 0, mb)

    halves = [slice(h * (rows // 2), (h + 1) * (rows // 2)) for h in range(2)]

    def forward_b(mb):
        slot = lax.rem(mb, 2)
        halo_arrived(CW, 0, mb)

        @pl.when(mb == 0)
        def _():
            weight_load(1).wait()
            weight_load(2).wait()

        @pl.when(mb >= 2)
        def _():
            when(first, lambda: hand_over(mb - 2, X).wait_send())
            when(second, lambda: store_end(mb - 2).wait())

        all_shifted(CW, mb, 1)

        def norm_c(half, product):
            n, _, scale, _ = normed(product + inner_biases[3:4, :])
            NC[mb, half, :] = n
            ST[mb, half, 3:4] = scale
            hidden = (gelu(n * inner_half_c + inner_shift_c) * valid_of(mb)[half, :]).astype(BF)
            HC[mb, half, :] = hidden
            return hidden

        def close(half, product):
            branch = (product + outer_biases[1:2, :]) * valid_of(mb)[half, :]
            oacc[3] += fold(branch * branch)
            value = X[mb, half, :].astype(F32) + branch
            handing[slot, half, :] = value.astype(BF)

        lower = nn(taps[halves[0], :], conv[...])
        upper = nn(taps[halves[1], :], conv[...])
        hidden = norm_c(halves[0], lower)
        lower = nn(hidden, up[...])
        hidden = norm_c(halves[1], upper)
        upper = nn(hidden, up[...])
        close(halves[0], lower)
        when(first, lambda: hand_over(mb, X).halves[0].start())
        close(halves[1], upper)
        when(first, lambda: hand_over(mb, X).halves[1].start())
        when(second, lambda: store_end(mb).start())

    def backward_a(mb):
        when(jnp.logical_and(first, mb < micro - 1), lambda: hand_over(mb, GY).wait_recv())

        @pl.when(jnp.logical_and(second, mb == 0))
        def _():
            for k in range(micro):
                end_load(k, GY).wait()

        valid = valid_of(mb)
        oacc[2] += fold(GY[mb].astype(F32) * valid)
        dv, terms, dz = norm_gelu_back(
            nt(GY[mb], up[...]) * valid, NC[mb], ST[mb, :, 3:4], inner_gains[1:2, :], inner_half_c, inner_shift_c
        )
        iacc[3] += fold(terms)
        iacc[4] += fold(dv)
        iacc[5] += fold(dz)
        GCW[mb, own, :] = dz.astype(BF)
        halo_start(GCW, 1, mb)

    def backward_b(mb):
        halo_arrived(GCW, 1, mb)
        all_shifted(GCW, mb, -1)
        total = nt(taps[:, 0:inner], conv[0:inner, :])
        for k in range(1, FILTER_TAPS):
            total = total + nt(taps[:, k * inner : (k + 1) * inner], conv[k * inner : (k + 1) * inner, :])
        dv, terms, dz = norm_gelu_back(
            total * valid_of(mb), NB[mb], ST[mb, :, 2:3], inner_gains[0:1, :], inner_half_b, inner_shift_b
        )
        iacc[0] += fold(terms)
        iacc[1] += fold(dv)
        iacc[2] += fold(dz)
        GP[mb] = dz.astype(BF)

    def backward_c(mb):
        slot = lax.rem(mb, 2)

        @pl.when(mb < 2)
        def _():
            when(first, lambda: hand_over(mb + micro - 2, X).wait_send())
            when(second, lambda: store_end(mb + micro - 2).wait())

        @pl.when(mb >= 2)
        def _():
            when(second, lambda: hand_over(mb - 2, GY).wait_send())
            when(first, lambda: store_end(mb - 2).wait())

        scale = ST[mb, :, 1:2]
        n = (X[mb].astype(F32) - ST[mb, :, 0:1]) * scale
        dv, terms, dz = norm_gelu_back(nt(GP[mb], down[...]), n, scale, outer_gain[...], outer_half, outer_shift)
        oacc[0] += fold(terms)
        oacc[1] += fold(dv)
        value = GY[mb].astype(F32) + dz
        handing[slot] = value.astype(BF)
        when(second, lambda: hand_over(mb, GY).start())
        when(first, lambda: store_end(mb).start())

    def weight_up():
        when(first, lambda: hand_over(micro - 1, GY).wait_recv())
        total = tn(HC[...].reshape(micro * rows, inner), GY[...].reshape(micro * rows, width)).astype(BF)
        for h in range(UP_BLOCKS):
            grad[h * BLOCK : (h + 1) * BLOCK, :] = total[:, h * inner : (h + 1) * inner]

    def weight_tap(tap):
        for k in range(FILTER_TAPS):

            @pl.when(tap == k)
            def _():
                for mb in range(micro):
                    shifted(CW, mb, k, 1, lhs, mb * rows, 0)

        y = GCW[:, own, :].reshape(micro * rows, inner)
        at = pl.multiple_of((UP_BLOCKS + tap) * BLOCK, BLOCK)
        grad[pl.ds(at, BLOCK), :] = tn(lhs[...], y).astype(BF)

    def weight_down():
        y = GP[...].reshape(micro * rows, inner)
        for h in range(BLOCKS - DOWN_AT):
            at = (DOWN_AT + h) * BLOCK
            a = HA[:, :, h * inner : (h + 1) * inner].reshape(micro * rows, inner)
            grad[at : at + BLOCK, :] = tn(a, y).astype(BF)

    def row(value):
        return jnp.sum(value, axis=0, keepdims=True)

    def smalls():
        place = 0

        def put(value):
            nonlocal place
            for at in range(0, value.shape[1], inner):
                small[0, place : place + 1, :] = value[:, at : at + inner]
                place += 1

        small[0] = jnp.zeros_like(small[0])
        for ref, j in ((oacc, 0), (iacc, 0), (iacc, 3), (oacc, 1), (oacc, 2), (iacc, 1), (iacc, 4), (iacc, 2), (iacc, 5)):
            put(row(ref[j]))
        lane = lax.broadcasted_iota(jnp.int32, (1, inner), 1)
        put(jnp.where(lane == 0, row(XS[...]) * width, 0.0))
        value = row(oacc[3])
        put(value[:, :inner] + value[:, inner:])
        count = jnp.float32(0)
        for mb in range(micro):
            count += jnp.clip(lengths[mb] - z * rows, 0, rows).astype(F32)
        put(jnp.zeros((1, inner), F32) + count)

    when(second, met)
    plans = [[(p * 8 + k) * 8 + steps for p, k, steps in plan] for plan in (FIRST_PLAN, SECOND_PLAN)]
    def mine(a, b):
        return a if a == b else jnp.where(first, a, b)

    begins = [mine(a, b) for a, b in zip(begins_of(FIRST_PLAN, FIRST_PACE), begins_of(SECOND_PLAN, SECOND_PACE))]
    square, line, late = (mine(a, b) for a, b in zip(FIRST_PACE[:3], SECOND_PACE[:3]))
    same = FIRST_PACE[0] == FIRST_PACE[1] and SECOND_PACE[0] == SECOND_PACE[1]
    pace = (line if same else square, line, late)
    planned = mine(planned_steps(FIRST_PLAN), planned_steps(SECOND_PLAN))
    ticks = mine(steps_of(FIRST_PLAN, FIRST_PACE), steps_of(SECOND_PLAN, SECOND_PACE))

    def tick(t, carry):
        sums.tick(t, begins, pace, planned)
        return carry

    def step(i, t):
        entry = jnp.int32(0)
        for j, (a, b) in enumerate(zip(*plans)):
            entry = jnp.where(i == j, jnp.where(first, a, b), entry)
        what, k = entry // 64, lax.rem(entry // 8, 8)
        for p, act in ((FA, forward_a), (FB, forward_b), (BA, backward_a), (BB, backward_b), (BC, backward_c), (WC, weight_tap)):
            when(what == p, functools.partial(act, k))
        when(what == WU, weight_up)
        when(what == WD, weight_down)
        then = t + lax.rem(entry, 8)
        if with_sums:
            lax.fori_loop(t, then, tick, 0)
        return then

    t = lax.fori_loop(0, len(FIRST_PLAN), step, jnp.int32(0))
    smalls()

    if with_sums:
        lax.fori_loop(t, ticks, tick, 0)
        sums.drain()
        done = pltpu.make_async_copy(small.at[4], small_out, load.at[0])
        done.start()
        done.wait()
    else:
        done = pltpu.make_async_copy(small.at[0], small_out, load.at[0])
        done.start()
        done.wait()
        done = pltpu.make_async_copy(grad, res, load.at[1])
        done.start()
        done.wait()
    for mb in range(micro):
        if mb >= micro - 2:
            when(first, functools.partial(lambda m: store_end(m).wait(), mb))
            when(second, functools.partial(lambda m: hand_over(m, GY).wait_send(), mb))
        halo_sent(CW, 0, mb)
        halo_sent(GCW, 1, mb)


def run_blocks(mesh_shape, ends, lengths, outer_gain, inner_gains, outer_biases, inner_biases, down, conv, up):
    micro, rows, width = ends.shape
    inner = down.shape[1]
    taps = FILTER_TAPS
    with_sums = (mesh_shape["dp"], mesh_shape["seq"]) == (4, 4)
    buffers = {k: pltpu.VMEM((GROUPS, n, BLOCK), BF) for k, n in RECEIVE.items()} if with_sums else {}
    names = tuple(buffers)
    total = BLOCKS * BLOCK
    anywhere = pl.BlockSpec(memory_space=pl.ANY)
    vmem = pl.BlockSpec(memory_space=pltpu.VMEM)
    dma = pltpu.SemaphoreType.DMA
    scratch = [
        pltpu.VMEM(down.shape, BF),
        pltpu.VMEM(conv.shape, BF),
        pltpu.VMEM(up.shape, BF),
        pltpu.VMEM((micro, rows, width), BF),
        pltpu.VMEM((micro, rows, width), BF),
        pltpu.VMEM((micro, rows, width), BF),
        pltpu.VMEM((micro, 3 * rows, inner), BF),
        pltpu.VMEM((micro, rows, inner), BF),
        pltpu.VMEM((micro, 3 * rows, inner), BF),
        pltpu.VMEM((micro, rows, inner), BF),
        pltpu.VMEM((micro, rows, inner), F32),
        pltpu.VMEM((micro, rows, inner), F32),
        pltpu.VMEM((micro, rows, 128), F32),
        pltpu.VMEM((rows, 1), F32),
        pltpu.VMEM((2, rows, width), BF),
        pltpu.VMEM((rows, taps * inner), BF),
        pltpu.VMEM((micro * rows, inner), BF),
        pltpu.VMEM((4, 8, width), F32),
        pltpu.VMEM((6, 8, inner), F32),
        pltpu.VMEM((total, BLOCK), BF),
        pltpu.VMEM((9, 16, inner), F32),
        *[buffers[k] for k in names],
        dma((len(KINDS),)),
        dma((GROUPS, max(ARRIVES.values()) + 1)),
        dma((2,)),
        dma((len(SMALL_KINDS),)),
        dma((len(SMALL_KINDS),)),
        dma((micro + 3,)),
        dma((micro, 2)),
        dma((micro, 2)),
        dma((2, micro, 2)),
        dma((2, micro, 2)),
        dma((micro,)),
    ]
    flops = 2 * 3 * micro * rows * (2 * width * inner + taps * inner * inner)
    return pl.pallas_call(
        functools.partial(blocks_kernel, names, with_sums, mesh_shape["seq"] - 1),
        name="two_blocks",
        out_shape=(
            jax.ShapeDtypeStruct((micro, rows, width), BF),
            jax.ShapeDtypeStruct((total, BLOCK), BF),
            jax.ShapeDtypeStruct((16, inner), F32),
        ),
        in_specs=[anywhere, pl.BlockSpec(memory_space=pltpu.SMEM), vmem, vmem, vmem, vmem, anywhere, anywhere, anywhere],
        out_specs=[anywhere] * 3,
        scratch_shapes=scratch,
        cost_estimate=pl.CostEstimate(flops=flops, bytes_accessed=40 * 2**20, transcendentals=0),
        compiler_params=pltpu.CompilerParams(collective_id=1, has_side_effects=True, vmem_limit_bytes=62 * 2**20),
    )(ends, lengths, outer_gain, inner_gains, outer_biases, inner_biases, down, conv, up)


AHEAD = 6


def finish_kernel(
    ends, rows, small, ends_out, outer_gain, inner_gains, outer_biases, inner_biases, down, conv, up, rms,
    raw, full, held, wide, load, store,
):
    micro, width = ends.shape[0], ends.shape[2]
    places = [up.at[0, :, pl.ds(h * BLOCK, BLOCK)] for h in range(UP_BLOCKS)]
    places += [conv.at[0, k] for k in range(FILTER_TAPS)]
    places += [down.at[0, pl.ds(h * BLOCK, BLOCK)] for h in range(BLOCKS - DOWN_AT)]
    moves = [(rows.at[pl.ds(g * BLOCK, BLOCK)], raw.at[g], full.at[g], places[g]) for g in range(BLOCKS)]
    moves += [(ends.at[mb], held.at[mb], wide.at[mb], ends_out.at[0, mb, 0]) for mb in range(micro)]
    loads = [pltpu.make_async_copy(m[0], m[1], load.at[i]) for i, m in enumerate(moves)]
    stores = [pltpu.make_async_copy(m[2], m[3], store.at[i]) for i, m in enumerate(moves)]
    for copy in loads[:AHEAD]:
        copy.start()
    outer_gain[0:1, 0:BLOCK] = small[0:1, :]
    outer_gain[0:1, BLOCK:] = small[1:2, :]
    inner_gains[0] = small[2:4, :]
    for j in range(2):
        outer_biases[0, j : j + 1, 0:BLOCK] = small[4 + 2 * j : 5 + 2 * j, :]
        outer_biases[0, j : j + 1, BLOCK:] = small[5 + 2 * j : 6 + 2 * j, :]
    inner_biases[0] = small[8:12, :]
    squares = jnp.sum(small[12:14, :], axis=1, keepdims=True)
    roots = jnp.sqrt(squares / (small[14:15, 0:1] * width))
    rms[0:1, 0:1] = roots[0:1, :]
    rms[0:1, 1:2] = roots[1:2, :]
    for i, (_, source, target, _) in enumerate(moves):
        loads[i].wait()
        if i + AHEAD < len(moves):
            loads[i + AHEAD].start()
        target[...] = source[...].astype(F32)
        stores[i].start()
    for copy in stores:
        copy.wait()


def finish(shapes, ends, rows, small):
    anywhere = pl.BlockSpec(memory_space=pl.ANY)
    vmem = pl.BlockSpec(memory_space=pltpu.VMEM)
    dma = pltpu.SemaphoreType.DMA
    return pl.pallas_call(
        finish_kernel,
        name="outputs",
        out_shape=tuple(jax.ShapeDtypeStruct(shape, F32) for shape in shapes),
        in_specs=[anywhere, anywhere, vmem],
        out_specs=[anywhere, vmem, vmem, vmem, vmem, anywhere, anywhere, anywhere, vmem],
        scratch_shapes=[
            pltpu.VMEM((BLOCKS, BLOCK, BLOCK), BF),
            pltpu.VMEM((BLOCKS, BLOCK, BLOCK), F32),
            pltpu.VMEM(ends.shape, BF),
            pltpu.VMEM(ends.shape, F32),
            dma((BLOCKS + ends.shape[0],)),
            dma((BLOCKS + ends.shape[0],)),
        ],
        compiler_params=pltpu.CompilerParams(vmem_limit_bytes=60 * 2**20),
    )(ends, rows, small)


def body(
    mesh_shape, ends_in, lengths, outer_gain, inner_gains, outer_biases, inner_biases, down_in, conv_weight, up_out
):
    width = ends_in.shape[-1]
    ends, rows, small = run_blocks(
        mesh_shape, ends_in.reshape(ends_in.shape[1], -1, width), lengths.reshape(-1), outer_gain, inner_gains[0],
        outer_biases[0], inner_biases[0], down_in[0], conv_weight[0].reshape(-1, conv_weight.shape[-1]), up_out[0],
    )
    if (mesh_shape["dp"], mesh_shape["seq"]) == (4, 4):
        weights = (outer_gain, inner_gains, outer_biases, inner_biases, down_in, conv_weight, up_out)
        return finish((ends_in.shape, *(w.shape for w in weights), (1, 2)), ends, rows, small)
    rows, small = lax.psum((rows.astype(F32), small), ("dp", "seq"))
    up = jnp.concatenate([rows[:BLOCK], rows[BLOCK : 2 * BLOCK]], axis=1)
    conv = rows[UP_BLOCKS * BLOCK : DOWN_AT * BLOCK].reshape(conv_weight.shape[1:])
    down = rows[DOWN_AT * BLOCK :]
    rms = jnp.sqrt(jnp.sum(small[12:14], axis=1) / (small[14, 0] * width))
    return (
        ends.astype(F32).reshape(ends_in.shape),
        small[0:2].reshape(1, -1),
        small[None, 2:4],
        small[4:8].reshape(1, 2, -1),
        small[None, 8:12],
        down[None],
        conv[None],
        up[None],
        rms[None],
    )


def solution(mesh):
    in_specs = (
        P("section", None, "dp", "seq", None),
        P(None, "dp"),
        P("section", None),
        P("section", None, None),
        P("section", None, None),
        P("section", None, None),
        P("section", None, None),
        P("section", None, None, None),
        P("section", None, None),
    )
    out_specs = (
        P("section", None, "dp", "seq", None),
        P("section", None),
        P("section", None, None),
        P("section", None, None),
        P("section", None, None),
        P("section", None, None),
        P("section", None, None, None),
        P("section", None, None),
        P("section", None),
    )
    return jax.shard_map(
        functools.partial(body, dict(mesh.shape)), mesh=mesh, in_specs=in_specs, out_specs=out_specs, check_vma=False
    )
```
